512 devices in a mesh: dp: 32 (over y, x, core), mp: 16 (over z).
Axes of the slice: x: 4, y: 4, z: 16, core: 2. Of those that a mesh axis runs over, the one named last changes fastest.
Arguments:
- activations: bfloat16 [4096, 8192], P('dp'), may hold values from -16 to 16
- out_grads: bfloat16 [4096, 16384], P('dp', 'mp'), may hold values from -1 to 1
- weight: float32 [8192, 16384], P('dp', 'mp'), may hold values from -16 to 16
- row_moment: float32 [8192], P('dp'), may hold values from 0.25 to 2
- col_moment: float32 [16384], P('mp'), may hold values from 0.25 to 2
Outputs:
- update: float32 [8192, 16384], P('dp', 'mp')
- new_rows: float32 [8192], P('dp')
- new_cols: float32 [16384], P('mp')
The draws below stay inside these ranges and needn't reach their ends.
All inputs are finite; a program needn't handle non-finite values.
Results may differ from the reference program's by a relative error of at most 0.0003.
Values may be sent and summed in bfloat16 or wider, within the bound.
No kernel may reach another device: no remote copies, remote signals or barrier semaphores. Data moves between devices by JAX's collectives and lax.ppermute only.
A program may use at most 64 MiB of HBM per device.

```python
import math
import jax
import jax.numpy as jnp
from jax import lax

D = 8192
FF = 16384
TOKENS = 4096


def column_scales(key, count):
    spread = jnp.exp(jax.random.uniform(key, (count,), jnp.float32, math.log(0.5), math.log(2.0)))
    ramp = 0.5 + jnp.arange(count, dtype=jnp.float32) / count
    return ramp * spread


def shared_parts(key):
    key = jax.random.fold_in(key, 5)
    key_token, key_group, key_row, key_col = jax.random.split(key, 4)
    strength = jnp.clip(jax.random.normal(key_token, (TOKENS, 1), jnp.float32), -4.0, 4.0)
    group = jax.random.randint(key_group, (TOKENS, 1), 0, 2).astype(jnp.float32)
    row_dir = jnp.clip(jax.random.normal(key_row, (D,), jnp.float32), -4.0, 4.0)
    col_dir = jnp.clip(jax.random.normal(key_col, (FF,), jnp.float32), -4.0, 4.0)
    return (strength, group, row_dir, col_dir)


def feature_gain(key, count, group):
    side = jax.random.randint(key, (count,), 0, 2).astype(jnp.float32)
    first = 1.0 - side
    return (1.0 - group) * (1.0 + 2.0 * first[None, :]) + group * (1.0 + 0.5 * side[None, :])


def draw_activations(key, part):
    strength, group, row_dir, col_dir = shared_parts(key)
    coupling = math.sqrt(0.4 / math.sqrt(TOKENS))
    key = jax.random.fold_in(key, 11)
    key_scale = jax.random.fold_in(key, 0)
    key_base = jax.random.fold_in(key, 1)
    key_side = jax.random.fold_in(key, 3)
    column_scale = column_scales(key_scale, D)
    gain = feature_gain(key_side, D, group)
    coupled = coupling * strength * row_dir[None, :]
    base = jnp.clip(jax.random.normal(key_base, (TOKENS, D), jnp.float32), -6.0, 6.0)
    values = (base + coupled) * gain * column_scale[None, :]
    return jnp.clip(values, -16.0, 16.0).astype(jnp.bfloat16)


def draw_out_grads(key, part):
    strength, group, row_dir, col_dir = shared_parts(key)
    coupling = math.sqrt(0.4 / math.sqrt(TOKENS))
    key = jax.random.fold_in(key, 23)
    key_scale = jax.random.fold_in(key, 0)
    key_base = jax.random.fold_in(key, 1)
    key_side = jax.random.fold_in(key, 4)
    column_scale = column_scales(key_scale, FF) / math.sqrt(TOKENS)
    gain = feature_gain(key_side, FF, group)
    coupled = coupling * strength * col_dir[None, :]
    base = jnp.clip(jax.random.normal(key_base, (TOKENS, FF), jnp.float32), -6.0, 6.0)
    values = (base + coupled) * gain * column_scale[None, :]
    return jnp.clip(values, -1.0, 1.0).astype(jnp.bfloat16)


def draw_weight(key, part):
    strength, group, row_dir, col_dir = shared_parts(key)
    key = jax.random.fold_in(key, 37)
    key_rows, key_base = jax.random.split(key, 2)
    row_scale = column_scales(key_rows, D)
    column_ramp = 0.5 + jnp.arange(FF, dtype=jnp.float32) / FF
    aligned = 0.5 * row_dir[:, None] * col_dir[None, :]
    base = jnp.clip(jax.random.normal(key_base, (D, FF), jnp.float32), -6.0, 6.0)
    values = (base + aligned) * row_scale[:, None] * column_ramp[None, :]
    return jnp.clip(values, -16.0, 16.0)


def block_levels(stream_key, shape, shards, least, top_value):
    def one(position, parts):
        heights = jax.random.uniform(jax.random.fold_in(jax.random.fold_in(stream_key, 6), position), (parts,), jnp.float32, least / len(shards), top_value / len(shards))
        return jnp.repeat(jnp.exp(heights), shape[position] // parts).reshape((-1,) + (1,) * (len(shape) - position - 1))

    level = one(*shards[0])
    for cut in shards[1:]:
        level = level * one(*cut)
    return level


def setup_inputs(seed: int = 0) -> dict:
    key_of = jax.random.split(jax.random.key(seed), 6)
    return {
        "activations": draw_activations(jax.random.fold_in(key_of[5], 71), 0),
        "out_grads": draw_out_grads(jax.random.fold_in(key_of[5], 71), 0),
        "weight": draw_weight(jax.random.fold_in(key_of[5], 71), 0),
        "row_moment": jnp.clip(jnp.exp(math.log(2.0) - 2.0794415 * jax.random.uniform(key_of[3], (D,), jnp.float32) ** block_levels(key_of[3], (D,), ((0, 32),), -0.2, 0.2)), 0.25, 2.0),
        "col_moment": jnp.clip(jnp.exp(math.log(2.0) - 2.0794415 * jax.random.uniform(key_of[4], (FF,), jnp.float32) ** block_levels(key_of[4], (FF,), ((0, 16),), -0.2, 0.2)), 0.25, 2.0),
    }


BETA_TWO = 0.8
CLIP_LEVEL = 0.25
WEIGHT_DECAY = 0.1
EPSILON = 1e-06

def reference(activations, out_grads, weight, row_moment, col_moment):
    weight_grad = jnp.dot(activations.T, out_grads, preferred_element_type=jnp.float32)
    squares = weight_grad * weight_grad
    new_rows = BETA_TWO * row_moment + (1.0 - BETA_TWO) * (lax.optimization_barrier(jnp.sum(squares, axis=1)) / FF)
    new_cols = BETA_TWO * col_moment + (1.0 - BETA_TWO) * (lax.optimization_barrier(jnp.sum(squares, axis=0)) / D)
    scaled = weight_grad / jnp.sqrt(new_rows[:, None] * new_cols[None, :])
    mean_square = jnp.sum(scaled * scaled) / (D * FF)
    factor = 1.0 / jnp.maximum(1.0, jnp.sqrt(mean_square) / CLIP_LEVEL)
    direction = factor * scaled + WEIGHT_DECAY * weight
    trust_ratio = jnp.sqrt(jnp.sum(weight * weight) / (jnp.sum(direction * direction) + EPSILON))
    return (trust_ratio * direction, new_rows, new_cols)
```

```python
import jax
import jax.numpy as jnp
from jax import lax
from jax.sharding import Mesh, PartitionSpec as P

D = 8192
FF = 16384


BETA_TWO = 0.8
CLIP_LEVEL = 0.25
WEIGHT_DECAY = 0.1
EPSILON = 1e-06

CHIPS = ("y", "x")
ROWS = ("y", "x", "core")
SIDE = 4


def total(value, axes, count):
    sent = jnp.broadcast_to(value, (count,) + value.shape)
    return jnp.sum(lax.all_to_all(sent, axes, 0, 0), axis=0)


def shards(activations, out_grads, weight, row_moment, col_moment):
    core = lax.axis_index("core")
    features = lax.all_to_all(activations, CHIPS, split_axis=1, concat_axis=0, tiled=True)
    grads = lax.all_gather(out_grads, CHIPS, axis=0, tiled=True)
    rows = features.shape[1] // 2

    def product(half):
        return lax.dot_general(
            lax.dynamic_slice_in_dim(features, half * rows, rows, 1),
            grads,
            (((0,), (0,)), ((), ())),
            preferred_element_type=jnp.float32,
        )

    received = lax.ppermute(product(1 - core), "core", [(0, 1), (1, 0)])
    weight_grad = product(core) + received
    squares = weight_grad * weight_grad
    col_total = total(jnp.sum(squares, axis=0).reshape(8, 128), ROWS, 32).reshape(-1)
    new_cols = BETA_TWO * col_moment + (1.0 - BETA_TWO) * (col_total / D)
    col_root = lax.rsqrt(new_cols)
    by_cols = weight_grad * col_root[None, :]
    row_parts = jnp.stack(
        [
            jnp.sum(squares, axis=1),
            jnp.sum(by_cols * by_cols, axis=1),
            jnp.sum(by_cols * weight, axis=1),
            jnp.sum(weight * weight, axis=1),
        ]
    )
    row_parts = total(row_parts.reshape(8, 128), "z", 16).reshape(4, rows)
    new_rows = BETA_TWO * row_moment + (1.0 - BETA_TWO) * (row_parts[0] / FF)
    row_root = lax.rsqrt(new_rows)
    sums = jnp.stack([row_parts[1] * row_root * row_root, row_parts[2] * row_root, row_parts[3], jnp.zeros_like(row_root)])
    sums = jnp.sum(total(sums.reshape(8, 128), ROWS, 32).reshape(4, rows), axis=1)
    scaled_sum, cross_sum, weight_sum = sums[0], sums[1], sums[2]
    factor = 1.0 / jnp.maximum(1.0, jnp.sqrt(scaled_sum / (D * FF)) / CLIP_LEVEL)
    direction_sum = (
        factor * factor * scaled_sum + 2.0 * WEIGHT_DECAY * factor * cross_sum + WEIGHT_DECAY * WEIGHT_DECAY * weight_sum
    )
    trust_ratio = jnp.sqrt(weight_sum / (jnp.maximum(direction_sum, 0.0) + EPSILON))
    update = by_cols * (trust_ratio * factor * row_root)[:, None] + (trust_ratio * WEIGHT_DECAY) * weight
    return (update, new_rows, new_cols)


def solution(mesh):
    mesh = Mesh(mesh.devices.reshape(SIDE, SIDE, 2, 16), ("y", "x", "core", "z"))
    placed = (P(ROWS, None), P(ROWS, "z"), P(ROWS, "z"), P(ROWS), P("z"))
    return jax.shard_map(
        shards,
        mesh=mesh,
        in_specs=placed,
        out_specs=(P(ROWS, "z"), P(ROWS), P("z")),
        check_vma=False,
    )
```

```python
import functools

import jax
import jax.numpy as jnp
from jax import lax
from jax.experimental import pallas as pl
from jax.experimental.pallas import tpu as pltpu
from jax.sharding import Mesh, PartitionSpec as P

D = 8192
FF = 16384


BETA_TWO = 0.8
CLIP_LEVEL = 0.25
WEIGHT_DECAY = 0.1
EPSILON = 1e-06

CHIPS = ("y", "x")
ROWS = ("y", "x", "core")
SIDE = 4
LAYERS = 16
TOKENS = 128
ROW_BLOCK = 256


def total(value, axes, count):
    sent = jnp.broadcast_to(value, (count,) + value.shape)
    return jnp.sum(lax.all_to_all(sent, axes, 0, 0), axis=0)


def device(y, x, core):
    return ((y % SIDE) * SIDE + x % SIDE) * 2 + core


def along(value, step, stage):
    pairs = []
    for y in range(SIDE):
        for x in range(SIDE):
            for core in range(2):
                on_x = core == stage
                to = device(y, x + step, core) if on_x else device(y + step, x, core)
                pairs.append((device(y, x, core), to))
    return lax.ppermute(value, ROWS, pairs)


def next_layer(value):
    pairs = [(i, (i + 1) % LAYERS) for i in range(LAYERS)]
    pairs += [(LAYERS + i, LAYERS + (i - 1) % LAYERS) for i in range(LAYERS)]
    return lax.ppermute(value, ("core", "z"), pairs)


def product_kernel(place, first, second, *refs):
    count = SIDE * SIDE
    grads, (out, first_buf, second_buf, grad_buf, turned, sems) = refs[:-6], refs[-6:]
    copies = [pltpu.make_async_copy(first, first_buf, sems.at[0]), pltpu.make_async_copy(second, second_buf, sems.at[1])]
    row = 0
    for i, grad in enumerate(grads):
        copies.append(pltpu.make_async_copy(grad, grad_buf.at[pl.ds(row, grad.shape[0])], sems.at[2 + i]))
        row += grad.shape[0]
    for copy in copies:
        copy.start()
    half = TOKENS // 2
    y, x, core, flipped = place[0], place[1], place[2], place[3] == 1
    column = pl.multiple_of(place[4], ROW_BLOCK)
    copies[0].wait()
    copies[1].wait()
    for i in range(count):
        j, k = i // SIDE, i % SIDE
        dx, dy = jnp.where(core == 0, k, j), jnp.where(core == 0, j, k)
        chip = ((y - dy) & (SIDE - 1)) * SIDE + ((x - dx) & (SIDE - 1))
        mine = first_buf[chip, :, pl.ds(column, ROW_BLOCK)]
        other = second_buf[chip, :, pl.ds(column, ROW_BLOCK)]
        low = jnp.where(flipped, other, mine)
        high = jnp.where(flipped, mine, other)
        turned[:, i * TOKENS : (i + 1) * TOKENS] = jnp.concatenate([low, high], axis=0).T
    for copy in copies[2:]:
        copy.wait()

    @pl.loop(0, out.shape[1] // 256)
    def _(n):
        columns = pl.ds(pl.multiple_of(n * 256, 256), 256)
        out[:, columns] = jnp.dot(turned[...], grad_buf[:, columns], preferred_element_type=jnp.float32)


def product(place, first, second, grads):
    depth = sum(g.shape[0] for g in grads)
    width = grads[0].shape[1]
    anywhere = pl.BlockSpec(memory_space=pl.ANY)
    return pl.pallas_call(
        product_kernel,
        out_shape=jax.ShapeDtypeStruct((ROW_BLOCK, width), jnp.float32),
        in_specs=[pl.BlockSpec(memory_space=pltpu.SMEM)] + [anywhere] * (2 + len(grads)),
        out_specs=pl.BlockSpec(memory_space=pltpu.VMEM),
        scratch_shapes=[
            pltpu.VMEM(first.shape, jnp.bfloat16),
            pltpu.VMEM(first.shape, jnp.bfloat16),
            pltpu.VMEM((depth, width), jnp.bfloat16),
            pltpu.VMEM((ROW_BLOCK, depth), jnp.bfloat16),
            pltpu.SemaphoreType.DMA((2 + len(grads),)),
        ],
        compiler_params=pltpu.CompilerParams(vmem_limit_bytes=24 * 2**20),
        cost_estimate=pl.CostEstimate(
            flops=2 * ROW_BLOCK * depth * width, bytes_accessed=8 * 2**20, transcendentals=0
        ),
    )(place, first, second, *grads)


def shards(activations, out_grads, weight, row_moment, col_moment):
    y, x, core, layer = (lax.axis_index(name) for name in ("y", "x", "core", "z"))
    half = layer % 2
    sent = lax.dynamic_slice_in_dim(activations, half * (TOKENS // 2), TOKENS // 2, 0)
    sent = sent.reshape(TOKENS // 2, SIDE * SIDE, 2 * ROW_BLOCK)
    first = lax.all_to_all(sent, CHIPS, split_axis=1, concat_axis=0, tiled=True)
    first = first.reshape(SIDE * SIDE, TOKENS // 2, 2 * ROW_BLOCK)
    second = next_layer(first)
    line = [out_grads] + [along(out_grads, k, 0) for k in range(1, SIDE)]
    line = jnp.concatenate(line, axis=0)
    grads = [line] + [along(line, j, 1) for j in range(1, SIDE)]
    place = lambda which: jnp.stack([y, x, core, half, which * ROW_BLOCK])
    theirs = product(place(1 - core), first, second, grads)
    received = lax.ppermute(theirs, "core", [(0, 1), (1, 0)])
    mine = product(place(core), first, second, grads)
    weight_grad = mine + received
    rows = ROW_BLOCK
    squares = weight_grad * weight_grad
    col_total = total(jnp.sum(squares, axis=0).reshape(8, 128), ROWS, 32).reshape(-1)
    new_cols = BETA_TWO * col_moment + (1.0 - BETA_TWO) * (col_total / D)
    col_root = lax.rsqrt(new_cols)
    by_cols = weight_grad * col_root[None, :]
    row_parts = jnp.stack(
        [
            jnp.sum(squares, axis=1),
            jnp.sum(by_cols * by_cols, axis=1),
            jnp.sum(by_cols * weight, axis=1),
            jnp.sum(weight * weight, axis=1),
        ]
    )
    row_parts = total(row_parts.reshape(8, 128), "z", 16).reshape(4, rows)
    new_rows = BETA_TWO * row_moment + (1.0 - BETA_TWO) * (row_parts[0] / FF)
    row_root = lax.rsqrt(new_rows)
    sums = jnp.stack([row_parts[1] * row_root * row_root, row_parts[2] * row_root, row_parts[3], jnp.zeros_like(row_root)])
    sums = jnp.sum(total(sums.reshape(8, 128), ROWS, 32).reshape(4, rows), axis=1)
    scaled_sum, cross_sum, weight_sum = sums[0], sums[1], sums[2]
    factor = 1.0 / jnp.maximum(1.0, jnp.sqrt(scaled_sum / (D * FF)) / CLIP_LEVEL)
    direction_sum = (
        factor * factor * scaled_sum + 2.0 * WEIGHT_DECAY * factor * cross_sum + WEIGHT_DECAY * WEIGHT_DECAY * weight_sum
    )
    trust_ratio = jnp.sqrt(weight_sum / (jnp.maximum(direction_sum, 0.0) + EPSILON))
    update = by_cols * (trust_ratio * factor * row_root)[:, None] + (trust_ratio * WEIGHT_DECAY) * weight
    return (update, new_rows, new_cols)


def solution(mesh):
    mesh = Mesh(mesh.devices.reshape(SIDE, SIDE, 2, LAYERS), ("y", "x", "core", "z"))
    placed = (P(ROWS, None), P(ROWS, "z"), P(ROWS, "z"), P(ROWS), P("z"))
    return jax.shard_map(
        shards,
        mesh=mesh,
        in_specs=placed,
        out_specs=(P(ROWS, "z"), P(ROWS), P("z")),
        check_vma=False,
    )
```

```python
import functools

import jax
import jax.numpy as jnp
from jax import lax
from jax.experimental import pallas as pl
from jax.experimental.pallas import tpu as pltpu
from jax.sharding import Mesh, PartitionSpec as P

D = 8192
FF = 16384


BETA_TWO = 0.8
CLIP_LEVEL = 0.25
WEIGHT_DECAY = 0.1
EPSILON = 1e-06

CHIPS = ("y", "x")
ROWS = ("y", "x", "core")
SIDE = 4
COUNT = SIDE * SIDE
LAYERS = 16
DEVICES = 2 * COUNT
TOKENS = 128
HALF = TOKENS // 2
GROUP = SIDE * TOKENS
ROW_BLOCK = 256
WIDTH = 1024
LANES = 128
TILE = (8, LANES)

ANYWHERE = pl.BlockSpec(memory_space=pl.ANY)
WHOLE = pl.BlockSpec(memory_space=pltpu.VMEM)
SCALARS = pl.BlockSpec(memory_space=pltpu.SMEM)
PARAMS = pltpu.CompilerParams(vmem_limit_bytes=16 * 2**20)


def shape(*dims, dtype=jnp.float32):
    return jax.ShapeDtypeStruct(dims, dtype)


def cost(flops, bytes_accessed):
    return pl.CostEstimate(flops=flops, bytes_accessed=bytes_accessed, transcendentals=0)


def device(y, x, core):
    return ((y % SIDE) * SIDE + x % SIDE) * 2 + core


def along(value, step, stage):
    pairs = []
    for y in range(SIDE):
        for x in range(SIDE):
            for core in range(2):
                on_x = core == stage
                to = device(y, x + step, core) if on_x else device(y + step, x, core)
                pairs.append((device(y, x, core), to))
    return lax.ppermute(value, ROWS, pairs)


def next_layer(value):
    pairs = [(i, (i + 1) % LAYERS) for i in range(LAYERS)]
    pairs += [(LAYERS + i, LAYERS + (i - 1) % LAYERS) for i in range(LAYERS)]
    return lax.ppermute(value, ("core", "z"), pairs)


def exchange(tiles, axes):
    return lax.all_to_all(tiles, axes, 0, 0)


def pack_kernel(place, source, out, sems):
    rows = pl.ds(pl.multiple_of(place[3] * HALF, HALF), HALF)
    copies = [
        pltpu.make_async_copy(source.at[rows, pl.ds(i * 2 * ROW_BLOCK, 2 * ROW_BLOCK)], out.at[i], sems.at[i])
        for i in range(COUNT)
    ]
    for copy in copies:
        copy.start()
    for copy in copies:
        copy.wait()


def pack(place, activations):
    return pl.pallas_call(
        pack_kernel,
        out_shape=shape(COUNT, HALF, 2 * ROW_BLOCK, dtype=jnp.bfloat16),
        in_specs=[SCALARS, ANYWHERE],
        out_specs=ANYWHERE,
        scratch_shapes=[pltpu.SemaphoreType.DMA((COUNT,))],
        compiler_params=PARAMS,
        cost_estimate=cost(0, 2**21),
    )(place, activations)


def join_kernel(*refs):
    blocks, out, sems = refs[:-2], refs[-2], refs[-1]
    copies = [
        pltpu.make_async_copy(block, out.at[pl.ds(i * TOKENS, TOKENS)], sems.at[i]) for i, block in enumerate(blocks)
    ]
    for copy in copies:
        copy.start()
    for copy in copies:
        copy.wait()


def join(blocks):
    return pl.pallas_call(
        join_kernel,
        out_shape=shape(GROUP, WIDTH, dtype=jnp.bfloat16),
        in_specs=[ANYWHERE] * len(blocks),
        out_specs=ANYWHERE,
        scratch_shapes=[pltpu.SemaphoreType.DMA((len(blocks),))],
        compiler_params=PARAMS,
        cost_estimate=cost(0, 2**21),
    )(*blocks)


def turn_kernel(place, part, out):
    y, x, core = place[0], place[1], place[2]

    def block(i):
        j, k = i // SIDE, i % SIDE
        dx, dy = jnp.where(core == 0, k, j), jnp.where(core == 0, j, k)
        return part[((y - dy) & (SIDE - 1)) * SIDE + ((x - dx) & (SIDE - 1))]

    for i in range(0, COUNT, 2):
        out[:, i * HALF : (i + 2) * HALF] = jnp.concatenate([block(i), block(i + 1)], axis=0).T


def turn(place, part):
    return pl.pallas_call(
        turn_kernel,
        out_shape=shape(2 * ROW_BLOCK, COUNT * HALF, dtype=jnp.bfloat16),
        in_specs=[SCALARS, WHOLE],
        out_specs=WHOLE,
        compiler_params=PARAMS,
        cost_estimate=cost(0, 2**21),
    )(place, part)


def product_kernel(place, first, second, grads, *refs):
    total, out = refs if len(refs) == 2 else (None, refs[0])
    start = place[3] * HALF

    def rows(offset):
        offset = pl.multiple_of(offset, HALF)
        return jnp.concatenate([grads[pl.ds(i * TOKENS + offset, HALF), :] for i in range(SIDE)], axis=0)

    value = jnp.dot(first[...], rows(start), preferred_element_type=jnp.float32)
    value += jnp.dot(second[...], rows(HALF - start), preferred_element_type=jnp.float32)
    out[...] = value if total is None else value + total[...]


def product(place, first, second, grads, total, group, which=None):
    block = WIDTH // 4
    count = 2 * ROW_BLOCK if which is None else ROW_BLOCK
    row = (lambda place: 0) if which is None else (lambda place: which(place[2]))
    turned = pl.BlockSpec((count, SIDE * HALF), lambda n, place: (row(place), group))
    totals = pl.BlockSpec((count, block), lambda n, place: (row(place), n))
    return pl.pallas_call(
        product_kernel,
        out_shape=shape(count, WIDTH),
        grid_spec=pltpu.PrefetchScalarGridSpec(
            num_scalar_prefetch=1,
            grid=(WIDTH // block,),
            in_specs=[turned, turned, pl.BlockSpec((GROUP, block), lambda n, place: (0, n))]
            + ([] if total is None else [totals]),
            out_specs=pl.BlockSpec((count, block), lambda n, place: (0, n)),
        ),
        compiler_params=PARAMS,
        cost_estimate=cost(2 * count * GROUP * WIDTH, 6 * 2**20),
    )(place, first, second, grads, *([] if total is None else [total]))


def columns_kernel(mine, theirs, grad, sent):
    value = mine[...] + theirs[...]
    grad[...] = value
    sums = jnp.sum(value * value, axis=0, keepdims=True)
    tile = jnp.concatenate([sums[:, i * LANES : (i + 1) * LANES] for i in range(8)], axis=0)
    for i in range(DEVICES):
        sent[i] = tile


def columns(mine, theirs):
    return pl.pallas_call(
        columns_kernel,
        out_shape=(shape(ROW_BLOCK, WIDTH), shape(DEVICES, *TILE)),
        in_specs=[WHOLE] * 2,
        out_specs=(WHOLE, WHOLE),
        compiler_params=PARAMS,
        cost_estimate=cost(2**20, 3 * 2**20),
    )(mine, theirs)


def rows_kernel(received, moment, grad, weight, cols, sent):
    new = BETA_TWO * moment[...] + (1.0 - BETA_TWO) * (jnp.sum(received[...], axis=0) / D)
    cols[...] = new
    root = lax.rsqrt(new)
    sums = [jnp.zeros((ROW_BLOCK, LANES), jnp.float32)] * 4
    for i in range(WIDTH // LANES):
        lanes = slice(i * LANES, (i + 1) * LANES)
        value, held = grad[:, lanes], weight[:, lanes]
        by_cols = value * root[i : i + 1, :]
        terms = (value * value, by_cols * by_cols, by_cols * held, held * held)
        sums = [a + b for a, b in zip(sums, terms)]
    parts = []
    for value in sums:
        for row in range(0, ROW_BLOCK, LANES):
            parts.append(jnp.sum(value[row : row + LANES, :].T, axis=0, keepdims=True))
    tile = jnp.concatenate(parts, axis=0)
    for i in range(LAYERS):
        sent[i] = tile


def rows(received, moment, grad, weight):
    return pl.pallas_call(
        rows_kernel,
        out_shape=(shape(*TILE), shape(LAYERS, *TILE)),
        in_specs=[WHOLE] * 4,
        out_specs=(WHOLE, WHOLE),
        compiler_params=PARAMS,
        cost_estimate=cost(2**21, 2**21),
    )(received, moment, grad, weight)


def scalars_kernel(received, moment, rows_out, sent):
    parts = jnp.sum(received[...], axis=0)
    new = BETA_TWO * moment[...] + (1.0 - BETA_TWO) * (parts[0:2] / FF)
    rows_out[...] = new
    root = lax.rsqrt(new)
    tile = jnp.concatenate([parts[2:4] * root * root, parts[4:6] * root, parts[6:8], jnp.zeros_like(root)], axis=0)
    for i in range(DEVICES):
        sent[i] = tile


def scalars(received, moment):
    return pl.pallas_call(
        scalars_kernel,
        out_shape=(shape(2, LANES), shape(DEVICES, *TILE)),
        in_specs=[WHOLE] * 2,
        out_specs=(WHOLE, WHOLE),
        compiler_params=PARAMS,
        cost_estimate=cost(2**14, 2**18),
    )(received, moment)


def update_kernel(received, new_rows, new_cols, grad, weight, out):
    parts = jnp.sum(received[...], axis=0)
    scaled_sum, cross_sum, weight_sum = (jnp.sum(parts[i : i + 2], keepdims=True) for i in (0, 2, 4))
    factor = 1.0 / jnp.maximum(1.0, jnp.sqrt(scaled_sum / (D * FF)) / CLIP_LEVEL)
    direction_sum = (
        factor * factor * scaled_sum + 2.0 * WEIGHT_DECAY * factor * cross_sum + WEIGHT_DECAY * WEIGHT_DECAY * weight_sum
    )
    trust_ratio = jnp.sqrt(weight_sum / (jnp.maximum(direction_sum, 0.0) + EPSILON))
    by_row = lax.rsqrt(new_rows[...]) * (trust_ratio * factor)
    by_col = lax.rsqrt(new_cols[...])
    decay = trust_ratio * WEIGHT_DECAY
    for half in range(2):
        here = slice(half * LANES, (half + 1) * LANES)
        scale = jnp.broadcast_to(by_row[half : half + 1, :], (LANES, LANES)).T
        for i in range(WIDTH // LANES):
            lanes = slice(i * LANES, (i + 1) * LANES)
            out[here, lanes] = grad[here, lanes] * by_col[i : i + 1, :] * scale + decay * weight[here, lanes]


def update(received, new_rows, new_cols, grad, weight):
    return pl.pallas_call(
        update_kernel,
        out_shape=shape(ROW_BLOCK, WIDTH),
        in_specs=[WHOLE] * 5,
        out_specs=WHOLE,
        compiler_params=PARAMS,
        cost_estimate=cost(2**20, 3 * 2**20),
    )(received, new_rows, new_cols, grad, weight)


def shards(activations, out_grads, weight, row_moment, col_moment):
    y, x, core, layer = (lax.axis_index(name) for name in ("y", "x", "core", "z"))
    place = jnp.stack([y, x, core, layer & 1])
    line = [out_grads] + [along(out_grads, k, 0) for k in range(1, SIDE)]
    packed = pack(place, activations)
    packed, line[1] = lax.optimization_barrier((packed, line[1]))
    first = lax.all_to_all(packed, CHIPS, 0, 0)
    second = next_layer(first)
    line = join(line)
    grads = [line] + [along(line, j, 1) for j in range(1, SIDE)]
    first, second = turn(place, first), turn(place, second)
    total = None
    for j in range(SIDE - 1):
        total = product(place, first, second, grads[j], total, j)
    theirs = product(place, first, second, grads[-1], total, SIDE - 1, lambda core: 1 - core)
    received = lax.ppermute(theirs, "core", [(0, 1), (1, 0)])
    mine = product(place, first, second, grads[-1], total, SIDE - 1, lambda core: core)
    weight_grad, tiles = columns(mine, received)
    new_cols, tiles = rows(exchange(tiles, ROWS), col_moment.reshape(TILE), weight_grad, weight)
    new_rows, tiles = scalars(exchange(tiles, "z"), row_moment.reshape(2, LANES))
    out = update(exchange(tiles, ROWS), new_rows, new_cols, weight_grad, weight)
    return (out, new_rows.reshape(-1), new_cols.reshape(-1))


def solution(mesh):
    mesh = Mesh(mesh.devices.reshape(SIDE, SIDE, 2, LAYERS), ("y", "x", "core", "z"))
    placed = (P(ROWS, None), P(ROWS, "z"), P(ROWS, "z"), P(ROWS), P("z"))
    return jax.shard_map(
        shards,
        mesh=mesh,
        in_specs=placed,
        out_specs=(P(ROWS, "z"), P(ROWS), P("z")),
        check_vma=False,
    )
```

```python
import functools

import jax
import jax.numpy as jnp
from jax import lax
from jax.experimental import pallas as pl
from jax.experimental.pallas import tpu as pltpu
from jax.sharding import Mesh, PartitionSpec as P

D = 8192
FF = 16384


BETA_TWO = 0.8
CLIP_LEVEL = 0.25
WEIGHT_DECAY = 0.1
EPSILON = 1e-06

CHIPS = ("y", "x")
ROWS = ("y", "x", "core")
SIDE = 4
COUNT = SIDE * SIDE
LAYERS = 16
DEVICES = 2 * COUNT
TOKENS = 128
HALF = TOKENS // 2
GROUP = SIDE * TOKENS
ROW_BLOCK = 256
WIDTH = 1024
LANES = 128
COLUMNS = 256
TILE = (8, LANES)

ANYWHERE = pl.BlockSpec(memory_space=pl.ANY)
WHOLE = pl.BlockSpec(memory_space=pltpu.VMEM)
SCALARS = pl.BlockSpec(memory_space=pltpu.SMEM)
PARAMS = pltpu.CompilerParams(vmem_limit_bytes=16 * 2**20)


def shape(*dims, dtype=jnp.float32):
    return jax.ShapeDtypeStruct(dims, dtype)


def cost(flops, bytes_accessed):
    return pl.CostEstimate(flops=flops, bytes_accessed=bytes_accessed, transcendentals=0)


def device(y, x, core):
    return ((y % SIDE) * SIDE + x % SIDE) * 2 + core


def along(value, step, stage):
    pairs = []
    for y in range(SIDE):
        for x in range(SIDE):
            for core in range(2):
                on_x = core == stage
                to = device(y, x + step, core) if on_x else device(y + step, x, core)
                pairs.append((device(y, x, core), to))
    return lax.ppermute(value, ROWS, pairs)


def next_layer(value):
    pairs = [(i, (i + 1) % LAYERS) for i in range(LAYERS)]
    pairs += [(LAYERS + i, LAYERS + (i - 1) % LAYERS) for i in range(LAYERS)]
    return lax.ppermute(value, ("core", "z"), pairs)


def exchange(tiles, axes):
    return lax.all_to_all(tiles, axes, 0, 0)


def pack_kernel(place, source, out, sems):
    rows = pl.ds(pl.multiple_of(place[3] * HALF, HALF), HALF)
    copies = [
        pltpu.make_async_copy(source.at[rows, pl.ds(i * 2 * ROW_BLOCK, 2 * ROW_BLOCK)], out.at[i], sems.at[i])
        for i in range(COUNT)
    ]
    for copy in copies:
        copy.start()
    for copy in copies:
        copy.wait()


def pack(place, activations):
    return pl.pallas_call(
        pack_kernel,
        out_shape=shape(COUNT, HALF, 2 * ROW_BLOCK, dtype=jnp.bfloat16),
        in_specs=[SCALARS, pl.BlockSpec(memory_space=pltpu.HBM)],
        out_specs=ANYWHERE,
        scratch_shapes=[pltpu.SemaphoreType.DMA((COUNT,))],
        compiler_params=PARAMS,
        cost_estimate=cost(0, 2**21),
    )(place, activations)


def join_kernel(*refs):
    blocks, out, sems = refs[:-2], refs[-2], refs[-1]
    copies = [
        pltpu.make_async_copy(block, out.at[pl.ds(i * TOKENS, TOKENS)], sems.at[i]) for i, block in enumerate(blocks)
    ]
    for copy in copies:
        copy.start()
    for copy in copies:
        copy.wait()


def join(blocks):
    return pl.pallas_call(
        join_kernel,
        out_shape=shape(GROUP, WIDTH, dtype=jnp.bfloat16),
        in_specs=[ANYWHERE] * len(blocks),
        out_specs=ANYWHERE,
        scratch_shapes=[pltpu.SemaphoreType.DMA((len(blocks),))],
        compiler_params=PARAMS,
        cost_estimate=cost(0, 2**21),
    )(*blocks)


def turn_kernel(place, part, out):
    y, x, core = place[0], place[1], place[2]

    def block(i):
        j, k = i // SIDE, i % SIDE
        dx, dy = jnp.where(core == 0, k, j), jnp.where(core == 0, j, k)
        return part[((y - dy) & (SIDE - 1)) * SIDE + ((x - dx) & (SIDE - 1))]

    for i in range(0, COUNT, 2):
        out[:, i * HALF : (i + 2) * HALF] = jnp.concatenate([block(i), block(i + 1)], axis=0).T


def turn(place, part):
    return pl.pallas_call(
        turn_kernel,
        out_shape=shape(2 * ROW_BLOCK, COUNT * HALF, dtype=jnp.bfloat16),
        in_specs=[SCALARS, WHOLE],
        out_specs=WHOLE,
        compiler_params=PARAMS,
        cost_estimate=cost(0, 2**21),
    )(place, part)


def product_kernel(group, which, place, first, second, grads, *refs):
    total, out = refs if len(refs) == 2 else (None, refs[0])
    start = place[3] * HALF
    rows = pl.ds(0 if which is None else pl.multiple_of(which(place[2]) * ROW_BLOCK, ROW_BLOCK), out.shape[0])
    depth = slice(group * SIDE * HALF, (group + 1) * SIDE * HALF)

    @pl.loop(0, WIDTH // COLUMNS)
    def _(n):
        columns = pl.ds(pl.multiple_of(n * COLUMNS, COLUMNS), COLUMNS)

        def tokens(offset):
            offset = pl.multiple_of(offset, HALF)
            return jnp.concatenate([grads[pl.ds(i * TOKENS + offset, HALF), columns] for i in range(SIDE)], axis=0)

        value = jnp.dot(first[rows, depth], tokens(start), preferred_element_type=jnp.float32)
        value += jnp.dot(second[rows, depth], tokens(HALF - start), preferred_element_type=jnp.float32)
        out[:, columns] = value if total is None else value + total[rows, columns]


def product(place, first, second, grads, total, group, which=None):
    count = 2 * ROW_BLOCK if which is None else ROW_BLOCK
    operands = [first, second, grads] + ([] if total is None else [total])
    return pl.pallas_call(
        functools.partial(product_kernel, group, which),
        out_shape=shape(count, WIDTH),
        in_specs=[SCALARS] + [WHOLE] * len(operands),
        out_specs=WHOLE,
        compiler_params=PARAMS,
        cost_estimate=cost(2 * count * GROUP * WIDTH, 2**20),
    )(place, *operands)


def columns_kernel(mine, theirs, grad, sent):
    value = mine[...] + theirs[...]
    grad[...] = value
    sums = jnp.sum(value * value, axis=0, keepdims=True)
    tile = jnp.concatenate([sums[:, i * LANES : (i + 1) * LANES] for i in range(8)], axis=0)
    for i in range(DEVICES):
        sent[i] = tile


def columns(mine, theirs):
    return pl.pallas_call(
        columns_kernel,
        out_shape=(shape(ROW_BLOCK, WIDTH), shape(DEVICES, *TILE)),
        in_specs=[WHOLE] * 2,
        out_specs=(WHOLE, WHOLE),
        compiler_params=PARAMS,
        cost_estimate=cost(2**20, 3 * 2**20),
    )(mine, theirs)


def rows_kernel(received, moment, grad, weight, cols, col_root, sent):
    new = BETA_TWO * moment[...] + (1.0 - BETA_TWO) * (jnp.sum(received[...], axis=0) / D)
    cols[...] = new
    root = lax.rsqrt(new)
    col_root[...] = root
    sums = [jnp.zeros((ROW_BLOCK, LANES), jnp.float32)] * 4
    for i in range(WIDTH // LANES):
        lanes = slice(i * LANES, (i + 1) * LANES)
        value, held = grad[:, lanes], weight[:, lanes]
        by_cols = value * root[i : i + 1, :]
        terms = (value * value, by_cols * by_cols, by_cols * held, held * held)
        sums = [a + b for a, b in zip(sums, terms)]
    parts = []
    for value in sums:
        for row in range(0, ROW_BLOCK, LANES):
            parts.append(jnp.sum(value[row : row + LANES, :].T, axis=0, keepdims=True))
    tile = jnp.concatenate(parts, axis=0)
    for i in range(LAYERS):
        sent[i] = tile


def rows(received, moment, grad, weight):
    return pl.pallas_call(
        rows_kernel,
        out_shape=(shape(*TILE), shape(*TILE), shape(LAYERS, *TILE)),
        in_specs=[WHOLE] * 4,
        out_specs=(WHOLE, WHOLE, WHOLE),
        compiler_params=PARAMS,
        cost_estimate=cost(2**21, 2**21),
    )(received, moment, grad, weight)


def scalars_kernel(received, moment, rows_out, row_root, sent):
    parts = jnp.sum(received[...], axis=0)
    new = BETA_TWO * moment[...] + (1.0 - BETA_TWO) * (parts[0:2] / FF)
    rows_out[...] = new
    root = lax.rsqrt(new)
    row_root[...] = root
    sums = [jnp.sum(part, axis=0, keepdims=True) for part in (parts[2:4] * root * root, parts[4:6] * root, parts[6:8])]
    tile = jnp.concatenate(sums + [jnp.zeros_like(sums[0])], axis=0)
    for i in range(DEVICES):
        sent[i] = tile


def scalars(received, moment):
    return pl.pallas_call(
        scalars_kernel,
        out_shape=(shape(2, LANES), shape(2, LANES), shape(DEVICES, 4, LANES)),
        in_specs=[WHOLE] * 2,
        out_specs=(WHOLE, WHOLE, WHOLE),
        compiler_params=PARAMS,
        cost_estimate=cost(2**14, 2**18),
    )(received, moment)


def update_kernel(received, row_root, col_root, grad, weight, out, done, sems):
    parts = jnp.sum(received[...], axis=0)
    scaled_sum, cross_sum, weight_sum = (jnp.sum(parts[i : i + 1], keepdims=True) for i in range(3))
    factor = 1.0 / jnp.maximum(1.0, jnp.sqrt(scaled_sum / (D * FF)) / CLIP_LEVEL)
    direction_sum = (
        factor * factor * scaled_sum + 2.0 * WEIGHT_DECAY * factor * cross_sum + WEIGHT_DECAY * WEIGHT_DECAY * weight_sum
    )
    trust_ratio = jnp.sqrt(weight_sum / (jnp.maximum(direction_sum, 0.0) + EPSILON))
    by_row = row_root[...] * (trust_ratio * factor)
    by_col = col_root[...]
    decay = trust_ratio * WEIGHT_DECAY
    copies = []
    for half in range(2):
        here = slice(half * LANES, (half + 1) * LANES)
        scale = jnp.broadcast_to(by_row[half : half + 1, :], (LANES, LANES)).T
        for i in range(WIDTH // LANES):
            lanes = slice(i * LANES, (i + 1) * LANES)
            done[here, lanes] = grad[here, lanes] * by_col[i : i + 1, :] * scale + decay * weight[here, lanes]
        copies.append(pltpu.make_async_copy(done.at[here], out.at[here], sems.at[half]))
        copies[-1].start()
    for copy in copies:
        copy.wait()


def update(received, row_root, col_root, grad, weight):
    return pl.pallas_call(
        update_kernel,
        out_shape=shape(ROW_BLOCK, WIDTH),
        in_specs=[WHOLE] * 5,
        out_specs=ANYWHERE,
        scratch_shapes=[pltpu.VMEM((ROW_BLOCK, WIDTH), jnp.float32), pltpu.SemaphoreType.DMA((2,))],
        compiler_params=PARAMS,
        cost_estimate=cost(2**20, 3 * 2**20),
    )(received, row_root, col_root, grad, weight)


def shards(activations, out_grads, weight, row_moment, col_moment):
    y, x, core, layer = (lax.axis_index(name) for name in ("y", "x", "core", "z"))
    place = jnp.stack([y, x, core, layer & 1])
    line = [out_grads] + [along(out_grads, k, 0) for k in range(1, SIDE)]
    packed = pack(place, activations)
    packed, *line[1:] = lax.optimization_barrier((packed, *line[1:]))
    first = lax.all_to_all(packed, CHIPS, 0, 0)
    second = next_layer(first)
    line = join(line)
    grads = [line] + [along(line, j, 1) for j in range(1, SIDE)]
    first, second = turn(place, first), turn(place, second)
    total = None
    for j in range(SIDE - 1):
        total = product(place, first, second, grads[j], total, j)
    theirs = product(place, first, second, grads[-1], total, SIDE - 1, lambda core: 1 - core)
    received = lax.ppermute(theirs, "core", [(0, 1), (1, 0)])
    mine = product(place, first, second, grads[-1], total, SIDE - 1, lambda core: core)
    weight_grad, tiles = columns(mine, received)
    new_cols, col_root, tiles = rows(exchange(tiles, ROWS), col_moment.reshape(TILE), weight_grad, weight)
    new_rows, row_root, tiles = scalars(exchange(tiles, "z"), row_moment.reshape(2, LANES))
    out = update(exchange(tiles, ROWS), row_root, col_root, weight_grad, weight)
    return (out, new_rows.reshape(-1), new_cols.reshape(-1))


def solution(mesh):
    mesh = Mesh(mesh.devices.reshape(SIDE, SIDE, 2, LAYERS), ("y", "x", "core", "z"))
    placed = (P(ROWS, None), P(ROWS, "z"), P(ROWS, "z"), P(ROWS), P("z"))
    return jax.shard_map(
        shards,
        mesh=mesh,
        in_specs=placed,
        out_specs=(P(ROWS, "z"), P(ROWS), P("z")),
        check_vma=False,
    )
```

```python
import functools

import jax
import jax.numpy as jnp
from jax import lax
from jax.experimental import pallas as pl
from jax.experimental.pallas import tpu as pltpu
from jax.sharding import Mesh, PartitionSpec as P

D = 8192
FF = 16384


BETA_TWO = 0.8
CLIP_LEVEL = 0.25
WEIGHT_DECAY = 0.1
EPSILON = 1e-06

CHIPS = ("y", "x")
ROWS = ("y", "x", "core")
SIDE = 4
COUNT = SIDE * SIDE
LAYERS = 16
DEVICES = 2 * COUNT
TOKENS = 128
HALF = TOKENS // 2
GROUP = SIDE * TOKENS
ROW_BLOCK = 256
WIDTH = 1024
LANES = 128
COLUMNS = 256
TILE = (8, LANES)

ANYWHERE = pl.BlockSpec(memory_space=pl.ANY)
WHOLE = pl.BlockSpec(memory_space=pltpu.VMEM)
SCALARS = pl.BlockSpec(memory_space=pltpu.SMEM)
PARAMS = pltpu.CompilerParams(vmem_limit_bytes=16 * 2**20)


def shape(*dims, dtype=jnp.float32):
    return jax.ShapeDtypeStruct(dims, dtype)


def cost(flops, bytes_accessed):
    return pl.CostEstimate(flops=flops, bytes_accessed=bytes_accessed, transcendentals=0)


def device(y, x, core):
    return ((y % SIDE) * SIDE + x % SIDE) * 2 + core


def along(value, step, stage):
    pairs = []
    for y in range(SIDE):
        for x in range(SIDE):
            for core in range(2):
                on_x = core == stage
                to = device(y, x + step, core) if on_x else device(y + step, x, core)
                pairs.append((device(y, x, core), to))
    return lax.ppermute(value, ROWS, pairs)


def next_layer(value):
    pairs = [(i, (i + 1) % LAYERS) for i in range(LAYERS)]
    pairs += [(LAYERS + i, LAYERS + (i - 1) % LAYERS) for i in range(LAYERS)]
    return lax.ppermute(value, ("core", "z"), pairs)


def exchange(tiles, axes):
    return lax.all_to_all(tiles, axes, 0, 0)


def pack_kernel(place, source, out, sems):
    rows = pl.ds(pl.multiple_of(place[3] * HALF, HALF), HALF)
    copies = [
        pltpu.make_async_copy(source.at[rows, pl.ds(i * 2 * ROW_BLOCK, 2 * ROW_BLOCK)], out.at[i], sems.at[i])
        for i in range(COUNT)
    ]
    for copy in copies:
        copy.start()
    for copy in copies:
        copy.wait()


def pack(place, activations):
    return pl.pallas_call(
        pack_kernel,
        out_shape=shape(COUNT, HALF, 2 * ROW_BLOCK, dtype=jnp.bfloat16),
        in_specs=[SCALARS, pl.BlockSpec(memory_space=pltpu.HBM)],
        out_specs=ANYWHERE,
        scratch_shapes=[pltpu.SemaphoreType.DMA((COUNT,))],
        compiler_params=PARAMS,
        cost_estimate=cost(0, 2**21),
    )(place, activations)


def join_kernel(*refs):
    blocks, out, sems = refs[:-2], refs[-2], refs[-1]
    copies = [
        pltpu.make_async_copy(block, out.at[pl.ds(i * TOKENS, TOKENS)], sems.at[i]) for i, block in enumerate(blocks)
    ]
    for copy in copies:
        copy.start()
    for copy in copies:
        copy.wait()


def join(blocks):
    return pl.pallas_call(
        join_kernel,
        out_shape=shape(GROUP, WIDTH, dtype=jnp.bfloat16),
        in_specs=[ANYWHERE] * len(blocks),
        out_specs=ANYWHERE,
        scratch_shapes=[pltpu.SemaphoreType.DMA((len(blocks),))],
        compiler_params=PARAMS,
        cost_estimate=cost(0, 2**21),
    )(*blocks)


def turn_kernel(place, part, out):
    y, x, core = place[0], place[1], place[2]

    def block(i):
        j, k = i // SIDE, i % SIDE
        dx, dy = jnp.where(core == 0, k, j), jnp.where(core == 0, j, k)
        return part[((y - dy) & (SIDE - 1)) * SIDE + ((x - dx) & (SIDE - 1))]

    for i in range(0, COUNT, 2):
        out[:, i * HALF : (i + 2) * HALF] = jnp.concatenate([block(i), block(i + 1)], axis=0).T


def turn(place, part):
    return pl.pallas_call(
        turn_kernel,
        out_shape=shape(2 * ROW_BLOCK, COUNT * HALF, dtype=jnp.bfloat16),
        in_specs=[SCALARS, WHOLE],
        out_specs=WHOLE,
        compiler_params=PARAMS,
        cost_estimate=cost(0, 2**21),
    )(place, part)


def product_kernel(parts, which, place, *refs):
    operands, out = refs[:-1], refs[-1]
    total = None if len(operands) == 1 + max(max(part[:2]) for part in parts) else operands[-1]
    start = place[3] * HALF
    rows = pl.ds(0 if which is None else pl.multiple_of(which(place[2]) * ROW_BLOCK, ROW_BLOCK), out.shape[0])

    @pl.loop(0, WIDTH // COLUMNS)
    def _(n):
        columns = pl.ds(pl.multiple_of(n * COLUMNS, COLUMNS), COLUMNS)
        value = None if total is None else total[rows, columns]
        for turned, grads, group, exchanged in parts:
            offset = pl.multiple_of(start if exchanged else HALF - start, HALF)
            blocks = [operands[grads][pl.ds(i * TOKENS + offset, HALF), columns] for i in range(SIDE)]
            features = operands[turned][rows, group * SIDE * HALF : (group + 1) * SIDE * HALF]
            term = jnp.dot(features, jnp.concatenate(blocks, axis=0), preferred_element_type=jnp.float32)
            value = term if value is None else value + term
        out[:, columns] = value


def product(place, operands, parts, total=None, which=None):
    count = 2 * ROW_BLOCK if which is None else ROW_BLOCK
    operands = operands + ([] if total is None else [total])
    return pl.pallas_call(
        functools.partial(product_kernel, parts, which),
        out_shape=shape(count, WIDTH),
        in_specs=[SCALARS] + [WHOLE] * len(operands),
        out_specs=WHOLE,
        compiler_params=PARAMS,
        cost_estimate=cost(2 * count * SIDE * HALF * WIDTH * len(parts), 2**20),
    )(place, *operands)


def columns_kernel(mine, theirs, grad, sent):
    value = mine[...] + theirs[...]
    grad[...] = value
    sums = jnp.sum(value * value, axis=0, keepdims=True)
    tile = jnp.concatenate([sums[:, i * LANES : (i + 1) * LANES] for i in range(8)], axis=0)
    for i in range(DEVICES):
        sent[i] = tile


def columns(mine, theirs):
    return pl.pallas_call(
        columns_kernel,
        out_shape=(shape(ROW_BLOCK, WIDTH), shape(DEVICES, *TILE)),
        in_specs=[WHOLE] * 2,
        out_specs=(WHOLE, WHOLE),
        compiler_params=PARAMS,
        cost_estimate=cost(2**20, 3 * 2**20),
    )(mine, theirs)


def rows_kernel(received, moment, grad, weight, cols, col_root, sent):
    new = BETA_TWO * moment[...] + (1.0 - BETA_TWO) * (jnp.sum(received[...], axis=0) / D)
    cols[...] = new
    root = lax.rsqrt(new)
    col_root[...] = root
    sums = [jnp.zeros((ROW_BLOCK, LANES), jnp.float32)] * 4
    for i in range(WIDTH // LANES):
        lanes = slice(i * LANES, (i + 1) * LANES)
        value, held = grad[:, lanes], weight[:, lanes]
        by_cols = value * root[i : i + 1, :]
        terms = (value * value, by_cols * by_cols, by_cols * held, held * held)
        sums = [a + b for a, b in zip(sums, terms)]
    parts = []
    for value in sums:
        for row in range(0, ROW_BLOCK, LANES):
            parts.append(jnp.sum(value[row : row + LANES, :].T, axis=0, keepdims=True))
    tile = jnp.concatenate(parts, axis=0)
    for i in range(LAYERS):
        sent[i] = tile


def rows(received, moment, grad, weight):
    return pl.pallas_call(
        rows_kernel,
        out_shape=(shape(*TILE), shape(*TILE), shape(LAYERS, *TILE)),
        in_specs=[WHOLE] * 4,
        out_specs=(WHOLE, WHOLE, WHOLE),
        compiler_params=PARAMS,
        cost_estimate=cost(2**21, 2**21),
    )(received, moment, grad, weight)


def scalars_kernel(received, moment, rows_out, row_root, sent):
    parts = jnp.sum(received[...], axis=0)
    new = BETA_TWO * moment[...] + (1.0 - BETA_TWO) * (parts[0:2] / FF)
    rows_out[...] = new
    root = lax.rsqrt(new)
    row_root[...] = root
    sums = [jnp.sum(part, axis=0, keepdims=True) for part in (parts[2:4] * root * root, parts[4:6] * root, parts[6:8])]
    tile = jnp.concatenate(sums + [jnp.zeros_like(sums[0])], axis=0)
    for i in range(DEVICES):
        sent[i] = tile


def scalars(received, moment):
    return pl.pallas_call(
        scalars_kernel,
        out_shape=(shape(2, LANES), shape(2, LANES), shape(DEVICES, 4, LANES)),
        in_specs=[WHOLE] * 2,
        out_specs=(WHOLE, WHOLE, WHOLE),
        compiler_params=PARAMS,
        cost_estimate=cost(2**14, 2**18),
    )(received, moment)


def update_kernel(received, row_root, col_root, grad, weight, out, done, sems):
    parts = jnp.sum(received[...], axis=0)
    scaled_sum, cross_sum, weight_sum = (jnp.sum(parts[i : i + 1], keepdims=True) for i in range(3))
    factor = 1.0 / jnp.maximum(1.0, jnp.sqrt(scaled_sum / (D * FF)) / CLIP_LEVEL)
    direction_sum = (
        factor * factor * scaled_sum + 2.0 * WEIGHT_DECAY * factor * cross_sum + WEIGHT_DECAY * WEIGHT_DECAY * weight_sum
    )
    trust_ratio = jnp.sqrt(weight_sum / (jnp.maximum(direction_sum, 0.0) + EPSILON))
    by_row = row_root[...] * (trust_ratio * factor)
    by_col = col_root[...]
    decay = trust_ratio * WEIGHT_DECAY
    copies = []
    for half in range(2):
        here = slice(half * LANES, (half + 1) * LANES)
        scale = jnp.broadcast_to(by_row[half : half + 1, :], (LANES, LANES)).T
        for i in range(WIDTH // LANES):
            lanes = slice(i * LANES, (i + 1) * LANES)
            done[here, lanes] = grad[here, lanes] * by_col[i : i + 1, :] * scale + decay * weight[here, lanes]
        copies.append(pltpu.make_async_copy(done.at[here], out.at[here], sems.at[half]))
        copies[-1].start()
    for copy in copies:
        copy.wait()


def update(received, row_root, col_root, grad, weight):
    return pl.pallas_call(
        update_kernel,
        out_shape=shape(ROW_BLOCK, WIDTH),
        in_specs=[WHOLE] * 5,
        out_specs=ANYWHERE,
        scratch_shapes=[pltpu.VMEM((ROW_BLOCK, WIDTH), jnp.float32), pltpu.SemaphoreType.DMA((2,))],
        compiler_params=PARAMS,
        cost_estimate=cost(2**20, 3 * 2**20),
    )(received, row_root, col_root, grad, weight)


def shards(activations, out_grads, weight, row_moment, col_moment):
    y, x, core, layer = (lax.axis_index(name) for name in ("y", "x", "core", "z"))
    place = jnp.stack([y, x, core, layer & 1])
    line = [out_grads] + [along(out_grads, k, 0) for k in range(1, SIDE)]
    packed = pack(place, activations)
    packed, *line[1:] = lax.optimization_barrier((packed, *line[1:]))
    first = lax.all_to_all(packed, CHIPS, 0, 0)
    second = next_layer(first)
    line = join(line)
    grads = [line] + [along(line, j, 1) for j in range(1, SIDE)]
    first = turn(place, first)
    total = None
    for j in range(SIDE - 1):
        total = product(place, [first, grads[j]], [(0, 1, j, True)], total)
    second, *grads = lax.optimization_barrier((second, *grads))
    operands = [first, turn(place, second)] + grads
    parts = [(0, 1 + SIDE, SIDE - 1, True)] + [(1, 2 + j, j, False) for j in range(SIDE)]
    theirs = product(place, operands, parts, total, lambda core: 1 - core)
    received = lax.ppermute(theirs, "core", [(0, 1), (1, 0)])
    mine = product(place, operands, parts, total, lambda core: core)
    weight_grad, tiles = columns(mine, received)
    new_cols, col_root, tiles = rows(exchange(tiles, ROWS), col_moment.reshape(TILE), weight_grad, weight)
    new_rows, row_root, tiles = scalars(exchange(tiles, "z"), row_moment.reshape(2, LANES))
    out = update(exchange(tiles, ROWS), row_root, col_root, weight_grad, weight)
    return (out, new_rows.reshape(-1), new_cols.reshape(-1))


def solution(mesh):
    mesh = Mesh(mesh.devices.reshape(SIDE, SIDE, 2, LAYERS), ("y", "x", "core", "z"))
    placed = (P(ROWS, None), P(ROWS, "z"), P(ROWS, "z"), P(ROWS), P("z"))
    return jax.shard_map(
        shards,
        mesh=mesh,
        in_specs=placed,
        out_specs=(P(ROWS, "z"), P(ROWS), P("z")),
        check_vma=False,
    )
```

```python
import functools

import jax
import jax.numpy as jnp
from jax import lax
from jax.experimental import pallas as pl
from jax.experimental.pallas import tpu as pltpu
from jax.sharding import Mesh, PartitionSpec as P

D = 8192
FF = 16384


BETA_TWO = 0.8
CLIP_LEVEL = 0.25
WEIGHT_DECAY = 0.1
EPSILON = 1e-06

CHIPS = ("y", "x")
ROWS = ("y", "x", "core")
SIDE = 4
COUNT = SIDE * SIDE
LAYERS = 16
DEVICES = 2 * COUNT
TOKENS = 128
HALF = TOKENS // 2
ROW_BLOCK = 256
WIDTH = 1024
LANES = 128
COLUMNS = 256
TILE = (8, LANES)

ANYWHERE = pl.BlockSpec(memory_space=pl.ANY)
WHOLE = pl.BlockSpec(memory_space=pltpu.VMEM)
SCALARS = pl.BlockSpec(memory_space=pltpu.SMEM)
PARAMS = pltpu.CompilerParams(vmem_limit_bytes=16 * 2**20)


def shape(*dims, dtype=jnp.float32):
    return jax.ShapeDtypeStruct(dims, dtype)


def cost(flops, bytes_accessed):
    return pl.CostEstimate(flops=flops, bytes_accessed=bytes_accessed, transcendentals=0)


def device(y, x, core):
    return ((y % SIDE) * SIDE + x % SIDE) * 2 + core


def along(value, step, stage):
    pairs = []
    for y in range(SIDE):
        for x in range(SIDE):
            for core in range(2):
                on_x = core == stage
                to = device(y, x + step, core) if on_x else device(y + step, x, core)
                pairs.append((device(y, x, core), to))
    return lax.ppermute(value, ROWS, pairs)


def next_layer(value):
    pairs = [(i, (i + 1) % LAYERS) for i in range(LAYERS)]
    pairs += [(LAYERS + i, LAYERS + (i - 1) % LAYERS) for i in range(LAYERS)]
    return lax.ppermute(value, ("core", "z"), pairs)


def exchange(tiles, axes):
    return lax.all_to_all(tiles, axes, 0, 0)


def pack_kernel(place, source, out, sems):
    rows = pl.ds(pl.multiple_of(place[3] * HALF, HALF), HALF)
    copies = [
        pltpu.make_async_copy(source.at[rows, pl.ds(i * 2 * ROW_BLOCK, 2 * ROW_BLOCK)], out.at[i], sems.at[i])
        for i in range(COUNT)
    ]
    for copy in copies:
        copy.start()
    for copy in copies:
        copy.wait()


def pack(place, activations):
    return pl.pallas_call(
        pack_kernel,
        out_shape=shape(COUNT, HALF, 2 * ROW_BLOCK, dtype=jnp.bfloat16),
        in_specs=[SCALARS, ANYWHERE],
        out_specs=ANYWHERE,
        scratch_shapes=[pltpu.SemaphoreType.DMA((COUNT,))],
        compiler_params=PARAMS,
        cost_estimate=cost(0, 2**21),
    )(place, pltpu.with_memory_space_constraint(activations, pltpu.HBM))


def join_kernel(*refs):
    blocks, out, sems = refs[:-2], refs[-2], refs[-1]
    copies = [
        pltpu.make_async_copy(block, out.at[pl.ds(i * TOKENS, TOKENS)], sems.at[i]) for i, block in enumerate(blocks)
    ]
    for copy in copies:
        copy.start()
    for copy in copies:
        copy.wait()


def join(blocks):
    return pl.pallas_call(
        join_kernel,
        out_shape=shape(len(blocks) * TOKENS, WIDTH, dtype=jnp.bfloat16),
        in_specs=[ANYWHERE] * len(blocks),
        out_specs=ANYWHERE,
        scratch_shapes=[pltpu.SemaphoreType.DMA((len(blocks),))],
        compiler_params=PARAMS,
        cost_estimate=cost(0, 2**21),
    )(*blocks)


def turn_kernel(place, part, out):
    y, x, core = place[0], place[1], place[2]

    def block(i):
        j, k = i // SIDE, i % SIDE
        dx, dy = jnp.where(core == 0, k, j), jnp.where(core == 0, j, k)
        return part[((y - dy) & (SIDE - 1)) * SIDE + ((x - dx) & (SIDE - 1))]

    for i in range(0, COUNT, 2):
        out[:, i * HALF : (i + 2) * HALF] = jnp.concatenate([block(i), block(i + 1)], axis=0).T


def turn(place, part):
    return pl.pallas_call(
        turn_kernel,
        out_shape=shape(2 * ROW_BLOCK, COUNT * HALF, dtype=jnp.bfloat16),
        in_specs=[SCALARS, WHOLE],
        out_specs=WHOLE,
        compiler_params=PARAMS,
        cost_estimate=cost(0, 2**21),
    )(place, part)


def product_kernel(parts, which, place, *refs):
    operands, out = refs[:-1], refs[-1]
    total = None if len(operands) == 2 + max(part[1] for part in parts) else operands[-1]
    start = place[3] * HALF
    rows = pl.ds(0 if which is None else pl.multiple_of(which(place[2]) * ROW_BLOCK, ROW_BLOCK), out.shape[0])

    @pl.loop(0, WIDTH // COLUMNS)
    def _(n):
        columns = pl.ds(pl.multiple_of(n * COLUMNS, COLUMNS), COLUMNS)
        value = None if total is None else total[rows, columns]
        for turned, grads, group, exchanged in parts:
            offset = pl.multiple_of(start if exchanged else HALF - start, HALF)
            blocks = [operands[grads][pl.ds(offset, HALF), columns]]
            blocks += [operands[grads + 1][pl.ds(i * TOKENS + offset, HALF), columns] for i in range(SIDE - 1)]
            features = operands[turned][rows, group * SIDE * HALF : (group + 1) * SIDE * HALF]
            term = jnp.dot(features, jnp.concatenate(blocks, axis=0), preferred_element_type=jnp.float32)
            value = term if value is None else value + term
        out[:, columns] = value


def product(place, operands, parts, total=None, which=None):
    count = 2 * ROW_BLOCK if which is None else ROW_BLOCK
    operands = operands + ([] if total is None else [total])
    return pl.pallas_call(
        functools.partial(product_kernel, parts, which),
        out_shape=shape(count, WIDTH),
        in_specs=[SCALARS] + [WHOLE] * len(operands),
        out_specs=WHOLE,
        compiler_params=PARAMS,
        cost_estimate=cost(2 * count * SIDE * HALF * WIDTH * len(parts), 2**20),
    )(place, *operands)


def columns_kernel(mine, theirs, grad, sent):
    value = mine[...] + theirs[...]
    grad[...] = value
    sums = jnp.sum(value * value, axis=0, keepdims=True)
    tile = jnp.concatenate([sums[:, i * LANES : (i + 1) * LANES] for i in range(8)], axis=0)
    for i in range(DEVICES):
        sent[i] = tile


def columns(mine, theirs):
    return pl.pallas_call(
        columns_kernel,
        out_shape=(shape(ROW_BLOCK, WIDTH), shape(DEVICES, *TILE)),
        in_specs=[WHOLE] * 2,
        out_specs=(WHOLE, WHOLE),
        compiler_params=PARAMS,
        cost_estimate=cost(2**20, 3 * 2**20),
    )(mine, theirs)


def rows_kernel(received, moment, grad, weight, cols, col_root, sent):
    new = BETA_TWO * moment[...] + (1.0 - BETA_TWO) * (jnp.sum(received[...], axis=0) / D)
    cols[...] = new
    root = lax.rsqrt(new)
    col_root[...] = root
    sums = [jnp.zeros((ROW_BLOCK, LANES), jnp.float32)] * 4
    for i in range(WIDTH // LANES):
        lanes = slice(i * LANES, (i + 1) * LANES)
        value, held = grad[:, lanes], weight[:, lanes]
        by_cols = value * root[i : i + 1, :]
        terms = (value * value, by_cols * by_cols, by_cols * held, held * held)
        sums = [a + b for a, b in zip(sums, terms)]
    parts = []
    for value in sums:
        for row in range(0, ROW_BLOCK, LANES):
            parts.append(jnp.sum(value[row : row + LANES, :].T, axis=0, keepdims=True))
    tile = jnp.concatenate(parts, axis=0)
    for i in range(LAYERS):
        sent[i] = tile


def rows(received, moment, grad, weight):
    return pl.pallas_call(
        rows_kernel,
        out_shape=(shape(*TILE), shape(*TILE), shape(LAYERS, *TILE)),
        in_specs=[WHOLE] * 4,
        out_specs=(WHOLE, WHOLE, WHOLE),
        compiler_params=PARAMS,
        cost_estimate=cost(2**21, 2**21),
    )(received, moment, grad, weight)


def scalars_kernel(received, moment, rows_out, row_root, sent):
    parts = jnp.sum(received[...], axis=0)
    new = BETA_TWO * moment[...] + (1.0 - BETA_TWO) * (parts[0:2] / FF)
    rows_out[...] = new
    root = lax.rsqrt(new)
    row_root[...] = root
    sums = [jnp.sum(part, axis=0, keepdims=True) for part in (parts[2:4] * root * root, parts[4:6] * root, parts[6:8])]
    tile = jnp.concatenate(sums + [jnp.zeros_like(sums[0])], axis=0)
    for i in range(DEVICES):
        sent[i] = tile


def scalars(received, moment):
    return pl.pallas_call(
        scalars_kernel,
        out_shape=(shape(2, LANES), shape(2, LANES), shape(DEVICES, 4, LANES)),
        in_specs=[WHOLE] * 2,
        out_specs=(WHOLE, WHOLE, WHOLE),
        compiler_params=PARAMS,
        cost_estimate=cost(2**14, 2**18),
    )(received, moment)


def update_kernel(received, row_root, col_root, grad, weight, out, done, sems):
    parts = jnp.sum(received[...], axis=0)
    scaled_sum, cross_sum, weight_sum = (jnp.sum(parts[i : i + 1], keepdims=True) for i in range(3))
    factor = 1.0 / jnp.maximum(1.0, jnp.sqrt(scaled_sum / (D * FF)) / CLIP_LEVEL)
    direction_sum = (
        factor * factor * scaled_sum + 2.0 * WEIGHT_DECAY * factor * cross_sum + WEIGHT_DECAY * WEIGHT_DECAY * weight_sum
    )
    trust_ratio = jnp.sqrt(weight_sum / (jnp.maximum(direction_sum, 0.0) + EPSILON))
    by_row = row_root[...] * (trust_ratio * factor)
    by_col = col_root[...]
    decay = trust_ratio * WEIGHT_DECAY
    copies = []
    for half in range(2):
        here = slice(half * LANES, (half + 1) * LANES)
        scale = jnp.broadcast_to(by_row[half : half + 1, :], (LANES, LANES)).T
        for i in range(WIDTH // LANES):
            lanes = slice(i * LANES, (i + 1) * LANES)
            done[here, lanes] = grad[here, lanes] * by_col[i : i + 1, :] * scale + decay * weight[here, lanes]
        copies.append(pltpu.make_async_copy(done.at[here], out.at[here], sems.at[half]))
        copies[-1].start()
    for copy in copies:
        copy.wait()


def update(received, row_root, col_root, grad, weight):
    return pl.pallas_call(
        update_kernel,
        out_shape=shape(ROW_BLOCK, WIDTH),
        in_specs=[WHOLE] * 5,
        out_specs=ANYWHERE,
        scratch_shapes=[pltpu.VMEM((ROW_BLOCK, WIDTH), jnp.float32), pltpu.SemaphoreType.DMA((2,))],
        compiler_params=PARAMS,
        cost_estimate=cost(2**20, 3 * 2**20),
    )(received, row_root, col_root, grad, weight)


def shards(activations, out_grads, weight, row_moment, col_moment):
    y, x, core, layer = (lax.axis_index(name) for name in ("y", "x", "core", "z"))
    place = jnp.stack([y, x, core, layer & 1])
    first = exchange(pack(place, activations), CHIPS)
    second = next_layer(first)
    line = [along(out_grads, k, 0) for k in range(1, SIDE)]
    grads = [out_grads] + [along(out_grads, j, 1) for j in range(1, SIDE)]
    line, grads[1:] = lax.optimization_barrier((line, grads[1:]))
    line = join(line)
    lines = [line] + [along(line, j, 1) for j in range(1, SIDE)]
    first = turn(place, first)
    total = None
    for j in range(SIDE - 1):
        total = product(place, [first, grads[j], lines[j]], [(0, 1, j, True)], total)
    second, *lines = lax.optimization_barrier((second, *lines))
    operands = [first, turn(place, second)] + [block for pair in zip(grads, lines) for block in pair]
    parts = [(0, 2 * SIDE, SIDE - 1, True)] + [(1, 2 + 2 * j, j, False) for j in range(SIDE)]
    theirs = product(place, operands, parts, total, lambda core: 1 - core)
    received = lax.ppermute(theirs, "core", [(0, 1), (1, 0)])
    mine = product(place, operands, parts, total, lambda core: core)
    weight_grad, tiles = columns(mine, received)
    new_cols, col_root, tiles = rows(exchange(tiles, ROWS), col_moment.reshape(TILE), weight_grad, weight)
    new_rows, row_root, tiles = scalars(exchange(tiles, "z"), row_moment.reshape(2, LANES))
    out = update(exchange(tiles, ROWS), row_root, col_root, weight_grad, weight)
    return (out, new_rows.reshape(-1), new_cols.reshape(-1))


def solution(mesh):
    mesh = Mesh(mesh.devices.reshape(SIDE, SIDE, 2, LAYERS), ("y", "x", "core", "z"))
    placed = (P(ROWS, None), P(ROWS, "z"), P(ROWS, "z"), P(ROWS), P("z"))
    return jax.shard_map(
        shards,
        mesh=mesh,
        in_specs=placed,
        out_specs=(P(ROWS, "z"), P(ROWS), P("z")),
        check_vma=False,
    )
```

```python
import functools

import jax
import jax.numpy as jnp
from jax import lax
from jax.experimental import pallas as pl
from jax.experimental.pallas import tpu as pltpu
from jax.sharding import Mesh, PartitionSpec as P

D = 8192
FF = 16384


BETA_TWO = 0.8
CLIP_LEVEL = 0.25
WEIGHT_DECAY = 0.1
EPSILON = 1e-06

CHIPS = ("y", "x")
ROWS = ("y", "x", "core")
SIDE = 4
COUNT = SIDE * SIDE
LAYERS = 16
DEVICES = 2 * COUNT
TOKENS = 128
HALF = TOKENS // 2
ROW_BLOCK = 256
WIDTH = 1024
LANES = 128
COLUMNS = 256
TILE = (8, LANES)

ANYWHERE = pl.BlockSpec(memory_space=pl.ANY)
WHOLE = pl.BlockSpec(memory_space=pltpu.VMEM)
SCALARS = pl.BlockSpec(memory_space=pltpu.SMEM)
PARAMS = pltpu.CompilerParams(vmem_limit_bytes=16 * 2**20)


def shape(*dims, dtype=jnp.float32):
    return jax.ShapeDtypeStruct(dims, dtype)


def cost(flops, bytes_accessed):
    return pl.CostEstimate(flops=flops, bytes_accessed=bytes_accessed, transcendentals=0)


def device(y, x, core):
    return ((y % SIDE) * SIDE + x % SIDE) * 2 + core


def along(value, step, stage):
    pairs = []
    for y in range(SIDE):
        for x in range(SIDE):
            for core in range(2):
                on_x = core == stage
                to = device(y, x + step, core) if on_x else device(y + step, x, core)
                pairs.append((device(y, x, core), to))
    return lax.ppermute(value, ROWS, pairs)


def next_layer(value):
    pairs = [(i, (i + 1) % LAYERS) for i in range(LAYERS)]
    pairs += [(LAYERS + i, LAYERS + (i - 1) % LAYERS) for i in range(LAYERS)]
    return lax.ppermute(value, ("core", "z"), pairs)


def exchange(tiles, axes):
    return lax.all_to_all(tiles, axes, 0, 0)


def pack_kernel(place, source, out, sems):
    rows = pl.ds(pl.multiple_of(place[3] * HALF, HALF), HALF)
    copies = [
        pltpu.make_async_copy(source.at[rows, pl.ds(i * 2 * ROW_BLOCK, 2 * ROW_BLOCK)], out.at[i], sems.at[i])
        for i in range(COUNT)
    ]
    for copy in copies:
        copy.start()
    for copy in copies:
        copy.wait()


def pack(place, activations):
    return pl.pallas_call(
        pack_kernel,
        out_shape=shape(COUNT, HALF, 2 * ROW_BLOCK, dtype=jnp.bfloat16),
        in_specs=[SCALARS, ANYWHERE],
        out_specs=WHOLE,
        scratch_shapes=[pltpu.SemaphoreType.DMA((COUNT,))],
        compiler_params=PARAMS,
        cost_estimate=cost(0, 2**21),
    )(place, pltpu.with_memory_space_constraint(activations, pltpu.HBM))


def join_kernel(*refs):
    blocks, out, sems = refs[:-2], refs[-2], refs[-1]
    copies = [
        pltpu.make_async_copy(block, out.at[pl.ds(i * TOKENS, TOKENS)], sems.at[i]) for i, block in enumerate(blocks)
    ]
    for copy in copies:
        copy.start()
    for copy in copies:
        copy.wait()


def join(blocks):
    return pl.pallas_call(
        join_kernel,
        out_shape=shape(len(blocks) * TOKENS, WIDTH, dtype=jnp.bfloat16),
        in_specs=[ANYWHERE] * len(blocks),
        out_specs=ANYWHERE,
        scratch_shapes=[pltpu.SemaphoreType.DMA((len(blocks),))],
        compiler_params=PARAMS,
        cost_estimate=cost(0, 2**21),
    )(*blocks)


def turn_kernel(place, part, out):
    y, x, core = place[0], place[1], place[2]

    def block(i):
        j, k = i // SIDE, i % SIDE
        dx, dy = jnp.where(core == 0, k, j), jnp.where(core == 0, j, k)
        return part[((y - dy) & (SIDE - 1)) * SIDE + ((x - dx) & (SIDE - 1))]

    for i in range(0, COUNT, 2):
        out[:, i * HALF : (i + 2) * HALF] = jnp.concatenate([block(i), block(i + 1)], axis=0).T


def turn(place, part):
    return pl.pallas_call(
        turn_kernel,
        out_shape=shape(2 * ROW_BLOCK, COUNT * HALF, dtype=jnp.bfloat16),
        in_specs=[SCALARS, WHOLE],
        out_specs=WHOLE,
        compiler_params=PARAMS,
        cost_estimate=cost(0, 2**21),
    )(place, part)


def product_kernel(parts, which, place, *refs):
    operands, out = refs[:-1], refs[-1]
    total = None if len(operands) == 2 + max(part[1] for part in parts) else operands[-1]
    start = place[3] * HALF
    rows = pl.ds(0 if which is None else pl.multiple_of(which(place[2]) * ROW_BLOCK, ROW_BLOCK), out.shape[0])

    @pl.loop(0, WIDTH // COLUMNS)
    def _(n):
        columns = pl.ds(pl.multiple_of(n * COLUMNS, COLUMNS), COLUMNS)
        value = None if total is None else total[rows, columns]
        for turned, grads, group, exchanged in parts:
            offset = pl.multiple_of(start if exchanged else HALF - start, HALF)
            blocks = [operands[grads][pl.ds(offset, HALF), columns]]
            blocks += [operands[grads + 1][pl.ds(i * TOKENS + offset, HALF), columns] for i in range(SIDE - 1)]
            features = operands[turned][rows, group * SIDE * HALF : (group + 1) * SIDE * HALF]
            term = jnp.dot(features, jnp.concatenate(blocks, axis=0), preferred_element_type=jnp.float32)
            value = term if value is None else value + term
        out[:, columns] = value


def product(place, operands, parts, total=None, which=None):
    count = 2 * ROW_BLOCK if which is None else ROW_BLOCK
    operands = operands + ([] if total is None else [total])
    return pl.pallas_call(
        functools.partial(product_kernel, parts, which),
        out_shape=shape(count, WIDTH),
        in_specs=[SCALARS] + [WHOLE] * len(operands),
        out_specs=WHOLE,
        compiler_params=PARAMS,
        cost_estimate=cost(2 * count * SIDE * HALF * WIDTH * len(parts), 2**20),
    )(place, *operands)


def columns_kernel(mine, theirs, grad, sent):
    value = mine[...] + theirs[...]
    grad[...] = value
    sums = jnp.sum(value * value, axis=0, keepdims=True)
    tile = jnp.concatenate([sums[:, i * LANES : (i + 1) * LANES] for i in range(8)], axis=0)
    for i in range(DEVICES):
        sent[i] = tile


def columns(mine, theirs):
    return pl.pallas_call(
        columns_kernel,
        out_shape=(shape(ROW_BLOCK, WIDTH), shape(DEVICES, *TILE)),
        in_specs=[WHOLE] * 2,
        out_specs=(WHOLE, WHOLE),
        compiler_params=PARAMS,
        cost_estimate=cost(2**20, 3 * 2**20),
    )(mine, theirs)


def rows_kernel(received, moment, grad, weight, cols, col_root, sent):
    new = BETA_TWO * moment[...] + (1.0 - BETA_TWO) * (jnp.sum(received[...], axis=0) / D)
    cols[...] = new
    root = lax.rsqrt(new)
    col_root[...] = root
    sums = [jnp.zeros((ROW_BLOCK, LANES), jnp.float32)] * 4
    for i in range(WIDTH // LANES):
        lanes = slice(i * LANES, (i + 1) * LANES)
        value, held = grad[:, lanes], weight[:, lanes]
        by_cols = value * root[i : i + 1, :]
        terms = (value * value, by_cols * by_cols, by_cols * held, held * held)
        sums = [a + b for a, b in zip(sums, terms)]
    parts = []
    for value in sums:
        for row in range(0, ROW_BLOCK, LANES):
            parts.append(jnp.sum(value[row : row + LANES, :].T, axis=0, keepdims=True))
    tile = jnp.concatenate(parts, axis=0)
    for i in range(LAYERS):
        sent[i] = tile


def rows(received, moment, grad, weight):
    return pl.pallas_call(
        rows_kernel,
        out_shape=(shape(*TILE), shape(*TILE), shape(LAYERS, *TILE)),
        in_specs=[WHOLE] * 4,
        out_specs=(WHOLE, WHOLE, WHOLE),
        compiler_params=PARAMS,
        cost_estimate=cost(2**21, 2**21),
    )(received, moment, grad, weight)


def scalars_kernel(received, moment, rows_out, row_root, sent):
    parts = jnp.sum(received[...], axis=0)
    new = BETA_TWO * moment[...] + (1.0 - BETA_TWO) * (parts[0:2] / FF)
    rows_out[...] = new
    root = lax.rsqrt(new)
    row_root[...] = root
    sums = [jnp.sum(part, axis=0, keepdims=True) for part in (parts[2:4] * root * root, parts[4:6] * root, parts[6:8])]
    tile = jnp.concatenate(sums + [jnp.zeros_like(sums[0])], axis=0)
    for i in range(DEVICES):
        sent[i] = tile


def scalars(received, moment):
    return pl.pallas_call(
        scalars_kernel,
        out_shape=(shape(2, LANES), shape(2, LANES), shape(DEVICES, 4, LANES)),
        in_specs=[WHOLE] * 2,
        out_specs=(WHOLE, WHOLE, WHOLE),
        compiler_params=PARAMS,
        cost_estimate=cost(2**14, 2**18),
    )(received, moment)


def update_kernel(received, row_root, col_root, grad, weight, out, done, sems):
    parts = jnp.sum(received[...], axis=0)
    scaled_sum, cross_sum, weight_sum = (jnp.sum(parts[i : i + 1], keepdims=True) for i in range(3))
    factor = 1.0 / jnp.maximum(1.0, jnp.sqrt(scaled_sum / (D * FF)) / CLIP_LEVEL)
    direction_sum = (
        factor * factor * scaled_sum + 2.0 * WEIGHT_DECAY * factor * cross_sum + WEIGHT_DECAY * WEIGHT_DECAY * weight_sum
    )
    trust_ratio = jnp.sqrt(weight_sum / (jnp.maximum(direction_sum, 0.0) + EPSILON))
    by_row = row_root[...] * (trust_ratio * factor)
    by_col = col_root[...]
    decay = trust_ratio * WEIGHT_DECAY
    copies = []
    for half in range(2):
        here = slice(half * LANES, (half + 1) * LANES)
        scale = jnp.broadcast_to(by_row[half : half + 1, :], (LANES, LANES)).T
        for i in range(WIDTH // LANES):
            lanes = slice(i * LANES, (i + 1) * LANES)
            done[here, lanes] = grad[here, lanes] * by_col[i : i + 1, :] * scale + decay * weight[here, lanes]
        copies.append(pltpu.make_async_copy(done.at[here], out.at[here], sems.at[half]))
        copies[-1].start()
    for copy in copies:
        copy.wait()


def update(received, row_root, col_root, grad, weight):
    return pl.pallas_call(
        update_kernel,
        out_shape=shape(ROW_BLOCK, WIDTH),
        in_specs=[WHOLE] * 5,
        out_specs=ANYWHERE,
        scratch_shapes=[pltpu.VMEM((ROW_BLOCK, WIDTH), jnp.float32), pltpu.SemaphoreType.DMA((2,))],
        compiler_params=PARAMS,
        cost_estimate=cost(2**20, 3 * 2**20),
    )(received, row_root, col_root, grad, weight)


def shards(activations, out_grads, weight, row_moment, col_moment):
    y, x, core, layer = (lax.axis_index(name) for name in ("y", "x", "core", "z"))
    place = jnp.stack([y, x, core, layer & 1])
    first = exchange(pack(place, activations), CHIPS)
    second = next_layer(first)
    line = [along(out_grads, k, 0) for k in range(1, SIDE)]
    grads = [out_grads] + [along(out_grads, j, 1) for j in range(1, SIDE)]
    line, grads[1:] = lax.optimization_barrier((line, grads[1:]))
    line = join(line)
    lines = [line] + [along(line, j, 1) for j in range(1, SIDE)]
    first = turn(place, first)
    total = None
    for j in range(SIDE - 1):
        total = product(place, [first, grads[j], lines[j]], [(0, 1, j, True)], total)
    second, *lines = lax.optimization_barrier((second, *lines))
    operands = [first, turn(place, second)] + [block for pair in zip(grads, lines) for block in pair]
    parts = [(0, 2 * SIDE, SIDE - 1, True)] + [(1, 2 + 2 * j, j, False) for j in range(SIDE)]
    theirs = product(place, operands, parts, total, lambda core: 1 - core)
    received = lax.ppermute(theirs, "core", [(0, 1), (1, 0)])
    mine = product(place, operands, parts, total, lambda core: core)
    weight_grad, tiles = columns(mine, received)
    new_cols, col_root, tiles = rows(exchange(tiles, ROWS), col_moment.reshape(TILE), weight_grad, weight)
    new_rows, row_root, tiles = scalars(exchange(tiles, "z"), row_moment.reshape(2, LANES))
    out = update(exchange(tiles, ROWS), row_root, col_root, weight_grad, weight)
    return (out, new_rows.reshape(-1), new_cols.reshape(-1))


def solution(mesh):
    mesh = Mesh(mesh.devices.reshape(SIDE, SIDE, 2, LAYERS), ("y", "x", "core", "z"))
    placed = (P(ROWS, None), P(ROWS, "z"), P(ROWS, "z"), P(ROWS), P("z"))
    return jax.shard_map(
        shards,
        mesh=mesh,
        in_specs=placed,
        out_specs=(P(ROWS, "z"), P(ROWS), P("z")),
        check_vma=False,
    )
```

```python
import functools

import jax
import jax.numpy as jnp
from jax import lax
from jax.experimental import pallas as pl
from jax.experimental.pallas import tpu as pltpu
from jax.sharding import Mesh, PartitionSpec as P

D = 8192
FF = 16384


BETA_TWO = 0.8
CLIP_LEVEL = 0.25
WEIGHT_DECAY = 0.1
EPSILON = 1e-06

CHIPS = ("y", "x")
ROWS = ("y", "x", "core")
SIDE = 4
COUNT = SIDE * SIDE
LAYERS = 16
DEVICES = 2 * COUNT
TOKENS = 128
HALF = TOKENS // 2
ROW_BLOCK = 256
WIDTH = 1024
LANES = 128
COLUMNS = 256
TILE = (8, LANES)

ANYWHERE = pl.BlockSpec(memory_space=pl.ANY)
WHOLE = pl.BlockSpec(memory_space=pltpu.VMEM)
SCALARS = pl.BlockSpec(memory_space=pltpu.SMEM)
PARAMS = pltpu.CompilerParams(vmem_limit_bytes=12 * 2**20)


def shape(*dims, dtype=jnp.float32):
    return jax.ShapeDtypeStruct(dims, dtype)


def cost(flops, bytes_accessed):
    return pl.CostEstimate(flops=flops, bytes_accessed=bytes_accessed, transcendentals=0)


def device(y, x, core):
    return ((y % SIDE) * SIDE + x % SIDE) * 2 + core


def along(value, step, stage):
    pairs = []
    for y in range(SIDE):
        for x in range(SIDE):
            for core in range(2):
                on_x = core == stage
                to = device(y, x + step, core) if on_x else device(y + step, x, core)
                pairs.append((device(y, x, core), to))
    return lax.ppermute(value, ROWS, pairs)


def next_layer(value):
    pairs = [(i, (i + 1) % LAYERS) for i in range(LAYERS)]
    pairs += [(LAYERS + i, LAYERS + (i - 1) % LAYERS) for i in range(LAYERS)]
    return lax.ppermute(value, ("core", "z"), pairs)


def exchange(tiles, axes):
    return lax.all_to_all(tiles, axes, 0, 0)


def pack_kernel(place, source, out, sems):
    rows = pl.ds(pl.multiple_of(place[3] * HALF, HALF), HALF)
    copies = [
        pltpu.make_async_copy(source.at[rows, pl.ds(i * 2 * ROW_BLOCK, 2 * ROW_BLOCK)], out.at[i], sems.at[i])
        for i in range(COUNT)
    ]
    for copy in copies:
        copy.start()
    for copy in copies:
        copy.wait()


def pack(place, activations):
    return pl.pallas_call(
        pack_kernel,
        out_shape=shape(COUNT, HALF, 2 * ROW_BLOCK, dtype=jnp.bfloat16),
        in_specs=[SCALARS, ANYWHERE],
        out_specs=WHOLE,
        scratch_shapes=[pltpu.SemaphoreType.DMA((COUNT,))],
        compiler_params=PARAMS,
        cost_estimate=cost(0, 2**21),
    )(place, pltpu.with_memory_space_constraint(activations, pltpu.HBM))


def join_kernel(*refs):
    blocks, out, sems = refs[:-2], refs[-2], refs[-1]
    copies = [
        pltpu.make_async_copy(block, out.at[pl.ds(i * TOKENS, TOKENS)], sems.at[i]) for i, block in enumerate(blocks)
    ]
    for copy in copies:
        copy.start()
    for copy in copies:
        copy.wait()


def join(blocks):
    return pl.pallas_call(
        join_kernel,
        out_shape=shape(len(blocks) * TOKENS, WIDTH, dtype=jnp.bfloat16),
        in_specs=[ANYWHERE] * len(blocks),
        out_specs=ANYWHERE,
        scratch_shapes=[pltpu.SemaphoreType.DMA((len(blocks),))],
        compiler_params=PARAMS,
        cost_estimate=cost(0, 2**21),
    )(*blocks)


def turn_kernel(place, part, *outs):
    y, x, core = place[0], place[1], place[2]

    def block(i):
        j, k = i // SIDE, i % SIDE
        dx, dy = jnp.where(core == 0, k, j), jnp.where(core == 0, j, k)
        return part[((y - dy) & (SIDE - 1)) * SIDE + ((x - dx) & (SIDE - 1))]

    for i in range(0, COUNT, 2):
        first = i % (2 * SIDE) * HALF
        outs[i // (2 * SIDE)][:, first : first + 2 * HALF] = jnp.concatenate([block(i), block(i + 1)], axis=0).T


def turn(place, part):
    return pl.pallas_call(
        turn_kernel,
        out_shape=(shape(2 * ROW_BLOCK, 2 * SIDE * HALF, dtype=jnp.bfloat16),) * 2,
        in_specs=[SCALARS, WHOLE],
        out_specs=(WHOLE, WHOLE),
        compiler_params=PARAMS,
        cost_estimate=cost(0, 2**21),
    )(place, part)


def product_kernel(parts, which, place, *refs):
    operands, out = refs[:-1], refs[-1]
    total = None if len(operands) == 2 + max(part[1] for part in parts) else operands[-1]
    start = place[3] * HALF
    rows = pl.ds(0 if which is None else pl.multiple_of(which(place[2]) * ROW_BLOCK, ROW_BLOCK), out.shape[0])

    @pl.loop(0, WIDTH // COLUMNS)
    def _(n):
        columns = pl.ds(pl.multiple_of(n * COLUMNS, COLUMNS), COLUMNS)
        value = None if total is None else total[rows, columns]
        for turned, grads, group, exchanged in parts:
            offset = pl.multiple_of(start if exchanged else HALF - start, HALF)
            blocks = [operands[grads][pl.ds(offset, HALF), columns]]
            blocks += [operands[grads + 1][pl.ds(i * TOKENS + offset, HALF), columns] for i in range(SIDE - 1)]
            lanes = group % 2 * SIDE * HALF
            features = operands[turned][rows, lanes : lanes + SIDE * HALF]
            term = jnp.dot(features, jnp.concatenate(blocks, axis=0), preferred_element_type=jnp.float32)
            value = term if value is None else value + term
        out[:, columns] = value


def product(place, operands, parts, total=None, which=None):
    count = 2 * ROW_BLOCK if which is None else ROW_BLOCK
    operands = operands + ([] if total is None else [total])
    return pl.pallas_call(
        functools.partial(product_kernel, parts, which),
        out_shape=shape(count, WIDTH),
        in_specs=[SCALARS] + [WHOLE] * len(operands),
        out_specs=WHOLE,
        compiler_params=PARAMS,
        cost_estimate=cost(2 * count * SIDE * HALF * WIDTH * len(parts), 2**20),
    )(place, *operands)


def columns_kernel(mine, theirs, grad, sent):
    value = mine[...] + theirs[...]
    grad[...] = value
    sums = jnp.sum(value * value, axis=0, keepdims=True)
    tile = jnp.concatenate([sums[:, i * LANES : (i + 1) * LANES] for i in range(8)], axis=0)
    for i in range(DEVICES):
        sent[i] = tile


def columns(mine, theirs):
    return pl.pallas_call(
        columns_kernel,
        out_shape=(shape(ROW_BLOCK, WIDTH), shape(DEVICES, *TILE)),
        in_specs=[WHOLE] * 2,
        out_specs=(WHOLE, WHOLE),
        compiler_params=PARAMS,
        cost_estimate=cost(2**20, 3 * 2**20),
    )(mine, theirs)


def rows_kernel(received, moment, grad, weight, cols, col_root, sent):
    new = BETA_TWO * moment[...] + (1.0 - BETA_TWO) * (jnp.sum(received[...], axis=0) / D)
    cols[...] = new
    root = lax.rsqrt(new)
    col_root[...] = root
    sums = [jnp.zeros((ROW_BLOCK, LANES), jnp.float32)] * 4
    for i in range(WIDTH // LANES):
        lanes = slice(i * LANES, (i + 1) * LANES)
        value, held = grad[:, lanes], weight[:, lanes]
        by_cols = value * root[i : i + 1, :]
        terms = (value * value, by_cols * by_cols, by_cols * held, held * held)
        sums = [a + b for a, b in zip(sums, terms)]
    parts = []
    for value in sums:
        for row in range(0, ROW_BLOCK, LANES):
            parts.append(jnp.sum(value[row : row + LANES, :].T, axis=0, keepdims=True))
    tile = jnp.concatenate(parts, axis=0)
    for i in range(LAYERS):
        sent[i] = tile


def rows(received, moment, grad, weight):
    return pl.pallas_call(
        rows_kernel,
        out_shape=(shape(*TILE), shape(*TILE), shape(LAYERS, *TILE)),
        in_specs=[WHOLE] * 4,
        out_specs=(WHOLE, WHOLE, WHOLE),
        compiler_params=PARAMS,
        cost_estimate=cost(2**21, 2**21),
    )(received, moment, grad, weight)


def scalars_kernel(received, moment, rows_out, row_root, sent):
    parts = jnp.sum(received[...], axis=0)
    new = BETA_TWO * moment[...] + (1.0 - BETA_TWO) * (parts[0:2] / FF)
    rows_out[...] = new
    root = lax.rsqrt(new)
    row_root[...] = root
    sums = [jnp.sum(part, axis=0, keepdims=True) for part in (parts[2:4] * root * root, parts[4:6] * root, parts[6:8])]
    tile = jnp.concatenate(sums + [jnp.zeros_like(sums[0])], axis=0)
    for i in range(DEVICES):
        sent[i] = tile


def scalars(received, moment):
    return pl.pallas_call(
        scalars_kernel,
        out_shape=(shape(2, LANES), shape(2, LANES), shape(DEVICES, 4, LANES)),
        in_specs=[WHOLE] * 2,
        out_specs=(WHOLE, WHOLE, WHOLE),
        compiler_params=PARAMS,
        cost_estimate=cost(2**14, 2**18),
    )(received, moment)


def update_kernel(received, row_root, col_root, grad, weight, out, done, sems):
    parts = jnp.sum(received[...], axis=0)
    scaled_sum, cross_sum, weight_sum = (jnp.sum(parts[i : i + 1], keepdims=True) for i in range(3))
    factor = 1.0 / jnp.maximum(1.0, jnp.sqrt(scaled_sum / (D * FF)) / CLIP_LEVEL)
    direction_sum = (
        factor * factor * scaled_sum + 2.0 * WEIGHT_DECAY * factor * cross_sum + WEIGHT_DECAY * WEIGHT_DECAY * weight_sum
    )
    trust_ratio = jnp.sqrt(weight_sum / (jnp.maximum(direction_sum, 0.0) + EPSILON))
    by_row = row_root[...] * (trust_ratio * factor)
    by_col = col_root[...]
    decay = trust_ratio * WEIGHT_DECAY
    copies = []
    for half in range(2):
        here = slice(half * LANES, (half + 1) * LANES)
        scale = jnp.broadcast_to(by_row[half : half + 1, :], (LANES, LANES)).T
        for i in range(WIDTH // LANES):
            lanes = slice(i * LANES, (i + 1) * LANES)
            done[here, lanes] = grad[here, lanes] * by_col[i : i + 1, :] * scale + decay * weight[here, lanes]
        copies.append(pltpu.make_async_copy(done.at[here], out.at[here], sems.at[half]))
        copies[-1].start()
    for copy in copies:
        copy.wait()


def update(received, row_root, col_root, grad, weight):
    return pl.pallas_call(
        update_kernel,
        out_shape=shape(ROW_BLOCK, WIDTH),
        in_specs=[WHOLE] * 5,
        out_specs=ANYWHERE,
        scratch_shapes=[pltpu.VMEM((ROW_BLOCK, WIDTH), jnp.float32), pltpu.SemaphoreType.DMA((2,))],
        compiler_params=PARAMS,
        cost_estimate=cost(2**20, 3 * 2**20),
    )(received, row_root, col_root, grad, weight)


def shards(activations, out_grads, weight, row_moment, col_moment):
    y, x, core, layer = (lax.axis_index(name) for name in ("y", "x", "core", "z"))
    place = jnp.stack([y, x, core, layer & 1])
    packed = pack(place, activations)
    line = [along(out_grads, k, 0) for k in range(1, SIDE)]
    grads = [out_grads] + [along(out_grads, j, 1) for j in range(1, SIDE)]
    packed, line, grads[1] = lax.optimization_barrier((packed, line, grads[1]))
    line, grads[2:] = lax.optimization_barrier((line, grads[2:]))
    first = turn(place, exchange(packed, CHIPS))
    second = [next_layer(part) for part in first]
    line = join(line)
    lines = [line] + [along(line, j, 1) for j in range(1, SIDE)]
    total = None
    for j in range(SIDE - 1):
        total = product(place, [first[j // 2], grads[j], lines[j]], [(0, 1, j, True)], total)
    operands = [first[1]] + second + [block for pair in zip(grads, lines) for block in pair]
    parts = [(0, 1 + 2 * SIDE, SIDE - 1, True)] + [(1 + j // 2, 3 + 2 * j, j, False) for j in range(SIDE)]
    theirs = product(place, operands, parts, total, lambda core: 1 - core)
    received = lax.ppermute(theirs, "core", [(0, 1), (1, 0)])
    mine = product(place, operands, parts, total, lambda core: core)
    weight_grad, tiles = columns(mine, received)
    new_cols, col_root, tiles = rows(exchange(tiles, ROWS), col_moment.reshape(TILE), weight_grad, weight)
    new_rows, row_root, tiles = scalars(exchange(tiles, "z"), row_moment.reshape(2, LANES))
    out = update(exchange(tiles, ROWS), row_root, col_root, weight_grad, weight)
    return (out, new_rows.reshape(-1), new_cols.reshape(-1))


def solution(mesh):
    mesh = Mesh(mesh.devices.reshape(SIDE, SIDE, 2, LAYERS), ("y", "x", "core", "z"))
    placed = (P(ROWS, None), P(ROWS, "z"), P(ROWS, "z"), P(ROWS), P("z"))
    return jax.shard_map(
        shards,
        mesh=mesh,
        in_specs=placed,
        out_specs=(P(ROWS, "z"), P(ROWS), P("z")),
        check_vma=False,
    )
```

```python
import functools

import jax
import jax.numpy as jnp
from jax import lax
from jax.experimental import pallas as pl
from jax.experimental.pallas import tpu as pltpu
from jax.sharding import Mesh, PartitionSpec as P

D = 8192
FF = 16384


BETA_TWO = 0.8
CLIP_LEVEL = 0.25
WEIGHT_DECAY = 0.1
EPSILON = 1e-06

CHIPS = ("y", "x")
ROWS = ("y", "x", "core")
SIDE = 4
COUNT = SIDE * SIDE
LAYERS = 16
DEVICES = 2 * COUNT
TOKENS = 128
HALF = TOKENS // 2
ROW_BLOCK = 256
WIDTH = 1024
LANES = 128
COLUMNS = 256
TILE = (8, LANES)

ANYWHERE = pl.BlockSpec(memory_space=pl.ANY)
WHOLE = pl.BlockSpec(memory_space=pltpu.VMEM)
SCALARS = pl.BlockSpec(memory_space=pltpu.SMEM)
PARAMS = pltpu.CompilerParams(vmem_limit_bytes=16 * 2**20)


def shape(*dims, dtype=jnp.float32):
    return jax.ShapeDtypeStruct(dims, dtype)


def cost(flops, bytes_accessed):
    return pl.CostEstimate(flops=flops, bytes_accessed=bytes_accessed, transcendentals=0)


def device(y, x, core):
    return ((y % SIDE) * SIDE + x % SIDE) * 2 + core


def along(value, step, stage):
    pairs = []
    for y in range(SIDE):
        for x in range(SIDE):
            for core in range(2):
                on_x = core == stage
                to = device(y, x + step, core) if on_x else device(y + step, x, core)
                pairs.append((device(y, x, core), to))
    return lax.ppermute(value, ROWS, pairs)


def next_layer(value):
    pairs = [(i, (i + 1) % LAYERS) for i in range(LAYERS)]
    pairs += [(LAYERS + i, LAYERS + (i - 1) % LAYERS) for i in range(LAYERS)]
    return lax.ppermute(value, ("core", "z"), pairs)


def exchange(tiles, axes):
    return lax.all_to_all(tiles, axes, 0, 0)


def pack_kernel(place, source, out, sems):
    rows = pl.ds(pl.multiple_of(place[3] * HALF, HALF), HALF)
    copies = [
        pltpu.make_async_copy(source.at[rows, pl.ds(i * 2 * ROW_BLOCK, 2 * ROW_BLOCK)], out.at[i], sems.at[i])
        for i in range(COUNT)
    ]
    for copy in copies:
        copy.start()
    for copy in copies:
        copy.wait()


def pack(place, activations):
    return pl.pallas_call(
        pack_kernel,
        out_shape=shape(COUNT, HALF, 2 * ROW_BLOCK, dtype=jnp.bfloat16),
        in_specs=[SCALARS, ANYWHERE],
        out_specs=WHOLE,
        scratch_shapes=[pltpu.SemaphoreType.DMA((COUNT,))],
        compiler_params=PARAMS,
        cost_estimate=cost(0, 2**21),
    )(place, pltpu.with_memory_space_constraint(activations, pltpu.HBM))


def join_kernel(*refs):
    blocks, out, sems = refs[:-2], refs[-2], refs[-1]
    copies = [
        pltpu.make_async_copy(block, out.at[pl.ds(i * TOKENS, TOKENS)], sems.at[i]) for i, block in enumerate(blocks)
    ]
    for copy in copies:
        copy.start()
    for copy in copies:
        copy.wait()


def join(blocks):
    return pl.pallas_call(
        join_kernel,
        out_shape=shape(len(blocks) * TOKENS, WIDTH, dtype=jnp.bfloat16),
        in_specs=[ANYWHERE] * len(blocks),
        out_specs=ANYWHERE,
        scratch_shapes=[pltpu.SemaphoreType.DMA((len(blocks),))],
        compiler_params=PARAMS,
        cost_estimate=cost(0, 2**21),
    )(*blocks)


def turn_kernel(place, part, out):
    y, x, core = place[0], place[1], place[2]

    def block(i):
        j, k = i // SIDE, i % SIDE
        dx, dy = jnp.where(core == 0, k, j), jnp.where(core == 0, j, k)
        return part[((y - dy) & (SIDE - 1)) * SIDE + ((x - dx) & (SIDE - 1))]

    for i in range(0, COUNT, 2):
        out[:, i * HALF : (i + 2) * HALF] = jnp.concatenate([block(i), block(i + 1)], axis=0).T


def turn(place, part):
    return pl.pallas_call(
        turn_kernel,
        out_shape=shape(2 * ROW_BLOCK, COUNT * HALF, dtype=jnp.bfloat16),
        in_specs=[SCALARS, WHOLE],
        out_specs=WHOLE,
        compiler_params=PARAMS,
        cost_estimate=cost(0, 2**21),
    )(place, part)


def product_kernel(parts, which, place, first, second, *refs):
    operands, out = refs[:-1], refs[-1]
    total = operands[-1] if len(operands) > 1 + max(index for *_, blocks in parts for index, _ in blocks) else None
    start = place[3] * HALF
    rows = pl.ds(0 if which is None else pl.multiple_of(which(place[2]) * ROW_BLOCK, ROW_BLOCK), out.shape[0])

    @pl.loop(0, WIDTH // COLUMNS)
    def _(n):
        columns = pl.ds(pl.multiple_of(n * COLUMNS, COLUMNS), COLUMNS)
        value = None if total is None else total[rows, columns]
        for group, exchanged, blocks in parts:
            depth = slice(group * SIDE * HALF, (group + 1) * SIDE * HALF)
            features, offset = (first, start) if exchanged else (second, HALF - start)
            offset = pl.multiple_of(offset, HALF)
            grads = [operands[index][pl.ds(i * TOKENS + offset, HALF), columns] for index, i in blocks]
            term = jnp.dot(features[rows, depth], jnp.concatenate(grads, axis=0), preferred_element_type=jnp.float32)
            value = term if value is None else value + term
        out[:, columns] = value


def product(place, features, operands, parts, total=None, which=None):
    count = 2 * ROW_BLOCK if which is None else ROW_BLOCK
    operands = [*features, *operands] + ([] if total is None else [total])
    return pl.pallas_call(
        functools.partial(product_kernel, parts, which),
        out_shape=shape(count, WIDTH),
        in_specs=[SCALARS] + [WHOLE] * len(operands),
        out_specs=WHOLE,
        compiler_params=PARAMS,
        cost_estimate=cost(2 * count * SIDE * HALF * WIDTH * len(parts), 2**20),
    )(place, *operands)


def columns_kernel(mine, theirs, grad, sent):
    value = mine[...] + theirs[...]
    grad[...] = value
    sums = jnp.sum(value * value, axis=0, keepdims=True)
    tile = jnp.concatenate([sums[:, i * LANES : (i + 1) * LANES] for i in range(8)], axis=0)
    for i in range(DEVICES):
        sent[i] = tile


def columns(mine, theirs):
    return pl.pallas_call(
        columns_kernel,
        out_shape=(shape(ROW_BLOCK, WIDTH), shape(DEVICES, *TILE)),
        in_specs=[WHOLE] * 2,
        out_specs=(WHOLE, WHOLE),
        compiler_params=PARAMS,
        cost_estimate=cost(2**20, 3 * 2**20),
    )(mine, theirs)


def rows_kernel(received, moment, grad, weight, cols, col_root, sent):
    new = BETA_TWO * moment[...] + (1.0 - BETA_TWO) * (jnp.sum(received[...], axis=0) / D)
    cols[...] = new
    root = lax.rsqrt(new)
    col_root[...] = root
    sums = [jnp.zeros((ROW_BLOCK, LANES), jnp.float32)] * 4
    for i in range(WIDTH // LANES):
        lanes = slice(i * LANES, (i + 1) * LANES)
        value, held = grad[:, lanes], weight[:, lanes]
        by_cols = value * root[i : i + 1, :]
        terms = (value * value, by_cols * by_cols, by_cols * held, held * held)
        sums = [a + b for a, b in zip(sums, terms)]
    parts = []
    for value in sums:
        for row in range(0, ROW_BLOCK, LANES):
            parts.append(jnp.sum(value[row : row + LANES, :].T, axis=0, keepdims=True))
    tile = jnp.concatenate(parts, axis=0)
    for i in range(LAYERS):
        sent[i] = tile


def rows(received, moment, grad, weight):
    return pl.pallas_call(
        rows_kernel,
        out_shape=(shape(*TILE), shape(*TILE), shape(LAYERS, *TILE)),
        in_specs=[WHOLE] * 4,
        out_specs=(WHOLE, WHOLE, WHOLE),
        compiler_params=PARAMS,
        cost_estimate=cost(2**21, 2**21),
    )(received, moment, grad, weight)


def scalars_kernel(received, moment, rows_out, row_root, sent):
    parts = jnp.sum(received[...], axis=0)
    new = BETA_TWO * moment[...] + (1.0 - BETA_TWO) * (parts[0:2] / FF)
    rows_out[...] = new
    root = lax.rsqrt(new)
    row_root[...] = root
    sums = [jnp.sum(part, axis=0, keepdims=True) for part in (parts[2:4] * root * root, parts[4:6] * root, parts[6:8])]
    tile = jnp.concatenate(sums + [jnp.zeros_like(sums[0])], axis=0)
    for i in range(DEVICES):
        sent[i] = tile


def scalars(received, moment):
    return pl.pallas_call(
        scalars_kernel,
        out_shape=(shape(2, LANES), shape(2, LANES), shape(DEVICES, 4, LANES)),
        in_specs=[WHOLE] * 2,
        out_specs=(WHOLE, WHOLE, WHOLE),
        compiler_params=PARAMS,
        cost_estimate=cost(2**14, 2**18),
    )(received, moment)


def update_kernel(received, row_root, col_root, grad, weight, out, done, sems):
    parts = jnp.sum(received[...], axis=0)
    scaled_sum, cross_sum, weight_sum = (jnp.sum(parts[i : i + 1], keepdims=True) for i in range(3))
    factor = 1.0 / jnp.maximum(1.0, jnp.sqrt(scaled_sum / (D * FF)) / CLIP_LEVEL)
    direction_sum = (
        factor * factor * scaled_sum + 2.0 * WEIGHT_DECAY * factor * cross_sum + WEIGHT_DECAY * WEIGHT_DECAY * weight_sum
    )
    trust_ratio = jnp.sqrt(weight_sum / (jnp.maximum(direction_sum, 0.0) + EPSILON))
    by_row = row_root[...] * (trust_ratio * factor)
    by_col = col_root[...]
    decay = trust_ratio * WEIGHT_DECAY
    copies = []
    for half in range(2):
        here = slice(half * LANES, (half + 1) * LANES)
        scale = jnp.broadcast_to(by_row[half : half + 1, :], (LANES, LANES)).T
        for i in range(WIDTH // LANES):
            lanes = slice(i * LANES, (i + 1) * LANES)
            done[here, lanes] = grad[here, lanes] * by_col[i : i + 1, :] * scale + decay * weight[here, lanes]
        copies.append(pltpu.make_async_copy(done.at[here], out.at[here], sems.at[half]))
        copies[-1].start()
    for copy in copies:
        copy.wait()


def update(received, row_root, col_root, grad, weight):
    return pl.pallas_call(
        update_kernel,
        out_shape=shape(ROW_BLOCK, WIDTH),
        in_specs=[WHOLE] * 5,
        out_specs=ANYWHERE,
        scratch_shapes=[pltpu.VMEM((ROW_BLOCK, WIDTH), jnp.float32), pltpu.SemaphoreType.DMA((2,))],
        compiler_params=PARAMS,
        cost_estimate=cost(2**20, 3 * 2**20),
    )(received, row_root, col_root, grad, weight)


def shards(activations, out_grads, weight, row_moment, col_moment):
    y, x, core, layer = (lax.axis_index(name) for name in ("y", "x", "core", "z"))
    place = jnp.stack([y, x, core, layer & 1])
    first = turn(place, exchange(pack(place, activations), CHIPS))
    second = next_layer(first)
    line = join([out_grads] + [along(out_grads, k, 0) for k in range(1, SIDE)])
    back, ahead = along(line, 1, 1), along(line, SIDE - 1, 1)
    middle = 2 * TOKENS
    far = [along(back[:middle], 1, 1), along(ahead[middle:], SIDE - 1, 1)]
    whole = lambda operand: [(operand, i) for i in range(SIDE)]
    total = None
    for group, lines in ((0, line), (1, back), (3, ahead)):
        total = product(place, (first, first), [lines], [(group, True, whole(0))], total)
    operands = [line, back, ahead] + far
    parts = [(2, True, [(3, 0), (3, 1), (4, 0), (4, 1)]), (2, False, [(3, 0), (3, 1), (4, 0), (4, 1)])]
    parts += [(group, False, whole(i)) for i, group in enumerate((0, 1, 3))]
    theirs = product(place, (first, second), operands, parts, total, lambda core: 1 - core)
    received = lax.ppermute(theirs, "core", [(0, 1), (1, 0)])
    mine = product(place, (first, second), operands, parts, total, lambda core: core)
    weight_grad, tiles = columns(mine, received)
    new_cols, col_root, tiles = rows(exchange(tiles, ROWS), col_moment.reshape(TILE), weight_grad, weight)
    new_rows, row_root, tiles = scalars(exchange(tiles, "z"), row_moment.reshape(2, LANES))
    out = update(exchange(tiles, ROWS), row_root, col_root, weight_grad, weight)
    return (out, new_rows.reshape(-1), new_cols.reshape(-1))


def solution(mesh):
    mesh = Mesh(mesh.devices.reshape(SIDE, SIDE, 2, LAYERS), ("y", "x", "core", "z"))
    placed = (P(ROWS, None), P(ROWS, "z"), P(ROWS, "z"), P(ROWS), P("z"))
    return jax.shard_map(
        shards,
        mesh=mesh,
        in_specs=placed,
        out_specs=(P(ROWS, "z"), P(ROWS), P("z")),
        check_vma=False,
    )
```

```python
import functools

import jax
import jax.numpy as jnp
from jax import lax
from jax.experimental import pallas as pl
from jax.experimental.pallas import tpu as pltpu
from jax.sharding import Mesh, PartitionSpec as P

D = 8192
FF = 16384


BETA_TWO = 0.8
CLIP_LEVEL = 0.25
WEIGHT_DECAY = 0.1
EPSILON = 1e-06

CHIPS = ("y", "x")
ROWS = ("y", "x", "core")
SIDE = 4
COUNT = SIDE * SIDE
LAYERS = 16
DEVICES = 2 * COUNT
TOKENS = 128
HALF = TOKENS // 2
ROW_BLOCK = 256
WIDTH = 1024
LANES = 128
COLUMNS = 256
TILE = (8, LANES)

ANYWHERE = pl.BlockSpec(memory_space=pl.ANY)
WHOLE = pl.BlockSpec(memory_space=pltpu.VMEM)
SCALARS = pl.BlockSpec(memory_space=pltpu.SMEM)
PARAMS = pltpu.CompilerParams(vmem_limit_bytes=16 * 2**20)


def shape(*dims, dtype=jnp.float32):
    return jax.ShapeDtypeStruct(dims, dtype)


def cost(flops, bytes_accessed):
    return pl.CostEstimate(flops=flops, bytes_accessed=bytes_accessed, transcendentals=0)


def device(y, x, core):
    return ((y % SIDE) * SIDE + x % SIDE) * 2 + core


def along(value, step, stage):
    pairs = []
    for y in range(SIDE):
        for x in range(SIDE):
            for core in range(2):
                on_x = core == stage
                to = device(y, x + step, core) if on_x else device(y + step, x, core)
                pairs.append((device(y, x, core), to))
    return lax.ppermute(value, ROWS, pairs)


def next_layer(value):
    pairs = [(i, (i + 1) % LAYERS) for i in range(LAYERS)]
    pairs += [(LAYERS + i, LAYERS + (i - 1) % LAYERS) for i in range(LAYERS)]
    return lax.ppermute(value, ("core", "z"), pairs)


def exchange(tiles, axes):
    return lax.all_to_all(tiles, axes, 0, 0)


def pack_kernel(place, source, out, sems):
    rows = pl.ds(pl.multiple_of(place[3] * HALF, HALF), HALF)
    copies = [
        pltpu.make_async_copy(source.at[rows, pl.ds(i * 2 * ROW_BLOCK, 2 * ROW_BLOCK)], out.at[i], sems.at[i])
        for i in range(COUNT)
    ]
    for copy in copies:
        copy.start()
    for copy in copies:
        copy.wait()


def pack(place, activations):
    return pl.pallas_call(
        pack_kernel,
        out_shape=shape(COUNT, HALF, 2 * ROW_BLOCK, dtype=jnp.bfloat16),
        in_specs=[SCALARS, ANYWHERE],
        out_specs=WHOLE,
        scratch_shapes=[pltpu.SemaphoreType.DMA((COUNT,))],
        compiler_params=PARAMS,
        cost_estimate=cost(0, 2**21),
    )(place, pltpu.with_memory_space_constraint(activations, pltpu.HBM))


def join_kernel(*refs):
    blocks, out, sems = refs[:-2], refs[-2], refs[-1]
    copies = [
        pltpu.make_async_copy(block, out.at[pl.ds(i * TOKENS, TOKENS)], sems.at[i]) for i, block in enumerate(blocks)
    ]
    for copy in copies:
        copy.start()
    for copy in copies:
        copy.wait()


def join(blocks):
    return pl.pallas_call(
        join_kernel,
        out_shape=shape(len(blocks) * TOKENS, WIDTH, dtype=jnp.bfloat16),
        in_specs=[ANYWHERE] * len(blocks),
        out_specs=ANYWHERE,
        scratch_shapes=[pltpu.SemaphoreType.DMA((len(blocks),))],
        compiler_params=PARAMS,
        cost_estimate=cost(0, 2**21),
    )(*blocks)


def turn_kernel(place, part, out):
    y, x, core = place[0], place[1], place[2]

    def block(i):
        j, k = i // SIDE, i % SIDE
        dx, dy = jnp.where(core == 0, k, j), jnp.where(core == 0, j, k)
        return part[((y - dy) & (SIDE - 1)) * SIDE + ((x - dx) & (SIDE - 1))]

    for i in range(0, COUNT, 2):
        out[:, i * HALF : (i + 2) * HALF] = jnp.concatenate([block(i), block(i + 1)], axis=0).T


def turn(place, part):
    return pl.pallas_call(
        turn_kernel,
        out_shape=shape(2 * ROW_BLOCK, COUNT * HALF, dtype=jnp.bfloat16),
        in_specs=[SCALARS, WHOLE],
        out_specs=WHOLE,
        compiler_params=PARAMS,
        cost_estimate=cost(0, 2**21),
    )(place, part)


def product_kernel(parts, which, place, first, second, *refs):
    operands, out = refs[:-1], refs[-1]
    total = operands[-1] if len(operands) > 1 + max(index for *_, blocks in parts for index, _ in blocks) else None
    start = place[3] * HALF
    rows = pl.ds(0 if which is None else pl.multiple_of(which(place[2]) * ROW_BLOCK, ROW_BLOCK), out.shape[0])

    @pl.loop(0, WIDTH // COLUMNS)
    def _(n):
        columns = pl.ds(pl.multiple_of(n * COLUMNS, COLUMNS), COLUMNS)
        value = None if total is None else total[rows, columns]
        for group, exchanged, blocks in parts:
            depth = slice(group * SIDE * HALF, (group + 1) * SIDE * HALF)
            features, offset = (first, start) if exchanged else (second, HALF - start)
            offset = pl.multiple_of(offset, HALF)
            grads = [operands[index][pl.ds(i * TOKENS + offset, HALF), columns] for index, i in blocks]
            term = jnp.dot(features[rows, depth], jnp.concatenate(grads, axis=0), preferred_element_type=jnp.float32)
            value = term if value is None else value + term
        out[:, columns] = value


def product(place, features, operands, parts, total=None, which=None):
    count = 2 * ROW_BLOCK if which is None else ROW_BLOCK
    operands = [*features, *operands] + ([] if total is None else [total])
    return pl.pallas_call(
        functools.partial(product_kernel, parts, which),
        out_shape=shape(count, WIDTH),
        in_specs=[SCALARS] + [WHOLE] * len(operands),
        out_specs=WHOLE,
        compiler_params=PARAMS,
        cost_estimate=cost(2 * count * SIDE * HALF * WIDTH * len(parts), 2**20),
    )(place, *operands)


def columns_kernel(mine, theirs, grad, sent):
    value = mine[...] + theirs[...]
    grad[...] = value
    sums = jnp.sum(value * value, axis=0, keepdims=True)
    tile = jnp.concatenate([sums[:, i * LANES : (i + 1) * LANES] for i in range(8)], axis=0)
    for i in range(DEVICES):
        sent[i] = tile


def columns(mine, theirs):
    return pl.pallas_call(
        columns_kernel,
        out_shape=(shape(ROW_BLOCK, WIDTH), shape(DEVICES, *TILE)),
        in_specs=[WHOLE] * 2,
        out_specs=(WHOLE, WHOLE),
        compiler_params=PARAMS,
        cost_estimate=cost(2**20, 3 * 2**20),
    )(mine, theirs)


def rows_kernel(received, moment, grad, weight, cols, col_root, sent):
    new = BETA_TWO * moment[...] + (1.0 - BETA_TWO) * (jnp.sum(received[...], axis=0) / D)
    cols[...] = new
    root = lax.rsqrt(new)
    col_root[...] = root
    sums = [jnp.zeros((ROW_BLOCK, LANES), jnp.float32)] * 4
    for i in range(WIDTH // LANES):
        lanes = slice(i * LANES, (i + 1) * LANES)
        value, held = grad[:, lanes], weight[:, lanes]
        by_cols = value * root[i : i + 1, :]
        terms = (value * value, by_cols * by_cols, by_cols * held, held * held)
        sums = [a + b for a, b in zip(sums, terms)]
    parts = []
    for value in sums:
        for row in range(0, ROW_BLOCK, LANES):
            parts.append(jnp.sum(value[row : row + LANES, :].T, axis=0, keepdims=True))
    tile = jnp.concatenate(parts, axis=0)
    for i in range(LAYERS):
        sent[i] = tile


def rows(received, moment, grad, weight):
    return pl.pallas_call(
        rows_kernel,
        out_shape=(shape(*TILE), shape(*TILE), shape(LAYERS, *TILE)),
        in_specs=[WHOLE] * 4,
        out_specs=(WHOLE, WHOLE, WHOLE),
        compiler_params=PARAMS,
        cost_estimate=cost(2**21, 2**21),
    )(received, moment, grad, weight)


def scalars_kernel(received, moment, rows_out, row_root, sent):
    parts = jnp.sum(received[...], axis=0)
    new = BETA_TWO * moment[...] + (1.0 - BETA_TWO) * (parts[0:2] / FF)
    rows_out[...] = new
    root = lax.rsqrt(new)
    row_root[...] = root
    sums = [jnp.sum(part, axis=0, keepdims=True) for part in (parts[2:4] * root * root, parts[4:6] * root, parts[6:8])]
    tile = jnp.concatenate(sums + [jnp.zeros_like(sums[0])], axis=0)
    for i in range(DEVICES):
        sent[i] = tile


def scalars(received, moment):
    return pl.pallas_call(
        scalars_kernel,
        out_shape=(shape(2, LANES), shape(2, LANES), shape(DEVICES, 4, LANES)),
        in_specs=[WHOLE] * 2,
        out_specs=(WHOLE, WHOLE, WHOLE),
        compiler_params=PARAMS,
        cost_estimate=cost(2**14, 2**18),
    )(received, moment)


def update_kernel(received, row_root, col_root, grad, weight, out, done, sems):
    parts = jnp.sum(received[...], axis=0)
    scaled_sum, cross_sum, weight_sum = (jnp.sum(parts[i : i + 1], keepdims=True) for i in range(3))
    factor = 1.0 / jnp.maximum(1.0, jnp.sqrt(scaled_sum / (D * FF)) / CLIP_LEVEL)
    direction_sum = (
        factor * factor * scaled_sum + 2.0 * WEIGHT_DECAY * factor * cross_sum + WEIGHT_DECAY * WEIGHT_DECAY * weight_sum
    )
    trust_ratio = jnp.sqrt(weight_sum / (jnp.maximum(direction_sum, 0.0) + EPSILON))
    by_row = row_root[...] * (trust_ratio * factor)
    by_col = col_root[...]
    decay = trust_ratio * WEIGHT_DECAY
    copies = []
    for half in range(2):
        here = slice(half * LANES, (half + 1) * LANES)
        scale = jnp.broadcast_to(by_row[half : half + 1, :], (LANES, LANES)).T
        for i in range(WIDTH // LANES):
            lanes = slice(i * LANES, (i + 1) * LANES)
            done[here, lanes] = grad[here, lanes] * by_col[i : i + 1, :] * scale + decay * weight[here, lanes]
        copies.append(pltpu.make_async_copy(done.at[here], out.at[here], sems.at[half]))
        copies[-1].start()
    for copy in copies:
        copy.wait()


def update(received, row_root, col_root, grad, weight):
    return pl.pallas_call(
        update_kernel,
        out_shape=shape(ROW_BLOCK, WIDTH),
        in_specs=[WHOLE] * 5,
        out_specs=ANYWHERE,
        scratch_shapes=[pltpu.VMEM((ROW_BLOCK, WIDTH), jnp.float32), pltpu.SemaphoreType.DMA((2,))],
        compiler_params=PARAMS,
        cost_estimate=cost(2**20, 3 * 2**20),
    )(received, row_root, col_root, grad, weight)


def shards(activations, out_grads, weight, row_moment, col_moment):
    y, x, core, layer = (lax.axis_index(name) for name in ("y", "x", "core", "z"))
    place = jnp.stack([y, x, core, layer & 1])
    first = turn(place, exchange(pack(place, activations), CHIPS))
    second = next_layer(first)
    line = [out_grads] + [along(out_grads, k, 0) for k in range(1, SIDE)]
    low, high = join(line[:2]), join(line[2:])
    back_low, ahead_high = along(low, 1, 1), along(high, SIDE - 1, 1)
    far = [along(back_low, 1, 1), along(ahead_high, SIDE - 1, 1)]
    back, ahead = [back_low, along(high, 1, 1)], [along(low, SIDE - 1, 1), ahead_high]
    blocks = lambda operand: [(operand, 0), (operand, 1), (operand + 1, 0), (operand + 1, 1)]
    total = None
    for group, halves in ((0, [low, high]), (1, back), (3, ahead)):
        total = product(place, (first, first), halves, [(group, True, blocks(0))], total)
    operands = [low, high] + back + ahead + far
    parts = [(2, True, blocks(6)), (2, False, blocks(6))]
    parts += [(group, False, blocks(2 * i)) for i, group in enumerate((0, 1, 3))]
    theirs = product(place, (first, second), operands, parts, total, lambda core: 1 - core)
    received = lax.ppermute(theirs, "core", [(0, 1), (1, 0)])
    mine = product(place, (first, second), operands, parts, total, lambda core: core)
    weight_grad, tiles = columns(mine, received)
    new_cols, col_root, tiles = rows(exchange(tiles, ROWS), col_moment.reshape(TILE), weight_grad, weight)
    new_rows, row_root, tiles = scalars(exchange(tiles, "z"), row_moment.reshape(2, LANES))
    out = update(exchange(tiles, ROWS), row_root, col_root, weight_grad, weight)
    return (out, new_rows.reshape(-1), new_cols.reshape(-1))


def solution(mesh):
    mesh = Mesh(mesh.devices.reshape(SIDE, SIDE, 2, LAYERS), ("y", "x", "core", "z"))
    placed = (P(ROWS, None), P(ROWS, "z"), P(ROWS, "z"), P(ROWS), P("z"))
    return jax.shard_map(
        shards,
        mesh=mesh,
        in_specs=placed,
        out_specs=(P(ROWS, "z"), P(ROWS), P("z")),
        check_vma=False,
    )
```

```python
import functools

import jax
import jax.numpy as jnp
from jax import lax
from jax.experimental import pallas as pl
from jax.experimental.pallas import tpu as pltpu
from jax.sharding import Mesh, PartitionSpec as P

D = 8192
FF = 16384


BETA_TWO = 0.8
CLIP_LEVEL = 0.25
WEIGHT_DECAY = 0.1
EPSILON = 1e-06

CHIPS = ("y", "x")
ROWS = ("y", "x", "core")
SIDE = 4
COUNT = SIDE * SIDE
LAYERS = 16
DEVICES = 2 * COUNT
TOKENS = 128
HALF = TOKENS // 2
ROW_BLOCK = 256
WIDTH = 1024
LANES = 128
COLUMNS = 256
TILE = (8, LANES)

ANYWHERE = pl.BlockSpec(memory_space=pl.ANY)
WHOLE = pl.BlockSpec(memory_space=pltpu.VMEM)
SCALARS = pl.BlockSpec(memory_space=pltpu.SMEM)
PARAMS = pltpu.CompilerParams(vmem_limit_bytes=16 * 2**20)


def shape(*dims, dtype=jnp.float32):
    return jax.ShapeDtypeStruct(dims, dtype)


def cost(flops, bytes_accessed):
    return pl.CostEstimate(flops=flops, bytes_accessed=bytes_accessed, transcendentals=0)


def device(y, x, core):
    return ((y % SIDE) * SIDE + x % SIDE) * 2 + core


def along(value, step, stage):
    pairs = []
    for y in range(SIDE):
        for x in range(SIDE):
            for core in range(2):
                on_x = core == stage
                to = device(y, x + step, core) if on_x else device(y + step, x, core)
                pairs.append((device(y, x, core), to))
    return lax.ppermute(value, ROWS, pairs)


def next_layer(value):
    pairs = [(i, (i + 1) % LAYERS) for i in range(LAYERS)]
    pairs += [(LAYERS + i, LAYERS + (i - 1) % LAYERS) for i in range(LAYERS)]
    return lax.ppermute(value, ("core", "z"), pairs)


def exchange(tiles, axes):
    return lax.all_to_all(tiles, axes, 0, 0)


def pack_kernel(place, source, out, sems):
    rows = pl.ds(pl.multiple_of(place[3] * HALF, HALF), HALF)
    copies = [
        pltpu.make_async_copy(source.at[rows, pl.ds(i * 2 * ROW_BLOCK, 2 * ROW_BLOCK)], out.at[i], sems.at[i])
        for i in range(COUNT)
    ]
    for copy in copies:
        copy.start()
    for copy in copies:
        copy.wait()


def pack(place, activations):
    return pl.pallas_call(
        pack_kernel,
        out_shape=shape(COUNT, HALF, 2 * ROW_BLOCK, dtype=jnp.bfloat16),
        in_specs=[SCALARS, ANYWHERE],
        out_specs=WHOLE,
        scratch_shapes=[pltpu.SemaphoreType.DMA((COUNT,))],
        compiler_params=PARAMS,
        cost_estimate=cost(0, 2**21),
    )(place, pltpu.with_memory_space_constraint(activations, pltpu.HBM))


def join_kernel(*refs):
    blocks, out, sems = refs[:-2], refs[-2], refs[-1]
    copies = [
        pltpu.make_async_copy(block, out.at[pl.ds(i * TOKENS, TOKENS)], sems.at[i]) for i, block in enumerate(blocks)
    ]
    for copy in copies:
        copy.start()
    for copy in copies:
        copy.wait()


def join(blocks):
    return pl.pallas_call(
        join_kernel,
        out_shape=shape(len(blocks) * TOKENS, WIDTH, dtype=jnp.bfloat16),
        in_specs=[ANYWHERE] * len(blocks),
        out_specs=ANYWHERE,
        scratch_shapes=[pltpu.SemaphoreType.DMA((len(blocks),))],
        compiler_params=PARAMS,
        cost_estimate=cost(0, 2**21),
    )(*blocks)


def turn_kernel(place, part, out):
    y, x, core = place[0], place[1], place[2]

    def block(i):
        j, k = i // SIDE, i % SIDE
        dx, dy = jnp.where(core == 0, k, j), jnp.where(core == 0, j, k)
        return part[((y - dy) & (SIDE - 1)) * SIDE + ((x - dx) & (SIDE - 1))]

    for i in range(0, COUNT, 2):
        out[:, i * HALF : (i + 2) * HALF] = jnp.concatenate([block(i), block(i + 1)], axis=0).T


def turn(place, part):
    return pl.pallas_call(
        turn_kernel,
        out_shape=shape(2 * ROW_BLOCK, COUNT * HALF, dtype=jnp.bfloat16),
        in_specs=[SCALARS, WHOLE],
        out_specs=WHOLE,
        compiler_params=PARAMS,
        cost_estimate=cost(0, 2**21),
    )(place, part)


def product_kernel(parts, which, place, first, second, *refs):
    operands, out = refs[:-1], refs[-1]
    total = operands[-1] if len(operands) > 1 + max(index for *_, blocks in parts for index, _ in blocks) else None
    start = place[3] * HALF
    rows = pl.ds(0 if which is None else pl.multiple_of(which(place[2]) * ROW_BLOCK, ROW_BLOCK), out.shape[0])

    @pl.loop(0, WIDTH // COLUMNS)
    def _(n):
        columns = pl.ds(pl.multiple_of(n * COLUMNS, COLUMNS), COLUMNS)
        value = None if total is None else total[rows, columns]
        for group, exchanged, blocks in parts:
            depth = slice(group * SIDE * HALF, (group + 1) * SIDE * HALF)
            features, offset = (first, start) if exchanged else (second, HALF - start)
            offset = pl.multiple_of(offset, HALF)
            grads = [operands[index][pl.ds(i * TOKENS + offset, HALF), columns] for index, i in blocks]
            term = jnp.dot(features[rows, depth], jnp.concatenate(grads, axis=0), preferred_element_type=jnp.float32)
            value = term if value is None else value + term
        out[:, columns] = value


def product(place, features, operands, parts, total=None, which=None):
    count = 2 * ROW_BLOCK if which is None else ROW_BLOCK
    operands = [*features, *operands] + ([] if total is None else [total])
    return pl.pallas_call(
        functools.partial(product_kernel, parts, which),
        out_shape=shape(count, WIDTH),
        in_specs=[SCALARS] + [WHOLE] * len(operands),
        out_specs=WHOLE,
        compiler_params=PARAMS,
        cost_estimate=cost(2 * count * SIDE * HALF * WIDTH * len(parts), 2**20),
    )(place, *operands)


def columns_kernel(mine, theirs, grad, sent):
    value = mine[...] + theirs[...]
    grad[...] = value
    sums = jnp.sum(value * value, axis=0, keepdims=True)
    tile = jnp.concatenate([sums[:, i * LANES : (i + 1) * LANES] for i in range(8)], axis=0)
    for i in range(DEVICES):
        sent[i] = tile


def columns(mine, theirs):
    return pl.pallas_call(
        columns_kernel,
        out_shape=(shape(ROW_BLOCK, WIDTH), shape(DEVICES, *TILE)),
        in_specs=[WHOLE] * 2,
        out_specs=(WHOLE, WHOLE),
        compiler_params=PARAMS,
        cost_estimate=cost(2**20, 3 * 2**20),
    )(mine, theirs)


def rows_kernel(received, moment, grad, weight, cols, col_root, sent):
    new = BETA_TWO * moment[...] + (1.0 - BETA_TWO) * (jnp.sum(received[...], axis=0) / D)
    cols[...] = new
    root = lax.rsqrt(new)
    col_root[...] = root
    sums = [jnp.zeros((ROW_BLOCK, LANES), jnp.float32)] * 4
    for i in range(WIDTH // LANES):
        lanes = slice(i * LANES, (i + 1) * LANES)
        value, held = grad[:, lanes], weight[:, lanes]
        by_cols = value * root[i : i + 1, :]
        terms = (value * value, by_cols * by_cols, by_cols * held, held * held)
        sums = [a + b for a, b in zip(sums, terms)]
    parts = []
    for value in sums:
        for row in range(0, ROW_BLOCK, LANES):
            parts.append(jnp.sum(value[row : row + LANES, :].T, axis=0, keepdims=True))
    tile = jnp.concatenate(parts, axis=0)
    for i in range(LAYERS):
        sent[i] = tile


def rows(received, moment, grad, weight):
    return pl.pallas_call(
        rows_kernel,
        out_shape=(shape(*TILE), shape(*TILE), shape(LAYERS, *TILE)),
        in_specs=[WHOLE] * 4,
        out_specs=(WHOLE, WHOLE, WHOLE),
        compiler_params=PARAMS,
        cost_estimate=cost(2**21, 2**21),
    )(received, moment, grad, weight)


def scalars_kernel(received, moment, rows_out, row_root, sent):
    parts = jnp.sum(received[...], axis=0)
    new = BETA_TWO * moment[...] + (1.0 - BETA_TWO) * (parts[0:2] / FF)
    rows_out[...] = new
    root = lax.rsqrt(new)
    row_root[...] = root
    sums = [jnp.sum(part, axis=0, keepdims=True) for part in (parts[2:4] * root * root, parts[4:6] * root, parts[6:8])]
    tile = jnp.concatenate(sums + [jnp.zeros_like(sums[0])], axis=0)
    for i in range(DEVICES):
        sent[i] = tile


def scalars(received, moment):
    return pl.pallas_call(
        scalars_kernel,
        out_shape=(shape(2, LANES), shape(2, LANES), shape(DEVICES, 4, LANES)),
        in_specs=[WHOLE] * 2,
        out_specs=(WHOLE, WHOLE, WHOLE),
        compiler_params=PARAMS,
        cost_estimate=cost(2**14, 2**18),
    )(received, moment)


def update_kernel(received, row_root, col_root, grad, weight, out, done, sems):
    parts = jnp.sum(received[...], axis=0)
    scaled_sum, cross_sum, weight_sum = (jnp.sum(parts[i : i + 1], keepdims=True) for i in range(3))
    factor = 1.0 / jnp.maximum(1.0, jnp.sqrt(scaled_sum / (D * FF)) / CLIP_LEVEL)
    direction_sum = (
        factor * factor * scaled_sum + 2.0 * WEIGHT_DECAY * factor * cross_sum + WEIGHT_DECAY * WEIGHT_DECAY * weight_sum
    )
    trust_ratio = jnp.sqrt(weight_sum / (jnp.maximum(direction_sum, 0.0) + EPSILON))
    by_row = row_root[...] * (trust_ratio * factor)
    by_col = col_root[...]
    decay = trust_ratio * WEIGHT_DECAY
    copies = []
    for half in range(2):
        here = slice(half * LANES, (half + 1) * LANES)
        scale = jnp.broadcast_to(by_row[half : half + 1, :], (LANES, LANES)).T
        for i in range(WIDTH // LANES):
            lanes = slice(i * LANES, (i + 1) * LANES)
            done[here, lanes] = grad[here, lanes] * by_col[i : i + 1, :] * scale + decay * weight[here, lanes]
        copies.append(pltpu.make_async_copy(done.at[here], out.at[here], sems.at[half]))
        copies[-1].start()
    for copy in copies:
        copy.wait()


def update(received, row_root, col_root, grad, weight):
    return pl.pallas_call(
        update_kernel,
        out_shape=shape(ROW_BLOCK, WIDTH),
        in_specs=[WHOLE] * 5,
        out_specs=ANYWHERE,
        scratch_shapes=[pltpu.VMEM((ROW_BLOCK, WIDTH), jnp.float32), pltpu.SemaphoreType.DMA((2,))],
        compiler_params=PARAMS,
        cost_estimate=cost(2**20, 3 * 2**20),
    )(received, row_root, col_root, grad, weight)


def shards(activations, out_grads, weight, row_moment, col_moment):
    y, x, core, layer = (lax.axis_index(name) for name in ("y", "x", "core", "z"))
    place = jnp.stack([y, x, core, layer & 1])
    line = [out_grads] + [along(out_grads, k, 0) for k in range(1, SIDE)]
    packed = pack(place, activations)
    packed, *line[1:] = lax.optimization_barrier((packed, *line[1:]))
    first = turn(place, exchange(packed, CHIPS))
    second = next_layer(first)
    low, high = join(line[:2]), join(line[2:])
    back_low, ahead_high = along(low, 1, 1), along(high, SIDE - 1, 1)
    far = [along(back_low, 1, 1), along(ahead_high, SIDE - 1, 1)]
    back, ahead = [back_low, along(high, 1, 1)], [along(low, SIDE - 1, 1), ahead_high]
    blocks = lambda operand: [(operand, 0), (operand, 1), (operand + 1, 0), (operand + 1, 1)]
    total = None
    for group, halves in ((0, [low, high]), (1, back), (3, ahead)):
        total = product(place, (first, first), halves, [(group, True, blocks(0))], total)
    operands = [low, high] + back + ahead + far
    parts = [(2, True, blocks(6)), (2, False, blocks(6))]
    parts += [(group, False, blocks(2 * i)) for i, group in enumerate((0, 1, 3))]
    theirs = product(place, (first, second), operands, parts, total, lambda core: 1 - core)
    received = lax.ppermute(theirs, "core", [(0, 1), (1, 0)])
    mine = product(place, (first, second), operands, parts, total, lambda core: core)
    weight_grad, tiles = columns(mine, received)
    new_cols, col_root, tiles = rows(exchange(tiles, ROWS), col_moment.reshape(TILE), weight_grad, weight)
    new_rows, row_root, tiles = scalars(exchange(tiles, "z"), row_moment.reshape(2, LANES))
    out = update(exchange(tiles, ROWS), row_root, col_root, weight_grad, weight)
    return (out, new_rows.reshape(-1), new_cols.reshape(-1))


def solution(mesh):
    mesh = Mesh(mesh.devices.reshape(SIDE, SIDE, 2, LAYERS), ("y", "x", "core", "z"))
    placed = (P(ROWS, None), P(ROWS, "z"), P(ROWS, "z"), P(ROWS), P("z"))
    return jax.shard_map(
        shards,
        mesh=mesh,
        in_specs=placed,
        out_specs=(P(ROWS, "z"), P(ROWS), P("z")),
        check_vma=False,
    )
```

```python
import functools

import jax
import jax.numpy as jnp
from jax import lax
from jax.experimental import pallas as pl
from jax.experimental.pallas import tpu as pltpu
from jax.sharding import Mesh, PartitionSpec as P

D = 8192
FF = 16384


BETA_TWO = 0.8
CLIP_LEVEL = 0.25
WEIGHT_DECAY = 0.1
EPSILON = 1e-06

CHIPS = ("y", "x")
ROWS = ("y", "x", "core")
SIDE = 4
COUNT = SIDE * SIDE
LAYERS = 16
DEVICES = 2 * COUNT
TOKENS = 128
HALF = TOKENS // 2
ROW_BLOCK = 256
WIDTH = 1024
LANES = 128
COLUMNS = 256
TILE = (8, LANES)

ANYWHERE = pl.BlockSpec(memory_space=pl.ANY)
WHOLE = pl.BlockSpec(memory_space=pltpu.VMEM)
SCALARS = pl.BlockSpec(memory_space=pltpu.SMEM)
PARAMS = pltpu.CompilerParams(vmem_limit_bytes=16 * 2**20)


def shape(*dims, dtype=jnp.float32):
    return jax.ShapeDtypeStruct(dims, dtype)


def cost(flops, bytes_accessed):
    return pl.CostEstimate(flops=flops, bytes_accessed=bytes_accessed, transcendentals=0)


def device(y, x, core):
    return ((y % SIDE) * SIDE + x % SIDE) * 2 + core


def along(value, step, stage):
    pairs = []
    for y in range(SIDE):
        for x in range(SIDE):
            for core in range(2):
                on_x = core == stage
                to = device(y, x + step, core) if on_x else device(y + step, x, core)
                pairs.append((device(y, x, core), to))
    return lax.ppermute(value, ROWS, pairs)


def next_layer(value):
    pairs = [(i, (i + 1) % LAYERS) for i in range(LAYERS)]
    pairs += [(LAYERS + i, LAYERS + (i - 1) % LAYERS) for i in range(LAYERS)]
    return lax.ppermute(value, ("core", "z"), pairs)


def exchange(tiles, axes):
    return lax.all_to_all(tiles, axes, 0, 0)


def pack_kernel(place, source, out, sems):
    rows = pl.ds(pl.multiple_of(place[3] * HALF, HALF), HALF)
    copies = [
        pltpu.make_async_copy(source.at[rows, pl.ds(i * 2 * ROW_BLOCK, 2 * ROW_BLOCK)], out.at[i], sems.at[i])
        for i in range(COUNT)
    ]
    for copy in copies:
        copy.start()
    for copy in copies:
        copy.wait()


def pack(place, activations):
    return pl.pallas_call(
        pack_kernel,
        out_shape=pltpu.VMEM((COUNT, HALF, 2 * ROW_BLOCK), jnp.bfloat16),
        in_specs=[SCALARS, ANYWHERE],
        out_specs=WHOLE,
        scratch_shapes=[pltpu.SemaphoreType.DMA((COUNT,))],
        compiler_params=PARAMS,
        cost_estimate=cost(0, 2**21),
    )(place, pltpu.with_memory_space_constraint(activations, pltpu.HBM))


def join_kernel(*refs):
    blocks, out, sems = refs[:-2], refs[-2], refs[-1]
    copies = [
        pltpu.make_async_copy(block, out.at[pl.ds(i * TOKENS, TOKENS)], sems.at[i]) for i, block in enumerate(blocks)
    ]
    for copy in copies:
        copy.start()
    for copy in copies:
        copy.wait()


def join(blocks):
    return pl.pallas_call(
        join_kernel,
        out_shape=shape(len(blocks) * TOKENS, WIDTH, dtype=jnp.bfloat16),
        in_specs=[ANYWHERE] * len(blocks),
        out_specs=ANYWHERE,
        scratch_shapes=[pltpu.SemaphoreType.DMA((len(blocks),))],
        compiler_params=PARAMS,
        cost_estimate=cost(0, 2**21),
    )(*blocks)


def turn_kernel(place, part, out):
    y, x, core = place[0], place[1], place[2]

    def block(i):
        j, k = i // SIDE, i % SIDE
        dx, dy = jnp.where(core == 0, k, j), jnp.where(core == 0, j, k)
        return part[((y - dy) & (SIDE - 1)) * SIDE + ((x - dx) & (SIDE - 1))]

    for i in range(0, COUNT, 2):
        out[:, i * HALF : (i + 2) * HALF] = jnp.concatenate([block(i), block(i + 1)], axis=0).T


def turn(place, part):
    return pl.pallas_call(
        turn_kernel,
        out_shape=shape(2 * ROW_BLOCK, COUNT * HALF, dtype=jnp.bfloat16),
        in_specs=[SCALARS, WHOLE],
        out_specs=WHOLE,
        compiler_params=PARAMS,
        cost_estimate=cost(0, 2**21),
    )(place, part)


def product_kernel(parts, which, place, first, second, *refs):
    operands, out = refs[:-1], refs[-1]
    total = operands[-1] if len(operands) > 1 + max(index for *_, blocks in parts for index, _ in blocks) else None
    start = place[3] * HALF
    rows = pl.ds(0 if which is None else pl.multiple_of(which(place[2]) * ROW_BLOCK, ROW_BLOCK), out.shape[0])

    @pl.loop(0, WIDTH // COLUMNS)
    def _(n):
        columns = pl.ds(pl.multiple_of(n * COLUMNS, COLUMNS), COLUMNS)
        value = None if total is None else total[rows, columns]
        for group, exchanged, blocks in parts:
            depth = slice(group * SIDE * HALF, (group + 1) * SIDE * HALF)
            features, offset = (first, start) if exchanged else (second, HALF - start)
            offset = pl.multiple_of(offset, HALF)
            grads = [operands[index][pl.ds(i * TOKENS + offset, HALF), columns] for index, i in blocks]
            term = jnp.dot(features[rows, depth], jnp.concatenate(grads, axis=0), preferred_element_type=jnp.float32)
            value = term if value is None else value + term
        out[:, columns] = value


def product(place, features, operands, parts, total=None, which=None):
    count = 2 * ROW_BLOCK if which is None else ROW_BLOCK
    operands = [*features, *operands] + ([] if total is None else [total])
    return pl.pallas_call(
        functools.partial(product_kernel, parts, which),
        out_shape=shape(count, WIDTH),
        in_specs=[SCALARS] + [WHOLE] * len(operands),
        out_specs=WHOLE,
        compiler_params=PARAMS,
        cost_estimate=cost(20 * count * SIDE * HALF * WIDTH * len(parts), 2**20),
    )(place, *operands)


def columns_kernel(mine, theirs, grad, sent):
    value = mine[...] + theirs[...]
    grad[...] = value
    sums = jnp.sum(value * value, axis=0, keepdims=True)
    tile = jnp.concatenate([sums[:, i * LANES : (i + 1) * LANES] for i in range(8)], axis=0)
    for i in range(DEVICES):
        sent[i] = tile


def columns(mine, theirs):
    return pl.pallas_call(
        columns_kernel,
        out_shape=(shape(ROW_BLOCK, WIDTH), shape(DEVICES, *TILE)),
        in_specs=[WHOLE] * 2,
        out_specs=(WHOLE, WHOLE),
        compiler_params=PARAMS,
        cost_estimate=cost(2**20, 3 * 2**20),
    )(mine, theirs)


def rows_kernel(received, moment, grad, weight, cols, col_root, sent):
    new = BETA_TWO * moment[...] + (1.0 - BETA_TWO) * (jnp.sum(received[...], axis=0) / D)
    cols[...] = new
    root = lax.rsqrt(new)
    col_root[...] = root
    sums = [jnp.zeros((ROW_BLOCK, LANES), jnp.float32)] * 4
    for i in range(WIDTH // LANES):
        lanes = slice(i * LANES, (i + 1) * LANES)
        value, held = grad[:, lanes], weight[:, lanes]
        by_cols = value * root[i : i + 1, :]
        terms = (value * value, by_cols * by_cols, by_cols * held, held * held)
        sums = [a + b for a, b in zip(sums, terms)]
    parts = []
    for value in sums:
        for row in range(0, ROW_BLOCK, LANES):
            parts.append(jnp.sum(value[row : row + LANES, :].T, axis=0, keepdims=True))
    tile = jnp.concatenate(parts, axis=0)
    for i in range(LAYERS):
        sent[i] = tile


def rows(received, moment, grad, weight):
    return pl.pallas_call(
        rows_kernel,
        out_shape=(shape(*TILE), shape(*TILE), shape(LAYERS, *TILE)),
        in_specs=[WHOLE] * 4,
        out_specs=(WHOLE, WHOLE, WHOLE),
        compiler_params=PARAMS,
        cost_estimate=cost(2**21, 2**21),
    )(received, moment, grad, weight)


def scalars_kernel(received, moment, rows_out, row_root, sent):
    parts = jnp.sum(received[...], axis=0)
    new = BETA_TWO * moment[...] + (1.0 - BETA_TWO) * (parts[0:2] / FF)
    rows_out[...] = new
    root = lax.rsqrt(new)
    row_root[...] = root
    sums = [jnp.sum(part, axis=0, keepdims=True) for part in (parts[2:4] * root * root, parts[4:6] * root, parts[6:8])]
    tile = jnp.concatenate(sums + [jnp.zeros_like(sums[0])], axis=0)
    for i in range(DEVICES):
        sent[i] = tile


def scalars(received, moment):
    return pl.pallas_call(
        scalars_kernel,
        out_shape=(shape(2, LANES), shape(2, LANES), shape(DEVICES, 4, LANES)),
        in_specs=[WHOLE] * 2,
        out_specs=(WHOLE, WHOLE, WHOLE),
        compiler_params=PARAMS,
        cost_estimate=cost(2**14, 2**18),
    )(received, moment)


def update_kernel(received, row_root, col_root, grad, weight, out, done, sems):
    parts = jnp.sum(received[...], axis=0)
    scaled_sum, cross_sum, weight_sum = (jnp.sum(parts[i : i + 1], keepdims=True) for i in range(3))
    factor = 1.0 / jnp.maximum(1.0, jnp.sqrt(scaled_sum / (D * FF)) / CLIP_LEVEL)
    direction_sum = (
        factor * factor * scaled_sum + 2.0 * WEIGHT_DECAY * factor * cross_sum + WEIGHT_DECAY * WEIGHT_DECAY * weight_sum
    )
    trust_ratio = jnp.sqrt(weight_sum / (jnp.maximum(direction_sum, 0.0) + EPSILON))
    by_row = row_root[...] * (trust_ratio * factor)
    by_col = col_root[...]
    decay = trust_ratio * WEIGHT_DECAY
    copies = []
    for half in range(2):
        here = slice(half * LANES, (half + 1) * LANES)
        scale = jnp.broadcast_to(by_row[half : half + 1, :], (LANES, LANES)).T
        for i in range(WIDTH // LANES):
            lanes = slice(i * LANES, (i + 1) * LANES)
            done[here, lanes] = grad[here, lanes] * by_col[i : i + 1, :] * scale + decay * weight[here, lanes]
        copies.append(pltpu.make_async_copy(done.at[here], out.at[here], sems.at[half]))
        copies[-1].start()
    for copy in copies:
        copy.wait()


def update(received, row_root, col_root, grad, weight):
    return pl.pallas_call(
        update_kernel,
        out_shape=shape(ROW_BLOCK, WIDTH),
        in_specs=[WHOLE] * 5,
        out_specs=ANYWHERE,
        scratch_shapes=[pltpu.VMEM((ROW_BLOCK, WIDTH), jnp.float32), pltpu.SemaphoreType.DMA((2,))],
        compiler_params=PARAMS,
        cost_estimate=cost(2**20, 3 * 2**20),
    )(received, row_root, col_root, grad, weight)


def shards(activations, out_grads, weight, row_moment, col_moment):
    y, x, core, layer = (lax.axis_index(name) for name in ("y", "x", "core", "z"))
    place = jnp.stack([y, x, core, layer & 1])
    first = turn(place, exchange(pack(place, activations), CHIPS))
    second = next_layer(first)
    line = [out_grads] + [along(out_grads, k, 0) for k in range(1, SIDE)]
    low, high = join(line[:2]), join(line[2:])
    back_low, ahead_high = along(low, 1, 1), along(high, SIDE - 1, 1)
    far = [along(back_low, 1, 1), along(ahead_high, SIDE - 1, 1)]
    back, ahead = [back_low, along(high, 1, 1)], [along(low, SIDE - 1, 1), ahead_high]
    blocks = lambda operand: [(operand, 0), (operand, 1), (operand + 1, 0), (operand + 1, 1)]
    total = product(place, (first, first), [low, high], [(0, True, blocks(0))])
    total = product(place, (first, first), back + ahead, [(1, True, blocks(0)), (3, True, blocks(2))], total)
    parts = [(group, False, blocks(2 * i)) for i, group in enumerate((0, 1, 3))]
    total = product(place, (second, second), [low, high] + back + ahead, parts, total)
    parts = [(2, True, blocks(0)), (2, False, blocks(0))]
    theirs = product(place, (first, second), far, parts, total, lambda core: 1 - core)
    received = lax.ppermute(theirs, "core", [(0, 1), (1, 0)])
    mine = product(place, (first, second), far, parts, total, lambda core: core)
    weight_grad, tiles = columns(mine, received)
    new_cols, col_root, tiles = rows(exchange(tiles, ROWS), col_moment.reshape(TILE), weight_grad, weight)
    new_rows, row_root, tiles = scalars(exchange(tiles, "z"), row_moment.reshape(2, LANES))
    out = update(exchange(tiles, ROWS), row_root, col_root, weight_grad, weight)
    return (out, new_rows.reshape(-1), new_cols.reshape(-1))


def solution(mesh):
    mesh = Mesh(mesh.devices.reshape(SIDE, SIDE, 2, LAYERS), ("y", "x", "core", "z"))
    placed = (P(ROWS, None), P(ROWS, "z"), P(ROWS, "z"), P(ROWS), P("z"))
    return jax.shard_map(
        shards,
        mesh=mesh,
        in_specs=placed,
        out_specs=(P(ROWS, "z"), P(ROWS), P("z")),
        check_vma=False,
    )
```

```python
import functools

import jax
import jax.numpy as jnp
from jax import lax
from jax.experimental import pallas as pl
from jax.experimental.pallas import tpu as pltpu
from jax.sharding import Mesh, PartitionSpec as P

D = 8192
FF = 16384


BETA_TWO = 0.8
CLIP_LEVEL = 0.25
WEIGHT_DECAY = 0.1
EPSILON = 1e-06

CHIPS = ("y", "x")
ROWS = ("y", "x", "core")
SIDE = 4
COUNT = SIDE * SIDE
LAYERS = 16
DEVICES = 2 * COUNT
TOKENS = 128
HALF = TOKENS // 2
ROW_BLOCK = 256
WIDTH = 1024
LANES = 128
COLUMNS = 256
TILE = (8, LANES)

ANYWHERE = pl.BlockSpec(memory_space=pl.ANY)
WHOLE = pl.BlockSpec(memory_space=pltpu.VMEM)
SCALARS = pl.BlockSpec(memory_space=pltpu.SMEM)
PARAMS = pltpu.CompilerParams(vmem_limit_bytes=16 * 2**20)


def shape(*dims, dtype=jnp.float32):
    return jax.ShapeDtypeStruct(dims, dtype)


def cost(flops, bytes_accessed):
    return pl.CostEstimate(flops=flops, bytes_accessed=bytes_accessed, transcendentals=0)


def device(y, x, core):
    return ((y % SIDE) * SIDE + x % SIDE) * 2 + core


def along(value, step):
    pairs = []
    for y in range(SIDE):
        for x in range(SIDE):
            pairs.append((device(y, x, 0), device(y + step, x, 0)))
            pairs.append((device(y, x, 1), device(y, x + step, 1)))
    return lax.ppermute(value, ROWS, pairs)


def gather_line(value):
    groups = [[device(y, x, 0) for x in range(SIDE)] for y in range(SIDE)]
    groups += [[device(y, x, 1) for y in range(SIDE)] for x in range(SIDE)]
    sent = jnp.broadcast_to(value, (SIDE,) + value.shape)
    return lax.all_to_all(sent, ROWS, 0, 0, axis_index_groups=groups)


def next_layer(value):
    pairs = [(i, (i + 1) % LAYERS) for i in range(LAYERS)]
    pairs += [(LAYERS + i, LAYERS + (i - 1) % LAYERS) for i in range(LAYERS)]
    return lax.ppermute(value, ("core", "z"), pairs)


def exchange(tiles, axes):
    return lax.all_to_all(tiles, axes, 0, 0)


def pack_kernel(place, source, out, sems):
    rows = pl.ds(pl.multiple_of(place[3] * HALF, HALF), HALF)
    copies = [
        pltpu.make_async_copy(source.at[rows, pl.ds(i * 2 * ROW_BLOCK, 2 * ROW_BLOCK)], out.at[i], sems.at[i])
        for i in range(COUNT)
    ]
    for copy in copies:
        copy.start()
    for copy in copies:
        copy.wait()


def pack(place, activations):
    return pl.pallas_call(
        pack_kernel,
        out_shape=pltpu.VMEM((COUNT, HALF, 2 * ROW_BLOCK), jnp.bfloat16),
        in_specs=[SCALARS, ANYWHERE],
        out_specs=WHOLE,
        scratch_shapes=[pltpu.SemaphoreType.DMA((COUNT,))],
        compiler_params=PARAMS,
        cost_estimate=cost(0, 2**21),
    )(place, pltpu.with_memory_space_constraint(activations, pltpu.HBM))


def turn_kernel(place, part, out):
    y, x, core = place[0], place[1], place[2]

    def block(i):
        j, k = i // SIDE, i % SIDE
        return part[jnp.where(core == 0, ((y - j) & (SIDE - 1)) * SIDE + k, k * SIDE + ((x - j) & (SIDE - 1)))]

    for i in range(0, COUNT, 2):
        out[:, i * HALF : (i + 2) * HALF] = jnp.concatenate([block(i), block(i + 1)], axis=0).T


def turn(place, part):
    return pl.pallas_call(
        turn_kernel,
        out_shape=shape(2 * ROW_BLOCK, COUNT * HALF, dtype=jnp.bfloat16),
        in_specs=[SCALARS, WHOLE],
        out_specs=WHOLE,
        compiler_params=PARAMS,
        cost_estimate=cost(0, 2**21),
    )(place, part)


def product_kernel(parts, which, place, first, second, *refs):
    operands, out = refs[:-1], refs[-1]
    total = operands[-1] if len(operands) > 1 + max(index for *_, blocks in parts for index, _ in blocks) else None
    start = place[3] * HALF
    rows = pl.ds(0 if which is None else pl.multiple_of(which(place[2]) * ROW_BLOCK, ROW_BLOCK), out.shape[0])

    @pl.loop(0, WIDTH // COLUMNS)
    def _(n):
        columns = pl.ds(pl.multiple_of(n * COLUMNS, COLUMNS), COLUMNS)
        value = None if total is None else total[rows, columns]
        for group, exchanged, blocks in parts:
            depth = slice(group * SIDE * HALF, (group + 1) * SIDE * HALF)
            features, offset = (first, start) if exchanged else (second, HALF - start)
            offset = pl.multiple_of(offset, HALF)
            grads = [operands[index][pl.ds(i * TOKENS + offset, HALF), columns] for index, i in blocks]
            term = jnp.dot(features[rows, depth], jnp.concatenate(grads, axis=0), preferred_element_type=jnp.float32)
            value = term if value is None else value + term
        out[:, columns] = value


def product(place, features, operands, parts, total=None, which=None):
    count = 2 * ROW_BLOCK if which is None else ROW_BLOCK
    operands = [*features, *operands] + ([] if total is None else [total])
    return pl.pallas_call(
        functools.partial(product_kernel, parts, which),
        out_shape=shape(count, WIDTH),
        in_specs=[SCALARS] + [WHOLE] * len(operands),
        out_specs=WHOLE,
        compiler_params=PARAMS,
        cost_estimate=cost(20 * count * SIDE * HALF * WIDTH * len(parts), 2**20),
    )(place, *operands)


def columns_kernel(mine, theirs, grad, sent):
    value = mine[...] + theirs[...]
    grad[...] = value
    sums = jnp.sum(value * value, axis=0, keepdims=True)
    tile = jnp.concatenate([sums[:, i * LANES : (i + 1) * LANES] for i in range(8)], axis=0)
    for i in range(DEVICES):
        sent[i] = tile


def columns(mine, theirs):
    return pl.pallas_call(
        columns_kernel,
        out_shape=(shape(ROW_BLOCK, WIDTH), shape(DEVICES, *TILE)),
        in_specs=[WHOLE] * 2,
        out_specs=(WHOLE, WHOLE),
        compiler_params=PARAMS,
        cost_estimate=cost(2**20, 3 * 2**20),
    )(mine, theirs)


def rows_kernel(received, moment, grad, weight, cols, col_root, sent):
    new = BETA_TWO * moment[...] + (1.0 - BETA_TWO) * (jnp.sum(received[...], axis=0) / D)
    cols[...] = new
    root = lax.rsqrt(new)
    col_root[...] = root
    sums = [jnp.zeros((ROW_BLOCK, LANES), jnp.float32)] * 4
    for i in range(WIDTH // LANES):
        lanes = slice(i * LANES, (i + 1) * LANES)
        value, held = grad[:, lanes], weight[:, lanes]
        by_cols = value * root[i : i + 1, :]
        terms = (value * value, by_cols * by_cols, by_cols * held, held * held)
        sums = [a + b for a, b in zip(sums, terms)]
    parts = []
    for value in sums:
        for row in range(0, ROW_BLOCK, LANES):
            parts.append(jnp.sum(value[row : row + LANES, :].T, axis=0, keepdims=True))
    tile = jnp.concatenate(parts, axis=0)
    for i in range(LAYERS):
        sent[i] = tile


def rows(received, moment, grad, weight):
    return pl.pallas_call(
        rows_kernel,
        out_shape=(shape(*TILE), shape(*TILE), shape(LAYERS, *TILE)),
        in_specs=[WHOLE] * 4,
        out_specs=(WHOLE, WHOLE, WHOLE),
        compiler_params=PARAMS,
        cost_estimate=cost(2**21, 2**21),
    )(received, moment, grad, weight)


def scalars_kernel(received, moment, rows_out, row_root, sent):
    parts = jnp.sum(received[...], axis=0)
    new = BETA_TWO * moment[...] + (1.0 - BETA_TWO) * (parts[0:2] / FF)
    rows_out[...] = new
    root = lax.rsqrt(new)
    row_root[...] = root
    sums = [jnp.sum(part, axis=0, keepdims=True) for part in (parts[2:4] * root * root, parts[4:6] * root, parts[6:8])]
    tile = jnp.concatenate(sums + [jnp.zeros_like(sums[0])], axis=0)
    for i in range(DEVICES):
        sent[i] = tile


def scalars(received, moment):
    return pl.pallas_call(
        scalars_kernel,
        out_shape=(shape(2, LANES), shape(2, LANES), shape(DEVICES, 4, LANES)),
        in_specs=[WHOLE] * 2,
        out_specs=(WHOLE, WHOLE, WHOLE),
        compiler_params=PARAMS,
        cost_estimate=cost(2**14, 2**18),
    )(received, moment)


def update_kernel(received, row_root, col_root, grad, weight, out, done, sems):
    parts = jnp.sum(received[...], axis=0)
    scaled_sum, cross_sum, weight_sum = (jnp.sum(parts[i : i + 1], keepdims=True) for i in range(3))
    factor = 1.0 / jnp.maximum(1.0, jnp.sqrt(scaled_sum / (D * FF)) / CLIP_LEVEL)
    direction_sum = (
        factor * factor * scaled_sum + 2.0 * WEIGHT_DECAY * factor * cross_sum + WEIGHT_DECAY * WEIGHT_DECAY * weight_sum
    )
    trust_ratio = jnp.sqrt(weight_sum / (jnp.maximum(direction_sum, 0.0) + EPSILON))
    by_row = row_root[...] * (trust_ratio * factor)
    by_col = col_root[...]
    decay = trust_ratio * WEIGHT_DECAY
    copies = []
    for half in range(2):
        here = slice(half * LANES, (half + 1) * LANES)
        scale = jnp.broadcast_to(by_row[half : half + 1, :], (LANES, LANES)).T
        for i in range(WIDTH // LANES):
            lanes = slice(i * LANES, (i + 1) * LANES)
            done[here, lanes] = grad[here, lanes] * by_col[i : i + 1, :] * scale + decay * weight[here, lanes]
        copies.append(pltpu.make_async_copy(done.at[here], out.at[here], sems.at[half]))
        copies[-1].start()
    for copy in copies:
        copy.wait()


def update(received, row_root, col_root, grad, weight):
    return pl.pallas_call(
        update_kernel,
        out_shape=shape(ROW_BLOCK, WIDTH),
        in_specs=[WHOLE] * 5,
        out_specs=ANYWHERE,
        scratch_shapes=[pltpu.VMEM((ROW_BLOCK, WIDTH), jnp.float32), pltpu.SemaphoreType.DMA((2,))],
        compiler_params=PARAMS,
        cost_estimate=cost(2**20, 3 * 2**20),
    )(received, row_root, col_root, grad, weight)


def shards(activations, out_grads, weight, row_moment, col_moment):
    y, x, core, layer = (lax.axis_index(name) for name in ("y", "x", "core", "z"))
    place = jnp.stack([y, x, core, layer & 1])
    line = gather_line(out_grads)
    packed, line = lax.optimization_barrier((pack(place, activations), line))
    first = turn(place, exchange(packed, CHIPS))
    second = next_layer(first)
    low, high = (line[i : i + 2].reshape(2 * TOKENS, WIDTH) for i in (0, 2))
    back_low, ahead_high = along(low, 1), along(high, SIDE - 1)
    far = [along(back_low, 1), along(ahead_high, SIDE - 1)]
    back, ahead = [back_low, along(high, 1)], [along(low, SIDE - 1), ahead_high]
    blocks = lambda operand: [(operand, 0), (operand, 1), (operand + 1, 0), (operand + 1, 1)]
    total = product(place, (first, first), [low, high], [(0, True, blocks(0))])
    total = product(place, (first, first), back + ahead, [(1, True, blocks(0)), (3, True, blocks(2))], total)
    parts = [(group, False, blocks(2 * i)) for i, group in enumerate((0, 1, 3))]
    total = product(place, (second, second), [low, high] + back + ahead, parts, total)
    parts = [(2, True, blocks(0)), (2, False, blocks(0))]
    theirs = product(place, (first, second), far, parts, total, lambda core: 1 - core)
    received = lax.ppermute(theirs, "core", [(0, 1), (1, 0)])
    mine = product(place, (first, second), far, parts, total, lambda core: core)
    weight_grad, tiles = columns(mine, received)
    new_cols, col_root, tiles = rows(exchange(tiles, ROWS), col_moment.reshape(TILE), weight_grad, weight)
    new_rows, row_root, tiles = scalars(exchange(tiles, "z"), row_moment.reshape(2, LANES))
    out = update(exchange(tiles, ROWS), row_root, col_root, weight_grad, weight)
    return (out, new_rows.reshape(-1), new_cols.reshape(-1))


def solution(mesh):
    mesh = Mesh(mesh.devices.reshape(SIDE, SIDE, 2, LAYERS), ("y", "x", "core", "z"))
    placed = (P(ROWS, None), P(ROWS, "z"), P(ROWS, "z"), P(ROWS), P("z"))
    return jax.shard_map(
        shards,
        mesh=mesh,
        in_specs=placed,
        out_specs=(P(ROWS, "z"), P(ROWS), P("z")),
        check_vma=False,
    )
```

```python
import functools

import jax
import jax.numpy as jnp
from jax import lax
from jax.experimental import pallas as pl
from jax.experimental.pallas import tpu as pltpu
from jax.sharding import Mesh, PartitionSpec as P

D = 8192
FF = 16384


BETA_TWO = 0.8
CLIP_LEVEL = 0.25
WEIGHT_DECAY = 0.1
EPSILON = 1e-06

CHIPS = ("y", "x")
ROWS = ("y", "x", "core")
SIDE = 4
COUNT = SIDE * SIDE
LAYERS = 16
DEVICES = 2 * COUNT
TOKENS = 128
HALF = TOKENS // 2
ROW_BLOCK = 256
WIDTH = 1024
LANES = 128
COLUMNS = 256
TILE = (8, LANES)

ANYWHERE = pl.BlockSpec(memory_space=pl.ANY)
WHOLE = pl.BlockSpec(memory_space=pltpu.VMEM)
SCALARS = pl.BlockSpec(memory_space=pltpu.SMEM)
PARAMS = pltpu.CompilerParams(vmem_limit_bytes=16 * 2**20)


def shape(*dims, dtype=jnp.float32):
    return jax.ShapeDtypeStruct(dims, dtype)


def cost(flops, bytes_accessed):
    return pl.CostEstimate(flops=flops, bytes_accessed=bytes_accessed, transcendentals=0)


def device(y, x, core):
    return ((y % SIDE) * SIDE + x % SIDE) * 2 + core


def along(value, step):
    pairs = []
    for y in range(SIDE):
        for x in range(SIDE):
            pairs.append((device(y, x, 0), device(y + step, x, 0)))
            pairs.append((device(y, x, 1), device(y, x + step, 1)))
    return lax.ppermute(value, ROWS, pairs)


def gather_line(value):
    groups = [[device(y, x, 0) for x in range(SIDE)] for y in range(SIDE)]
    groups += [[device(y, x, 1) for y in range(SIDE)] for x in range(SIDE)]
    sent = jnp.broadcast_to(value, (SIDE,) + value.shape)
    return lax.all_to_all(sent, ROWS, 0, 0, axis_index_groups=groups)


def next_layer(value):
    pairs = [(i, (i + 1) % LAYERS) for i in range(LAYERS)]
    pairs += [(LAYERS + i, LAYERS + (i - 1) % LAYERS) for i in range(LAYERS)]
    return lax.ppermute(value, ("core", "z"), pairs)


def exchange(tiles, axes):
    return lax.all_to_all(tiles, axes, 0, 0)


def pack_kernel(place, source, out, sems):
    rows = pl.ds(pl.multiple_of(place[3] * HALF, HALF), HALF)
    copies = [
        pltpu.make_async_copy(source.at[rows, pl.ds(i * 2 * ROW_BLOCK, 2 * ROW_BLOCK)], out.at[i], sems.at[i])
        for i in range(COUNT)
    ]
    for copy in copies:
        copy.start()
    for copy in copies:
        copy.wait()


def pack(place, activations):
    return pl.pallas_call(
        pack_kernel,
        out_shape=pltpu.VMEM((COUNT, HALF, 2 * ROW_BLOCK), jnp.bfloat16),
        in_specs=[SCALARS, ANYWHERE],
        out_specs=WHOLE,
        scratch_shapes=[pltpu.SemaphoreType.DMA((COUNT,))],
        compiler_params=PARAMS,
        cost_estimate=cost(0, 2**21),
    )(place, pltpu.with_memory_space_constraint(activations, pltpu.HBM))


def turn_kernel(place, part, out):
    y, x, core = place[0], place[1], place[2]

    def block(i):
        j, k = i // SIDE, i % SIDE
        return part[jnp.where(core == 0, ((y - j) & (SIDE - 1)) * SIDE + k, k * SIDE + ((x - j) & (SIDE - 1)))]

    for i in range(0, COUNT, 2):
        out[:, i * HALF : (i + 2) * HALF] = jnp.concatenate([block(i), block(i + 1)], axis=0).T


def turn(place, part):
    return pl.pallas_call(
        turn_kernel,
        out_shape=shape(2 * ROW_BLOCK, COUNT * HALF, dtype=jnp.bfloat16),
        in_specs=[SCALARS, WHOLE],
        out_specs=WHOLE,
        compiler_params=PARAMS,
        cost_estimate=cost(0, 2**21),
    )(place, part)


def product_kernel(parts, which, place, first, second, *refs):
    operands, out = refs[:-1], refs[-1]
    total = operands[-1] if len(operands) > 1 + max(index for *_, blocks in parts for index, _ in blocks) else None
    start = place[3] * HALF
    rows = pl.ds(0 if which is None else pl.multiple_of(which(place[2]) * ROW_BLOCK, ROW_BLOCK), out.shape[0])

    @pl.loop(0, WIDTH // COLUMNS)
    def _(n):
        columns = pl.ds(pl.multiple_of(n * COLUMNS, COLUMNS), COLUMNS)
        value = None if total is None else total[rows, columns]
        for group, exchanged, blocks in parts:
            depth = slice(group * SIDE * HALF, (group + 1) * SIDE * HALF)
            features, offset = (first, start) if exchanged else (second, HALF - start)
            offset = pl.multiple_of(offset, HALF)
            grads = [operands[index][pl.ds(i * TOKENS + offset, HALF), columns] for index, i in blocks]
            term = jnp.dot(features[rows, depth], jnp.concatenate(grads, axis=0), preferred_element_type=jnp.float32)
            value = term if value is None else value + term
        out[:, columns] = value


def product(place, features, operands, parts, total=None, which=None):
    count = 2 * ROW_BLOCK if which is None else ROW_BLOCK
    operands = [*features, *operands] + ([] if total is None else [total])
    return pl.pallas_call(
        functools.partial(product_kernel, parts, which),
        out_shape=shape(count, WIDTH),
        in_specs=[SCALARS] + [WHOLE] * len(operands),
        out_specs=WHOLE,
        compiler_params=PARAMS,
        cost_estimate=cost(24 * count * SIDE * HALF * WIDTH * len(parts), 2**20),
    )(place, *operands)


def columns_kernel(mine, theirs, grad, sent):
    value = mine[...] + theirs[...]
    grad[...] = value
    sums = jnp.sum(value * value, axis=0, keepdims=True)
    tile = jnp.concatenate([sums[:, i * LANES : (i + 1) * LANES] for i in range(8)], axis=0)
    for i in range(DEVICES):
        sent[i] = tile


def columns(mine, theirs):
    return pl.pallas_call(
        columns_kernel,
        out_shape=(shape(ROW_BLOCK, WIDTH), shape(DEVICES, *TILE)),
        in_specs=[WHOLE] * 2,
        out_specs=(WHOLE, WHOLE),
        compiler_params=PARAMS,
        cost_estimate=cost(2**20, 3 * 2**20),
    )(mine, theirs)


def rows_kernel(received, moment, grad, weight, cols, col_root, sent):
    new = BETA_TWO * moment[...] + (1.0 - BETA_TWO) * (jnp.sum(received[...], axis=0) / D)
    cols[...] = new
    root = lax.rsqrt(new)
    col_root[...] = root
    sums = [jnp.zeros((ROW_BLOCK, LANES), jnp.float32)] * 4
    for i in range(WIDTH // LANES):
        lanes = slice(i * LANES, (i + 1) * LANES)
        value, held = grad[:, lanes], weight[:, lanes]
        by_cols = value * root[i : i + 1, :]
        terms = (value * value, by_cols * by_cols, by_cols * held, held * held)
        sums = [a + b for a, b in zip(sums, terms)]
    parts = []
    for value in sums:
        for row in range(0, ROW_BLOCK, LANES):
            parts.append(jnp.sum(value[row : row + LANES, :].T, axis=0, keepdims=True))
    tile = jnp.concatenate(parts, axis=0)
    for i in range(LAYERS):
        sent[i] = tile


def rows(received, moment, grad, weight):
    return pl.pallas_call(
        rows_kernel,
        out_shape=(shape(*TILE), shape(*TILE), shape(LAYERS, *TILE)),
        in_specs=[WHOLE] * 4,
        out_specs=(WHOLE, WHOLE, WHOLE),
        compiler_params=PARAMS,
        cost_estimate=cost(2**21, 2**21),
    )(received, moment, grad, weight)


def scalars_kernel(received, moment, rows_out, row_root, sent):
    parts = jnp.sum(received[...], axis=0)
    new = BETA_TWO * moment[...] + (1.0 - BETA_TWO) * (parts[0:2] / FF)
    rows_out[...] = new
    root = lax.rsqrt(new)
    row_root[...] = root
    sums = [jnp.sum(part, axis=0, keepdims=True) for part in (parts[2:4] * root * root, parts[4:6] * root, parts[6:8])]
    tile = jnp.concatenate(sums + [jnp.zeros_like(sums[0])], axis=0)
    for i in range(DEVICES):
        sent[i] = tile


def scalars(received, moment):
    return pl.pallas_call(
        scalars_kernel,
        out_shape=(shape(2, LANES), shape(2, LANES), shape(DEVICES, 4, LANES)),
        in_specs=[WHOLE] * 2,
        out_specs=(WHOLE, WHOLE, WHOLE),
        compiler_params=PARAMS,
        cost_estimate=cost(2**14, 2**18),
    )(received, moment)


def update_kernel(received, row_root, col_root, grad, weight, out, done, sems):
    parts = jnp.sum(received[...], axis=0)
    scaled_sum, cross_sum, weight_sum = (jnp.sum(parts[i : i + 1], keepdims=True) for i in range(3))
    factor = 1.0 / jnp.maximum(1.0, jnp.sqrt(scaled_sum / (D * FF)) / CLIP_LEVEL)
    direction_sum = (
        factor * factor * scaled_sum + 2.0 * WEIGHT_DECAY * factor * cross_sum + WEIGHT_DECAY * WEIGHT_DECAY * weight_sum
    )
    trust_ratio = jnp.sqrt(weight_sum / (jnp.maximum(direction_sum, 0.0) + EPSILON))
    by_row = row_root[...] * (trust_ratio * factor)
    by_col = col_root[...]
    decay = trust_ratio * WEIGHT_DECAY
    copies = []
    for half in range(2):
        here = slice(half * LANES, (half + 1) * LANES)
        scale = jnp.broadcast_to(by_row[half : half + 1, :], (LANES, LANES)).T
        for i in range(WIDTH // LANES):
            lanes = slice(i * LANES, (i + 1) * LANES)
            done[here, lanes] = grad[here, lanes] * by_col[i : i + 1, :] * scale + decay * weight[here, lanes]
        copies.append(pltpu.make_async_copy(done.at[here], out.at[here], sems.at[half]))
        copies[-1].start()
    for copy in copies:
        copy.wait()


def update(received, row_root, col_root, grad, weight):
    return pl.pallas_call(
        update_kernel,
        out_shape=shape(ROW_BLOCK, WIDTH),
        in_specs=[WHOLE] * 5,
        out_specs=ANYWHERE,
        scratch_shapes=[pltpu.VMEM((ROW_BLOCK, WIDTH), jnp.float32), pltpu.SemaphoreType.DMA((2,))],
        compiler_params=PARAMS,
        cost_estimate=cost(2**20, 3 * 2**20),
    )(received, row_root, col_root, grad, weight)


def shards(activations, out_grads, weight, row_moment, col_moment):
    y, x, core, layer = (lax.axis_index(name) for name in ("y", "x", "core", "z"))
    place = jnp.stack([y, x, core, layer & 1])
    line = gather_line(out_grads)
    packed, line = lax.optimization_barrier((pack(place, activations), line))
    first = turn(place, exchange(packed, CHIPS))
    second = next_layer(first)
    low, high = (line[i : i + 2].reshape(2 * TOKENS, WIDTH) for i in (0, 2))
    back_low, ahead_high = along(low, 1), along(high, SIDE - 1)
    far = [along(back_low, 1), along(ahead_high, SIDE - 1)]
    back, ahead = [back_low, along(high, 1)], [along(low, SIDE - 1), ahead_high]
    blocks = lambda operand: [(operand, 0), (operand, 1), (operand + 1, 0), (operand + 1, 1)]
    total = product(place, (first, first), [low, high], [(0, True, blocks(0))])
    total = product(place, (first, first), back + ahead, [(1, True, blocks(0)), (3, True, blocks(2))], total)
    parts = [(group, False, blocks(2 * i)) for i, group in enumerate((0, 1, 3))]
    total = product(place, (second, second), [low, high] + back + ahead, parts, total)
    parts = [(2, True, blocks(0)), (2, False, blocks(0))]
    theirs = product(place, (first, second), far, parts, total, lambda core: 1 - core)
    received = lax.ppermute(theirs, "core", [(0, 1), (1, 0)])
    mine = product(place, (first, second), far, parts, total, lambda core: core)
    weight_grad, tiles = columns(mine, received)
    new_cols, col_root, tiles = rows(exchange(tiles, ROWS), col_moment.reshape(TILE), weight_grad, weight)
    new_rows, row_root, tiles = scalars(exchange(tiles, "z"), row_moment.reshape(2, LANES))
    out = update(exchange(tiles, ROWS), row_root, col_root, weight_grad, weight)
    return (out, new_rows.reshape(-1), new_cols.reshape(-1))


def solution(mesh):
    mesh = Mesh(mesh.devices.reshape(SIDE, SIDE, 2, LAYERS), ("y", "x", "core", "z"))
    placed = (P(ROWS, None), P(ROWS, "z"), P(ROWS, "z"), P(ROWS), P("z"))
    return jax.shard_map(
        shards,
        mesh=mesh,
        in_specs=placed,
        out_specs=(P(ROWS, "z"), P(ROWS), P("z")),
        check_vma=False,
    )
```

```python
import functools

import jax
import jax.numpy as jnp
from jax import lax
from jax.experimental import pallas as pl
from jax.experimental.pallas import tpu as pltpu
from jax.sharding import Mesh, PartitionSpec as P

D = 8192
FF = 16384


BETA_TWO = 0.8
CLIP_LEVEL = 0.25
WEIGHT_DECAY = 0.1
EPSILON = 1e-06

CHIPS = ("y", "x")
ROWS = ("y", "x", "core")
SIDE = 4
COUNT = SIDE * SIDE
LAYERS = 16
DEVICES = 2 * COUNT
TOKENS = 128
HALF = TOKENS // 2
ROW_BLOCK = 256
WIDTH = 1024
LANES = 128
COLUMNS = 256
TILE = (8, LANES)

ANYWHERE = pl.BlockSpec(memory_space=pl.ANY)
WHOLE = pl.BlockSpec(memory_space=pltpu.VMEM)
SCALARS = pl.BlockSpec(memory_space=pltpu.SMEM)
PARAMS = pltpu.CompilerParams(vmem_limit_bytes=16 * 2**20)


def shape(*dims, dtype=jnp.float32):
    return jax.ShapeDtypeStruct(dims, dtype)


def cost(flops, bytes_accessed):
    return pl.CostEstimate(flops=flops, bytes_accessed=bytes_accessed, transcendentals=0)


def device(y, x, core):
    return ((y % SIDE) * SIDE + x % SIDE) * 2 + core


def along(value, step):
    pairs = []
    for y in range(SIDE):
        for x in range(SIDE):
            pairs.append((device(y, x, 0), device(y + step, x, 0)))
            pairs.append((device(y, x, 1), device(y, x + step, 1)))
    return lax.ppermute(value, ROWS, pairs)


def gather_line(value):
    groups = [[device(y, x, 0) for x in range(SIDE)] for y in range(SIDE)]
    groups += [[device(y, x, 1) for y in range(SIDE)] for x in range(SIDE)]
    sent = jnp.broadcast_to(value, (SIDE,) + value.shape)
    return lax.all_to_all(sent, ROWS, 0, 0, axis_index_groups=groups)


def next_layer(value):
    pairs = [(i, (i + 1) % LAYERS) for i in range(LAYERS)]
    pairs += [(LAYERS + i, LAYERS + (i - 1) % LAYERS) for i in range(LAYERS)]
    return lax.ppermute(value, ("core", "z"), pairs)


def exchange(tiles, axes):
    return lax.all_to_all(tiles, axes, 0, 0)


def pack_kernel(place, source, out, sems):
    rows = pl.ds(pl.multiple_of(place[3] * HALF, HALF), HALF)
    copies = [
        pltpu.make_async_copy(source.at[rows, pl.ds(i * 2 * ROW_BLOCK, 2 * ROW_BLOCK)], out.at[i], sems.at[i])
        for i in range(COUNT)
    ]
    for copy in copies:
        copy.start()
    for copy in copies:
        copy.wait()


def pack(place, activations):
    return pl.pallas_call(
        pack_kernel,
        out_shape=pltpu.VMEM((COUNT, HALF, 2 * ROW_BLOCK), jnp.bfloat16),
        in_specs=[SCALARS, ANYWHERE],
        out_specs=WHOLE,
        scratch_shapes=[pltpu.SemaphoreType.DMA((COUNT,))],
        compiler_params=PARAMS,
        cost_estimate=cost(0, 2**21),
    )(place, pltpu.with_memory_space_constraint(activations, pltpu.HBM))


def turn_kernel(place, part, out):
    y, x, core = place[0], place[1], place[2]

    def block(i):
        j, k = i // SIDE, i % SIDE
        return part[jnp.where(core == 0, ((y - j) & (SIDE - 1)) * SIDE + k, k * SIDE + ((x - j) & (SIDE - 1)))]

    for i in range(0, COUNT, 2):
        out[:, i * HALF : (i + 2) * HALF] = jnp.concatenate([block(i), block(i + 1)], axis=0).T


def turn(place, part):
    return pl.pallas_call(
        turn_kernel,
        out_shape=shape(2 * ROW_BLOCK, COUNT * HALF, dtype=jnp.bfloat16),
        in_specs=[SCALARS, WHOLE],
        out_specs=WHOLE,
        compiler_params=PARAMS,
        cost_estimate=cost(0, 2**21),
    )(place, part)


def product_kernel(parts, which, place, first, second, *refs):
    operands, out = refs[:-1], refs[-1]
    total = operands[-1] if len(operands) > 1 + max(index for *_, blocks in parts for index, _ in blocks) else None
    start = place[3] * HALF
    rows = pl.ds(0 if which is None else pl.multiple_of(which(place[2]) * ROW_BLOCK, ROW_BLOCK), out.shape[0])

    @pl.loop(0, WIDTH // COLUMNS)
    def _(n):
        columns = pl.ds(pl.multiple_of(n * COLUMNS, COLUMNS), COLUMNS)
        value = None if total is None else total[rows, columns]
        for group, exchanged, blocks in parts:
            depth = slice(group * SIDE * HALF, (group + 1) * SIDE * HALF)
            features, offset = (first, start) if exchanged else (second, HALF - start)
            offset = pl.multiple_of(offset, HALF)
            grads = [operands[index][pl.ds(i * TOKENS + offset, HALF), columns] for index, i in blocks]
            term = jnp.dot(features[rows, depth], jnp.concatenate(grads, axis=0), preferred_element_type=jnp.float32)
            value = term if value is None else value + term
        out[:, columns] = value


def product(place, features, operands, parts, total=None, which=None):
    count = 2 * ROW_BLOCK if which is None else ROW_BLOCK
    operands = [*features, *operands] + ([] if total is None else [total])
    return pl.pallas_call(
        functools.partial(product_kernel, parts, which),
        out_shape=shape(count, WIDTH),
        in_specs=[SCALARS] + [WHOLE] * len(operands),
        out_specs=WHOLE,
        compiler_params=PARAMS,
        cost_estimate=cost(24 * count * SIDE * HALF * WIDTH * len(parts), 2**20),
    )(place, *operands)


def columns_kernel(mine, theirs, grad, sent):
    value = mine[...] + theirs[...]
    grad[...] = value
    sums = jnp.sum(value * value, axis=0, keepdims=True)
    tile = jnp.concatenate([sums[:, i * LANES : (i + 1) * LANES] for i in range(8)], axis=0)
    for i in range(DEVICES):
        sent[i] = tile


def columns(mine, theirs):
    return pl.pallas_call(
        columns_kernel,
        out_shape=(shape(ROW_BLOCK, WIDTH), shape(DEVICES, *TILE)),
        in_specs=[WHOLE] * 2,
        out_specs=(WHOLE, WHOLE),
        compiler_params=PARAMS,
        cost_estimate=cost(2**20, 3 * 2**20),
    )(mine, theirs)


def rows_kernel(received, moment, grad, weight, cols, col_root, sent):
    new = BETA_TWO * moment[...] + (1.0 - BETA_TWO) * (jnp.sum(received[...], axis=0) / D)
    cols[...] = new
    root = lax.rsqrt(new)
    col_root[...] = root
    sums = [jnp.zeros((ROW_BLOCK, LANES), jnp.float32)] * 4
    for i in range(WIDTH // LANES):
        lanes = slice(i * LANES, (i + 1) * LANES)
        value, held = grad[:, lanes], weight[:, lanes]
        by_cols = value * root[i : i + 1, :]
        terms = (value * value, by_cols * by_cols, by_cols * held, held * held)
        sums = [a + b for a, b in zip(sums, terms)]
    parts = []
    for value in sums:
        for row in range(0, ROW_BLOCK, LANES):
            parts.append(jnp.sum(value[row : row + LANES, :].T, axis=0, keepdims=True))
    tile = jnp.concatenate(parts, axis=0)
    for i in range(LAYERS):
        sent[i] = tile


def rows(received, moment, grad, weight):
    return pl.pallas_call(
        rows_kernel,
        out_shape=(shape(*TILE), shape(*TILE), shape(LAYERS, *TILE)),
        in_specs=[WHOLE] * 4,
        out_specs=(WHOLE, WHOLE, WHOLE),
        compiler_params=PARAMS,
        cost_estimate=cost(2**21, 2**21),
    )(received, moment, grad, weight)


def scalars_kernel(received, moment, rows_out, row_root, sent):
    parts = jnp.sum(received[...], axis=0)
    new = BETA_TWO * moment[...] + (1.0 - BETA_TWO) * (parts[0:2] / FF)
    rows_out[...] = new
    root = lax.rsqrt(new)
    row_root[...] = root
    sums = [jnp.sum(part, axis=0, keepdims=True) for part in (parts[2:4] * root * root, parts[4:6] * root, parts[6:8])]
    tile = jnp.concatenate(sums + [jnp.zeros_like(sums[0])], axis=0)
    for i in range(DEVICES):
        sent[i] = tile


def scalars(received, moment):
    return pl.pallas_call(
        scalars_kernel,
        out_shape=(shape(2, LANES), shape(2, LANES), shape(DEVICES, 4, LANES)),
        in_specs=[WHOLE] * 2,
        out_specs=(WHOLE, WHOLE, WHOLE),
        compiler_params=PARAMS,
        cost_estimate=cost(2**14, 2**18),
    )(received, moment)


def update_kernel(received, row_root, col_root, grad, weight, out, done, sems):
    parts = jnp.sum(received[...], axis=0)
    scaled_sum, cross_sum, weight_sum = (jnp.sum(parts[i : i + 1], keepdims=True) for i in range(3))
    factor = 1.0 / jnp.maximum(1.0, jnp.sqrt(scaled_sum / (D * FF)) / CLIP_LEVEL)
    direction_sum = (
        factor * factor * scaled_sum + 2.0 * WEIGHT_DECAY * factor * cross_sum + WEIGHT_DECAY * WEIGHT_DECAY * weight_sum
    )
    trust_ratio = jnp.sqrt(weight_sum / (jnp.maximum(direction_sum, 0.0) + EPSILON))
    by_row = row_root[...] * (trust_ratio * factor)
    by_col = col_root[...]
    decay = trust_ratio * WEIGHT_DECAY
    copies = []
    for half in range(2):
        here = slice(half * LANES, (half + 1) * LANES)
        scale = jnp.broadcast_to(by_row[half : half + 1, :], (LANES, LANES)).T
        for i in range(WIDTH // LANES):
            lanes = slice(i * LANES, (i + 1) * LANES)
            done[here, lanes] = grad[here, lanes] * by_col[i : i + 1, :] * scale + decay * weight[here, lanes]
        copies.append(pltpu.make_async_copy(done.at[here], out.at[here], sems.at[half]))
        copies[-1].start()
    for copy in copies:
        copy.wait()


def update(received, row_root, col_root, grad, weight):
    return pl.pallas_call(
        update_kernel,
        out_shape=shape(ROW_BLOCK, WIDTH),
        in_specs=[WHOLE] * 5,
        out_specs=ANYWHERE,
        scratch_shapes=[pltpu.VMEM((ROW_BLOCK, WIDTH), jnp.float32), pltpu.SemaphoreType.DMA((2,))],
        compiler_params=PARAMS,
        cost_estimate=cost(2**20, 3 * 2**20),
    )(received, row_root, col_root, grad, weight)


def shards(activations, out_grads, weight, row_moment, col_moment):
    y, x, core, layer = (lax.axis_index(name) for name in ("y", "x", "core", "z"))
    place = jnp.stack([y, x, core, layer & 1])
    line = gather_line(out_grads)
    packed, line = lax.optimization_barrier((pack(place, activations), line))
    first = turn(place, exchange(packed, CHIPS))
    second = next_layer(first)
    low, high = (line[i : i + 2].reshape(2 * TOKENS, WIDTH) for i in (0, 2))
    back_low, ahead_high = along(low, 1), along(high, SIDE - 1)
    far = [along(back_low, 1), along(ahead_high, SIDE - 1)]
    back, ahead = [back_low, along(high, 1)], [along(low, SIDE - 1), ahead_high]
    blocks = lambda operand: [(operand, 0), (operand, 1), (operand + 1, 0), (operand + 1, 1)]
    total = product(place, (first, first), [low, high], [(0, True, blocks(0))])
    total = product(place, (first, first), back + ahead, [(1, True, blocks(0)), (3, True, blocks(2))], total)
    operands = [low, high] + back + ahead + far
    parts = [(2, True, blocks(6)), (2, False, blocks(6))]
    parts += [(group, False, blocks(2 * i)) for i, group in enumerate((0, 1, 3))]
    theirs = product(place, (first, second), operands, parts, total, lambda core: 1 - core)
    received = lax.ppermute(theirs, "core", [(0, 1), (1, 0)])
    mine = product(place, (first, second), operands, parts, total, lambda core: core)
    weight_grad, tiles = columns(mine, received)
    new_cols, col_root, tiles = rows(exchange(tiles, ROWS), col_moment.reshape(TILE), weight_grad, weight)
    new_rows, row_root, tiles = scalars(exchange(tiles, "z"), row_moment.reshape(2, LANES))
    out = update(exchange(tiles, ROWS), row_root, col_root, weight_grad, weight)
    return (out, new_rows.reshape(-1), new_cols.reshape(-1))


def solution(mesh):
    mesh = Mesh(mesh.devices.reshape(SIDE, SIDE, 2, LAYERS), ("y", "x", "core", "z"))
    placed = (P(ROWS, None), P(ROWS, "z"), P(ROWS, "z"), P(ROWS), P("z"))
    return jax.shard_map(
        shards,
        mesh=mesh,
        in_specs=placed,
        out_specs=(P(ROWS, "z"), P(ROWS), P("z")),
        check_vma=False,
    )
```

```python
import functools

import jax
import jax.numpy as jnp
from jax import lax
from jax.experimental import pallas as pl
from jax.experimental.pallas import tpu as pltpu
from jax.sharding import Mesh, PartitionSpec as P

D = 8192
FF = 16384


BETA_TWO = 0.8
CLIP_LEVEL = 0.25
WEIGHT_DECAY = 0.1
EPSILON = 1e-06

CHIPS = ("y", "x")
ROWS = ("y", "x", "core")
SIDE = 4
COUNT = SIDE * SIDE
LAYERS = 16
DEVICES = 2 * COUNT
TOKENS = 128
HALF = TOKENS // 2
ROW_BLOCK = 256
WIDTH = 1024
LANES = 128
COLUMNS = 256
TILE = (8, LANES)

ANYWHERE = pl.BlockSpec(memory_space=pl.ANY)
WHOLE = pl.BlockSpec(memory_space=pltpu.VMEM)
SCALARS = pl.BlockSpec(memory_space=pltpu.SMEM)
PARAMS = pltpu.CompilerParams(vmem_limit_bytes=16 * 2**20)


def shape(*dims, dtype=jnp.float32):
    return jax.ShapeDtypeStruct(dims, dtype)


def cost(flops, bytes_accessed):
    return pl.CostEstimate(flops=flops, bytes_accessed=bytes_accessed, transcendentals=0)


def device(y, x, core):
    return ((y % SIDE) * SIDE + x % SIDE) * 2 + core


def along(value, step):
    pairs = []
    for y in range(SIDE):
        for x in range(SIDE):
            pairs.append((device(y, x, 0), device(y + step, x, 0)))
            pairs.append((device(y, x, 1), device(y, x + step, 1)))
    return lax.ppermute(value, ROWS, pairs)


def gather_line(value):
    groups = [[device(y, x, 0) for x in range(SIDE)] for y in range(SIDE)]
    groups += [[device(y, x, 1) for y in range(SIDE)] for x in range(SIDE)]
    sent = jnp.broadcast_to(value, (SIDE,) + value.shape)
    return lax.all_to_all(sent, ROWS, 0, 0, axis_index_groups=groups)


def next_layer(value):
    pairs = [(i, (i + 1) % LAYERS) for i in range(LAYERS)]
    pairs += [(LAYERS + i, LAYERS + (i - 1) % LAYERS) for i in range(LAYERS)]
    return lax.ppermute(value, ("core", "z"), pairs)


def exchange(tiles, axes):
    return lax.all_to_all(tiles, axes, 0, 0)


def pack_kernel(place, source, out, sems):
    rows = pl.ds(pl.multiple_of(place[3] * HALF, HALF), HALF)
    copies = [
        pltpu.make_async_copy(source.at[rows, pl.ds(i * 2 * ROW_BLOCK, 2 * ROW_BLOCK)], out.at[i], sems.at[i])
        for i in range(COUNT)
    ]
    for copy in copies:
        copy.start()
    for copy in copies:
        copy.wait()


def pack(place, activations):
    return pl.pallas_call(
        pack_kernel,
        out_shape=pltpu.VMEM((COUNT, HALF, 2 * ROW_BLOCK), jnp.bfloat16),
        in_specs=[SCALARS, ANYWHERE],
        out_specs=WHOLE,
        scratch_shapes=[pltpu.SemaphoreType.DMA((COUNT,))],
        compiler_params=PARAMS,
        cost_estimate=cost(0, 2**21),
    )(place, pltpu.with_memory_space_constraint(activations, pltpu.HBM))


def turn_kernel(place, part, out):
    y, x, core = place[0], place[1], place[2]

    def block(i):
        j, k = i // SIDE, i % SIDE
        return part[jnp.where(core == 0, ((y - j) & (SIDE - 1)) * SIDE + k, k * SIDE + ((x - j) & (SIDE - 1)))]

    for i in range(0, COUNT, 2):
        out[:, i * HALF : (i + 2) * HALF] = jnp.concatenate([block(i), block(i + 1)], axis=0).T


def turn(place, part):
    return pl.pallas_call(
        turn_kernel,
        out_shape=shape(2 * ROW_BLOCK, COUNT * HALF, dtype=jnp.bfloat16),
        in_specs=[SCALARS, WHOLE],
        out_specs=WHOLE,
        compiler_params=PARAMS,
        cost_estimate=cost(0, 2**21),
    )(place, part)


def product_kernel(parts, which, place, first, second, *refs):
    operands, out = refs[:-1], refs[-1]
    total = operands[-1] if len(operands) > 1 + max(index for *_, blocks in parts for index, _ in blocks) else None
    start = place[3] * HALF
    rows = pl.ds(0 if which is None else pl.multiple_of(which(place[2]) * ROW_BLOCK, ROW_BLOCK), out.shape[0])

    @pl.loop(0, WIDTH // COLUMNS)
    def _(n):
        columns = pl.ds(pl.multiple_of(n * COLUMNS, COLUMNS), COLUMNS)
        value = None if total is None else total[rows, columns]
        for group, exchanged, blocks in parts:
            depth = slice(group * SIDE * HALF, group * SIDE * HALF + len(blocks) * HALF)
            features, offset = (first, start) if exchanged else (second, HALF - start)
            offset = pl.multiple_of(offset, HALF)
            grads = [operands[index][pl.ds(i * TOKENS + offset, HALF), columns] for index, i in blocks]
            term = jnp.dot(features[rows, depth], jnp.concatenate(grads, axis=0), preferred_element_type=jnp.float32)
            value = term if value is None else value + term
        out[:, columns] = value


def product(place, features, operands, parts, total=None, which=None):
    count = 2 * ROW_BLOCK if which is None else ROW_BLOCK
    operands = [*features, *operands] + ([] if total is None else [total])
    return pl.pallas_call(
        functools.partial(product_kernel, parts, which),
        out_shape=shape(count, WIDTH),
        in_specs=[SCALARS] + [WHOLE] * len(operands),
        out_specs=WHOLE,
        input_output_aliases={len(operands): 0} if total is not None and which is None else {},
        compiler_params=PARAMS,
        cost_estimate=cost(24 * count * HALF * WIDTH * sum(len(part[2]) for part in parts), 2**20),
    )(place, *operands)


def columns_kernel(mine, theirs, grad, sent):
    value = mine[...] + theirs[...]
    grad[...] = value
    sums = jnp.sum(value * value, axis=0, keepdims=True)
    tile = jnp.concatenate([sums[:, i * LANES : (i + 1) * LANES] for i in range(8)], axis=0)
    for i in range(DEVICES):
        sent[i] = tile


def columns(mine, theirs):
    return pl.pallas_call(
        columns_kernel,
        out_shape=(shape(ROW_BLOCK, WIDTH), shape(DEVICES, *TILE)),
        in_specs=[WHOLE] * 2,
        out_specs=(WHOLE, WHOLE),
        compiler_params=PARAMS,
        cost_estimate=cost(2**20, 3 * 2**20),
    )(mine, theirs)


def rows_kernel(received, moment, grad, weight, cols, col_root, sent):
    new = BETA_TWO * moment[...] + (1.0 - BETA_TWO) * (jnp.sum(received[...], axis=0) / D)
    cols[...] = new
    root = lax.rsqrt(new)
    col_root[...] = root
    sums = [jnp.zeros((ROW_BLOCK, LANES), jnp.float32)] * 4
    for i in range(WIDTH // LANES):
        lanes = slice(i * LANES, (i + 1) * LANES)
        value, held = grad[:, lanes], weight[:, lanes]
        by_cols = value * root[i : i + 1, :]
        terms = (value * value, by_cols * by_cols, by_cols * held, held * held)
        sums = [a + b for a, b in zip(sums, terms)]
    parts = []
    for value in sums:
        for row in range(0, ROW_BLOCK, LANES):
            parts.append(jnp.sum(value[row : row + LANES, :].T, axis=0, keepdims=True))
    tile = jnp.concatenate(parts, axis=0)
    for i in range(LAYERS):
        sent[i] = tile


def rows(received, moment, grad, weight):
    return pl.pallas_call(
        rows_kernel,
        out_shape=(shape(*TILE), shape(*TILE), shape(LAYERS, *TILE)),
        in_specs=[WHOLE] * 4,
        out_specs=(WHOLE, WHOLE, WHOLE),
        compiler_params=PARAMS,
        cost_estimate=cost(2**21, 2**21),
    )(received, moment, grad, weight)


def scalars_kernel(received, moment, rows_out, row_root, sent):
    parts = jnp.sum(received[...], axis=0)
    new = BETA_TWO * moment[...] + (1.0 - BETA_TWO) * (parts[0:2] / FF)
    rows_out[...] = new
    root = lax.rsqrt(new)
    row_root[...] = root
    sums = [jnp.sum(part, axis=0, keepdims=True) for part in (parts[2:4] * root * root, parts[4:6] * root, parts[6:8])]
    tile = jnp.concatenate(sums + [jnp.zeros_like(sums[0])], axis=0)
    for i in range(DEVICES):
        sent[i] = tile


def scalars(received, moment):
    return pl.pallas_call(
        scalars_kernel,
        out_shape=(shape(2, LANES), shape(2, LANES), shape(DEVICES, 4, LANES)),
        in_specs=[WHOLE] * 2,
        out_specs=(WHOLE, WHOLE, WHOLE),
        compiler_params=PARAMS,
        cost_estimate=cost(2**14, 2**18),
    )(received, moment)


def update_kernel(received, row_root, col_root, grad, weight, out, done, sems):
    parts = jnp.sum(received[...], axis=0)
    scaled_sum, cross_sum, weight_sum = (jnp.sum(parts[i : i + 1], keepdims=True) for i in range(3))
    factor = 1.0 / jnp.maximum(1.0, jnp.sqrt(scaled_sum / (D * FF)) / CLIP_LEVEL)
    direction_sum = (
        factor * factor * scaled_sum + 2.0 * WEIGHT_DECAY * factor * cross_sum + WEIGHT_DECAY * WEIGHT_DECAY * weight_sum
    )
    trust_ratio = jnp.sqrt(weight_sum / (jnp.maximum(direction_sum, 0.0) + EPSILON))
    by_row = row_root[...] * (trust_ratio * factor)
    by_col = col_root[...]
    decay = trust_ratio * WEIGHT_DECAY
    copies = []
    for half in range(2):
        here = slice(half * LANES, (half + 1) * LANES)
        scale = jnp.broadcast_to(by_row[half : half + 1, :], (LANES, LANES)).T
        for i in range(WIDTH // LANES):
            lanes = slice(i * LANES, (i + 1) * LANES)
            done[here, lanes] = grad[here, lanes] * by_col[i : i + 1, :] * scale + decay * weight[here, lanes]
        copies.append(pltpu.make_async_copy(done.at[here], out.at[here], sems.at[half]))
        copies[-1].start()
    for copy in copies:
        copy.wait()


def update(received, row_root, col_root, grad, weight):
    return pl.pallas_call(
        update_kernel,
        out_shape=shape(ROW_BLOCK, WIDTH),
        in_specs=[WHOLE] * 5,
        out_specs=ANYWHERE,
        scratch_shapes=[pltpu.VMEM((ROW_BLOCK, WIDTH), jnp.float32), pltpu.SemaphoreType.DMA((2,))],
        compiler_params=PARAMS,
        cost_estimate=cost(2**20, 3 * 2**20),
    )(received, row_root, col_root, grad, weight)


def shards(activations, out_grads, weight, row_moment, col_moment):
    y, x, core, layer = (lax.axis_index(name) for name in ("y", "x", "core", "z"))
    place = jnp.stack([y, x, core, layer & 1])
    line = gather_line(out_grads)
    packed, line = lax.optimization_barrier((pack(place, activations), line))
    first = turn(place, exchange(packed, CHIPS))
    second = next_layer(first)
    low, high = (line[i : i + 2].reshape(2 * TOKENS, WIDTH) for i in (0, 2))
    back_low, ahead_high = along(low, 1), along(high, SIDE - 1)
    far = [along(back_low, 1), along(ahead_high, SIDE - 1)]
    back, ahead = [back_low, along(high, 1)], [along(low, SIDE - 1), ahead_high]
    blocks = lambda operand: [(operand, 0), (operand, 1), (operand + 1, 0), (operand + 1, 1)]
    total = product(place, (first, first), [low, high], [(0, True, blocks(0))])
    parts = [(1, True, blocks(0)), (3, True, blocks(2))]
    total = product(place, (first, first), back + ahead, parts, total)
    operands = [low, high] + back + far + ahead
    parts = [(2, True, blocks(4)), (0, False, blocks(0) + blocks(2) + blocks(4) + blocks(6))]
    theirs = product(place, (first, second), operands, parts, total, lambda core: 1 - core)
    received = lax.ppermute(theirs, "core", [(0, 1), (1, 0)])
    mine = product(place, (first, second), operands, parts, total, lambda core: core)
    weight_grad, tiles = columns(mine, received)
    new_cols, col_root, tiles = rows(exchange(tiles, ROWS), col_moment.reshape(TILE), weight_grad, weight)
    new_rows, row_root, tiles = scalars(exchange(tiles, "z"), row_moment.reshape(2, LANES))
    out = update(exchange(tiles, ROWS), row_root, col_root, weight_grad, weight)
    return (out, new_rows.reshape(-1), new_cols.reshape(-1))


def solution(mesh):
    mesh = Mesh(mesh.devices.reshape(SIDE, SIDE, 2, LAYERS), ("y", "x", "core", "z"))
    placed = (P(ROWS, None), P(ROWS, "z"), P(ROWS, "z"), P(ROWS), P("z"))
    return jax.shard_map(
        shards,
        mesh=mesh,
        in_specs=placed,
        out_specs=(P(ROWS, "z"), P(ROWS), P("z")),
        check_vma=False,
    )
```

```python
import functools

import jax
import jax.numpy as jnp
from jax import lax
from jax.experimental import pallas as pl
from jax.experimental.pallas import tpu as pltpu
from jax.sharding import Mesh, PartitionSpec as P

D = 8192
FF = 16384


BETA_TWO = 0.8
CLIP_LEVEL = 0.25
WEIGHT_DECAY = 0.1
EPSILON = 1e-06

CHIPS = ("y", "x")
ROWS = ("y", "x", "core")
SIDE = 4
COUNT = SIDE * SIDE
LAYERS = 16
DEVICES = 2 * COUNT
TOKENS = 128
HALF = TOKENS // 2
ROW_BLOCK = 256
WIDTH = 1024
LANES = 128
COLUMNS = 256
TILE = (8, LANES)

ANYWHERE = pl.BlockSpec(memory_space=pl.ANY)
WHOLE = pl.BlockSpec(memory_space=pltpu.VMEM)
SCALARS = pl.BlockSpec(memory_space=pltpu.SMEM)
PARAMS = pltpu.CompilerParams(vmem_limit_bytes=16 * 2**20)


def shape(*dims, dtype=jnp.float32):
    return jax.ShapeDtypeStruct(dims, dtype)


def cost(flops, bytes_accessed):
    return pl.CostEstimate(flops=flops, bytes_accessed=bytes_accessed, transcendentals=0)


def device(y, x, core):
    return ((y % SIDE) * SIDE + x % SIDE) * 2 + core


def along(value, step):
    pairs = []
    for y in range(SIDE):
        for x in range(SIDE):
            pairs.append((device(y, x, 0), device(y, x + step, 0)))
            pairs.append((device(y, x, 1), device(y + step, x, 1)))
    return lax.ppermute(value, ROWS, pairs)


def gather_line(value):
    groups = [[device(y, x, 0) for y in range(SIDE)] for x in range(SIDE)]
    groups += [[device(y, x, 1) for x in range(SIDE)] for y in range(SIDE)]
    sent = jnp.broadcast_to(value, (SIDE,) + value.shape)
    return lax.all_to_all(sent, ROWS, 0, 0, axis_index_groups=groups)


def next_layer(value):
    pairs = [(i, (i + 1) % LAYERS) for i in range(LAYERS)]
    pairs += [(LAYERS + i, LAYERS + (i - 1) % LAYERS) for i in range(LAYERS)]
    return lax.ppermute(value, ("core", "z"), pairs)


def exchange(tiles, axes):
    return lax.all_to_all(tiles, axes, 0, 0)


def pack_kernel(place, source, out, sems):
    rows = pl.ds(pl.multiple_of(place[3] * HALF, HALF), HALF)
    copies = [
        pltpu.make_async_copy(source.at[rows, pl.ds(i * 2 * ROW_BLOCK, 2 * ROW_BLOCK)], out.at[i], sems.at[i])
        for i in range(COUNT)
    ]
    for copy in copies:
        copy.start()
    for copy in copies:
        copy.wait()


def pack(place, activations):
    return pl.pallas_call(
        pack_kernel,
        out_shape=pltpu.VMEM((COUNT, HALF, 2 * ROW_BLOCK), jnp.bfloat16),
        in_specs=[SCALARS, ANYWHERE],
        out_specs=WHOLE,
        scratch_shapes=[pltpu.SemaphoreType.DMA((COUNT,))],
        compiler_params=PARAMS,
        cost_estimate=cost(0, 2**21),
    )(place, pltpu.with_memory_space_constraint(activations, pltpu.HBM))


def turn_kernel(place, part, out):
    y, x, core = place[0], place[1], place[2]

    def block(i):
        j, k = i // SIDE, i % SIDE
        return part[jnp.where(core == 1, ((y - j) & (SIDE - 1)) * SIDE + k, k * SIDE + ((x - j) & (SIDE - 1)))]

    for i in range(0, COUNT, 2):
        out[:, i * HALF : (i + 2) * HALF] = jnp.concatenate([block(i), block(i + 1)], axis=0).T


def turn(place, part):
    return pl.pallas_call(
        turn_kernel,
        out_shape=shape(2 * ROW_BLOCK, COUNT * HALF, dtype=jnp.bfloat16),
        in_specs=[SCALARS, WHOLE],
        out_specs=WHOLE,
        compiler_params=PARAMS,
        cost_estimate=cost(0, 2**21),
    )(place, part)


def product_kernel(parts, which, place, first, second, *refs):
    operands, out = refs[:-1], refs[-1]
    total = operands[-1] if len(operands) > 1 + max(index for *_, blocks in parts for index, _ in blocks) else None
    start = place[3] * HALF
    rows = pl.ds(0 if which is None else pl.multiple_of(which(place[2]) * ROW_BLOCK, ROW_BLOCK), out.shape[0])

    @pl.loop(0, WIDTH // COLUMNS)
    def _(n):
        columns = pl.ds(pl.multiple_of(n * COLUMNS, COLUMNS), COLUMNS)
        value = None if total is None else total[rows, columns]
        for group, exchanged, blocks in parts:
            depth = slice(group * SIDE * HALF, group * SIDE * HALF + len(blocks) * HALF)
            features, offset = (first, start) if exchanged else (second, HALF - start)
            offset = pl.multiple_of(offset, HALF)
            grads = [operands[index][pl.ds(i * TOKENS + offset, HALF), columns] for index, i in blocks]
            term = jnp.dot(features[rows, depth], jnp.concatenate(grads, axis=0), preferred_element_type=jnp.float32)
            value = term if value is None else value + term
        out[:, columns] = value


def product(place, features, operands, parts, total=None, which=None):
    count = 2 * ROW_BLOCK if which is None else ROW_BLOCK
    operands = [*features, *operands] + ([] if total is None else [total])
    return pl.pallas_call(
        functools.partial(product_kernel, parts, which),
        out_shape=shape(count, WIDTH),
        in_specs=[SCALARS] + [WHOLE] * len(operands),
        out_specs=WHOLE,
        input_output_aliases={len(operands): 0} if total is not None and which is None else {},
        compiler_params=PARAMS,
        cost_estimate=cost(24 * count * HALF * WIDTH * sum(len(part[2]) for part in parts), 2**20),
    )(place, *operands)


def columns_kernel(mine, theirs, grad, sent):
    value = mine[...] + theirs[...]
    grad[...] = value
    sums = jnp.sum(value * value, axis=0, keepdims=True)
    tile = jnp.concatenate([sums[:, i * LANES : (i + 1) * LANES] for i in range(8)], axis=0)
    for i in range(DEVICES):
        sent[i] = tile


def columns(mine, theirs):
    return pl.pallas_call(
        columns_kernel,
        out_shape=(shape(ROW_BLOCK, WIDTH), shape(DEVICES, *TILE)),
        in_specs=[WHOLE] * 2,
        out_specs=(WHOLE, WHOLE),
        compiler_params=PARAMS,
        cost_estimate=cost(2**20, 3 * 2**20),
    )(mine, theirs)


def rows_kernel(received, moment, grad, weight, cols, col_root, sent):
    new = BETA_TWO * moment[...] + (1.0 - BETA_TWO) * (jnp.sum(received[...], axis=0) / D)
    cols[...] = new
    root = lax.rsqrt(new)
    col_root[...] = root
    sums = [jnp.zeros((ROW_BLOCK, LANES), jnp.float32)] * 4
    for i in range(WIDTH // LANES):
        lanes = slice(i * LANES, (i + 1) * LANES)
        value, held = grad[:, lanes], weight[:, lanes]
        by_cols = value * root[i : i + 1, :]
        terms = (value * value, by_cols * by_cols, by_cols * held, held * held)
        sums = [a + b for a, b in zip(sums, terms)]
    parts = []
    for value in sums:
        for row in range(0, ROW_BLOCK, LANES):
            parts.append(jnp.sum(value[row : row + LANES, :].T, axis=0, keepdims=True))
    tile = jnp.concatenate(parts, axis=0)
    for i in range(LAYERS):
        sent[i] = tile


def rows(received, moment, grad, weight):
    return pl.pallas_call(
        rows_kernel,
        out_shape=(shape(*TILE), shape(*TILE), shape(LAYERS, *TILE)),
        in_specs=[WHOLE] * 4,
        out_specs=(WHOLE, WHOLE, WHOLE),
        compiler_params=PARAMS,
        cost_estimate=cost(2**21, 2**21),
    )(received, moment, grad, weight)


def scalars_kernel(received, moment, rows_out, row_root, sent):
    parts = jnp.sum(received[...], axis=0)
    new = BETA_TWO * moment[...] + (1.0 - BETA_TWO) * (parts[0:2] / FF)
    rows_out[...] = new
    root = lax.rsqrt(new)
    row_root[...] = root
    sums = [jnp.sum(part, axis=0, keepdims=True) for part in (parts[2:4] * root * root, parts[4:6] * root, parts[6:8])]
    tile = jnp.concatenate(sums + [jnp.zeros_like(sums[0])], axis=0)
    for i in range(DEVICES):
        sent[i] = tile


def scalars(received, moment):
    return pl.pallas_call(
        scalars_kernel,
        out_shape=(shape(2, LANES), shape(2, LANES), shape(DEVICES, 4, LANES)),
        in_specs=[WHOLE] * 2,
        out_specs=(WHOLE, WHOLE, WHOLE),
        compiler_params=PARAMS,
        cost_estimate=cost(2**14, 2**18),
    )(received, moment)


def update_kernel(received, row_root, col_root, grad, weight, out, done, sems):
    parts = jnp.sum(received[...], axis=0)
    scaled_sum, cross_sum, weight_sum = (jnp.sum(parts[i : i + 1], keepdims=True) for i in range(3))
    factor = 1.0 / jnp.maximum(1.0, jnp.sqrt(scaled_sum / (D * FF)) / CLIP_LEVEL)
    direction_sum = (
        factor * factor * scaled_sum + 2.0 * WEIGHT_DECAY * factor * cross_sum + WEIGHT_DECAY * WEIGHT_DECAY * weight_sum
    )
    trust_ratio = jnp.sqrt(weight_sum / (jnp.maximum(direction_sum, 0.0) + EPSILON))
    by_row = row_root[...] * (trust_ratio * factor)
    by_col = col_root[...]
    decay = trust_ratio * WEIGHT_DECAY
    copies = []
    for half in range(2):
        here = slice(half * LANES, (half + 1) * LANES)
        scale = jnp.broadcast_to(by_row[half : half + 1, :], (LANES, LANES)).T
        for i in range(WIDTH // LANES):
            lanes = slice(i * LANES, (i + 1) * LANES)
            done[here, lanes] = grad[here, lanes] * by_col[i : i + 1, :] * scale + decay * weight[here, lanes]
        copies.append(pltpu.make_async_copy(done.at[here], out.at[here], sems.at[half]))
        copies[-1].start()
    for copy in copies:
        copy.wait()


def update(received, row_root, col_root, grad, weight):
    return pl.pallas_call(
        update_kernel,
        out_shape=shape(ROW_BLOCK, WIDTH),
        in_specs=[WHOLE] * 5,
        out_specs=ANYWHERE,
        scratch_shapes=[pltpu.VMEM((ROW_BLOCK, WIDTH), jnp.float32), pltpu.SemaphoreType.DMA((2,))],
        compiler_params=PARAMS,
        cost_estimate=cost(2**20, 3 * 2**20),
    )(received, row_root, col_root, grad, weight)


def shards(activations, out_grads, weight, row_moment, col_moment):
    y, x, core, layer = (lax.axis_index(name) for name in ("y", "x", "core", "z"))
    place = jnp.stack([y, x, core, layer & 1])
    line = gather_line(out_grads)
    packed, line = lax.optimization_barrier((pack(place, activations), line))
    first = turn(place, exchange(packed, CHIPS))
    second = next_layer(first)
    low, high = (line[i : i + 2].reshape(2 * TOKENS, WIDTH) for i in (0, 2))
    back_low, ahead_high = along(low, 1), along(high, SIDE - 1)
    far = [along(back_low, 1), along(ahead_high, SIDE - 1)]
    back, ahead = [back_low, along(high, 1)], [along(low, SIDE - 1), ahead_high]
    blocks = lambda operand: [(operand, 0), (operand, 1), (operand + 1, 0), (operand + 1, 1)]
    total = product(place, (first, first), [low, high], [(0, True, blocks(0))])
    parts = [(1, True, blocks(0)), (3, True, blocks(2))]
    total = product(place, (first, first), back + ahead, parts, total)
    operands = [low, high] + back + far + ahead
    parts = [(2, True, blocks(4)), (0, False, blocks(0) + blocks(2) + blocks(4) + blocks(6))]
    theirs = product(place, (first, second), operands, parts, total, lambda core: 1 - core)
    received = lax.ppermute(theirs, "core", [(0, 1), (1, 0)])
    mine = product(place, (first, second), operands, parts, total, lambda core: core)
    weight_grad, tiles = columns(mine, received)
    new_cols, col_root, tiles = rows(exchange(tiles, ROWS), col_moment.reshape(TILE), weight_grad, weight)
    new_rows, row_root, tiles = scalars(exchange(tiles, "z"), row_moment.reshape(2, LANES))
    out = update(exchange(tiles, ROWS), row_root, col_root, weight_grad, weight)
    return (out, new_rows.reshape(-1), new_cols.reshape(-1))


def solution(mesh):
    mesh = Mesh(mesh.devices.reshape(SIDE, SIDE, 2, LAYERS), ("y", "x", "core", "z"))
    placed = (P(ROWS, None), P(ROWS, "z"), P(ROWS, "z"), P(ROWS), P("z"))
    return jax.shard_map(
        shards,
        mesh=mesh,
        in_specs=placed,
        out_specs=(P(ROWS, "z"), P(ROWS), P("z")),
        check_vma=False,
    )
```

```python
import functools

import jax
import jax.numpy as jnp
from jax import lax
from jax.experimental import pallas as pl
from jax.experimental.pallas import tpu as pltpu
from jax.sharding import Mesh, PartitionSpec as P

D = 8192
FF = 16384


BETA_TWO = 0.8
CLIP_LEVEL = 0.25
WEIGHT_DECAY = 0.1
EPSILON = 1e-06

CHIPS = ("y", "x")
ROWS = ("y", "x", "core")
SIDE = 4
COUNT = SIDE * SIDE
LAYERS = 16
DEVICES = 2 * COUNT
TOKENS = 128
HALF = TOKENS // 2
ROW_BLOCK = 256
WIDTH = 1024
LANES = 128
COLUMNS = 512
TILE = (8, LANES)

ANYWHERE = pl.BlockSpec(memory_space=pl.ANY)
WHOLE = pl.BlockSpec(memory_space=pltpu.VMEM)
SCALARS = pl.BlockSpec(memory_space=pltpu.SMEM)
PARAMS = pltpu.CompilerParams(vmem_limit_bytes=16 * 2**20)


def shape(*dims, dtype=jnp.float32):
    return jax.ShapeDtypeStruct(dims, dtype)


def cost(flops, bytes_accessed):
    return pl.CostEstimate(flops=flops, bytes_accessed=bytes_accessed, transcendentals=0)


def device(y, x, core):
    return ((y % SIDE) * SIDE + x % SIDE) * 2 + core


def along(value, step):
    pairs = []
    for y in range(SIDE):
        for x in range(SIDE):
            pairs.append((device(y, x, 0), device(y, x + step, 0)))
            pairs.append((device(y, x, 1), device(y + step, x, 1)))
    return lax.ppermute(value, ROWS, pairs)


def gather_line(value):
    groups = [[device(y, x, 0) for y in range(SIDE)] for x in range(SIDE)]
    groups += [[device(y, x, 1) for x in range(SIDE)] for y in range(SIDE)]
    sent = jnp.broadcast_to(value, (SIDE,) + value.shape)
    return lax.all_to_all(sent, ROWS, 0, 0, axis_index_groups=groups)


def next_layer(value):
    pairs = [(i, (i + 1) % LAYERS) for i in range(LAYERS)]
    pairs += [(LAYERS + i, LAYERS + (i - 1) % LAYERS) for i in range(LAYERS)]
    return lax.ppermute(value, ("core", "z"), pairs)


def exchange(tiles, axes):
    return lax.all_to_all(tiles, axes, 0, 0)


def pack_kernel(place, source, out, sems):
    rows = pl.ds(pl.multiple_of(place[3] * HALF, HALF), HALF)
    copies = [
        pltpu.make_async_copy(source.at[rows, pl.ds(i * 2 * ROW_BLOCK, 2 * ROW_BLOCK)], out.at[i], sems.at[i])
        for i in range(COUNT)
    ]
    for copy in copies:
        copy.start()
    for copy in copies:
        copy.wait()


def pack(place, activations):
    return pl.pallas_call(
        pack_kernel,
        out_shape=pltpu.VMEM((COUNT, HALF, 2 * ROW_BLOCK), jnp.bfloat16),
        in_specs=[SCALARS, ANYWHERE],
        out_specs=WHOLE,
        scratch_shapes=[pltpu.SemaphoreType.DMA((COUNT,))],
        compiler_params=PARAMS,
        cost_estimate=cost(0, 2**21),
    )(place, pltpu.with_memory_space_constraint(activations, pltpu.HBM))


def turn_kernel(place, part, out):
    y, x, core = place[0], place[1], place[2]

    def block(i):
        j, k = i // SIDE, i % SIDE
        return part[jnp.where(core == 1, ((y - j) & (SIDE - 1)) * SIDE + k, k * SIDE + ((x - j) & (SIDE - 1)))]

    for i in range(0, COUNT, 2):
        out[:, i * HALF : (i + 2) * HALF] = jnp.concatenate([block(i), block(i + 1)], axis=0).T


def turn(place, part):
    return pl.pallas_call(
        turn_kernel,
        out_shape=shape(2 * ROW_BLOCK, COUNT * HALF, dtype=jnp.bfloat16),
        in_specs=[SCALARS, WHOLE],
        out_specs=WHOLE,
        compiler_params=PARAMS,
        cost_estimate=cost(0, 2**21),
    )(place, part)


def product_kernel(parts, which, place, first, second, *refs):
    operands, out = refs[:-1], refs[-1]
    total = operands[-1] if len(operands) > 1 + max(index for *_, blocks in parts for index, _ in blocks) else None
    start = place[3] * HALF
    rows = pl.ds(0 if which is None else pl.multiple_of(which(place[2]) * ROW_BLOCK, ROW_BLOCK), out.shape[0])

    for n in range(WIDTH // COLUMNS):
        columns = slice(n * COLUMNS, (n + 1) * COLUMNS)
        value = None if total is None else total[rows, columns]
        for group, exchanged, blocks in parts:
            depth = slice(group * SIDE * HALF, group * SIDE * HALF + len(blocks) * HALF)
            features, offset = (first, start) if exchanged else (second, HALF - start)
            offset = pl.multiple_of(offset, HALF)
            grads = [operands[index][pl.ds(i * TOKENS + offset, HALF), columns] for index, i in blocks]
            term = jnp.dot(features[rows, depth], jnp.concatenate(grads, axis=0), preferred_element_type=jnp.float32)
            value = term if value is None else value + term
        out[:, columns] = value


def product(place, features, operands, parts, total=None, which=None):
    count = 2 * ROW_BLOCK if which is None else ROW_BLOCK
    operands = [*features, *operands] + ([] if total is None else [total])
    return pl.pallas_call(
        functools.partial(product_kernel, parts, which),
        out_shape=shape(count, WIDTH),
        in_specs=[SCALARS] + [WHOLE] * len(operands),
        out_specs=WHOLE,
        input_output_aliases={len(operands): 0} if total is not None and which is None else {},
        compiler_params=PARAMS,
        cost_estimate=cost(24 * count * HALF * WIDTH * sum(len(part[2]) for part in parts), 2**20),
    )(place, *operands)


def columns_kernel(mine, theirs, grad, sent):
    value = mine[...] + theirs[...]
    grad[...] = value
    sums = jnp.sum(value * value, axis=0, keepdims=True)
    tile = jnp.concatenate([sums[:, i * LANES : (i + 1) * LANES] for i in range(8)], axis=0)
    for i in range(DEVICES):
        sent[i] = tile


def columns(mine, theirs):
    return pl.pallas_call(
        columns_kernel,
        out_shape=(shape(ROW_BLOCK, WIDTH), shape(DEVICES, *TILE)),
        in_specs=[WHOLE] * 2,
        out_specs=(WHOLE, WHOLE),
        compiler_params=PARAMS,
        cost_estimate=cost(2**20, 3 * 2**20),
    )(mine, theirs)


def rows_kernel(received, moment, grad, weight, cols, col_root, sent):
    new = BETA_TWO * moment[...] + (1.0 - BETA_TWO) * (jnp.sum(received[...], axis=0) / D)
    cols[...] = new
    root = lax.rsqrt(new)
    col_root[...] = root
    sums = [jnp.zeros((ROW_BLOCK, LANES), jnp.float32)] * 4
    for i in range(WIDTH // LANES):
        lanes = slice(i * LANES, (i + 1) * LANES)
        value, held = grad[:, lanes], weight[:, lanes]
        by_cols = value * root[i : i + 1, :]
        terms = (value * value, by_cols * by_cols, by_cols * held, held * held)
        sums = [a + b for a, b in zip(sums, terms)]
    parts = []
    for value in sums:
        for row in range(0, ROW_BLOCK, LANES):
            parts.append(jnp.sum(value[row : row + LANES, :].T, axis=0, keepdims=True))
    tile = jnp.concatenate(parts, axis=0)
    for i in range(LAYERS):
        sent[i] = tile


def rows(received, moment, grad, weight):
    return pl.pallas_call(
        rows_kernel,
        out_shape=(shape(*TILE), shape(*TILE), shape(LAYERS, *TILE)),
        in_specs=[WHOLE] * 4,
        out_specs=(WHOLE, WHOLE, WHOLE),
        compiler_params=PARAMS,
        cost_estimate=cost(2**21, 2**21),
    )(received, moment, grad, weight)


def scalars_kernel(received, moment, rows_out, row_root, sent):
    parts = jnp.sum(received[...], axis=0)
    new = BETA_TWO * moment[...] + (1.0 - BETA_TWO) * (parts[0:2] / FF)
    rows_out[...] = new
    root = lax.rsqrt(new)
    row_root[...] = root
    sums = [jnp.sum(part, axis=0, keepdims=True) for part in (parts[2:4] * root * root, parts[4:6] * root, parts[6:8])]
    tile = jnp.concatenate(sums + [jnp.zeros_like(sums[0])], axis=0)
    for i in range(DEVICES):
        sent[i] = tile


def scalars(received, moment):
    return pl.pallas_call(
        scalars_kernel,
        out_shape=(shape(2, LANES), shape(2, LANES), shape(DEVICES, 4, LANES)),
        in_specs=[WHOLE] * 2,
        out_specs=(WHOLE, WHOLE, WHOLE),
        compiler_params=PARAMS,
        cost_estimate=cost(2**14, 2**18),
    )(received, moment)


def update_kernel(received, row_root, col_root, grad, weight, out, done, sems):
    parts = jnp.sum(received[...], axis=0)
    scaled_sum, cross_sum, weight_sum = (jnp.sum(parts[i : i + 1], keepdims=True) for i in range(3))
    factor = 1.0 / jnp.maximum(1.0, jnp.sqrt(scaled_sum / (D * FF)) / CLIP_LEVEL)
    direction_sum = (
        factor * factor * scaled_sum + 2.0 * WEIGHT_DECAY * factor * cross_sum + WEIGHT_DECAY * WEIGHT_DECAY * weight_sum
    )
    trust_ratio = jnp.sqrt(weight_sum / (jnp.maximum(direction_sum, 0.0) + EPSILON))
    by_row = row_root[...] * (trust_ratio * factor)
    by_col = col_root[...]
    decay = trust_ratio * WEIGHT_DECAY
    copies = []
    for half in range(2):
        scales = jnp.broadcast_to(by_row[half : half + 1, :], (LANES, LANES)).T
        for part in range(2):
            scale = scales[part * HALF : (part + 1) * HALF]
            here = slice(half * LANES + part * HALF, half * LANES + (part + 1) * HALF)
            for i in range(WIDTH // LANES):
                lanes = slice(i * LANES, (i + 1) * LANES)
                done[here, lanes] = grad[here, lanes] * by_col[i : i + 1, :] * scale + decay * weight[here, lanes]
            copies.append(pltpu.make_async_copy(done.at[here], out.at[here], sems.at[len(copies)]))
            copies[-1].start()
    for copy in copies:
        copy.wait()


def update(received, row_root, col_root, grad, weight):
    return pl.pallas_call(
        update_kernel,
        out_shape=shape(ROW_BLOCK, WIDTH),
        in_specs=[WHOLE] * 5,
        out_specs=ANYWHERE,
        scratch_shapes=[pltpu.VMEM((ROW_BLOCK, WIDTH), jnp.float32), pltpu.SemaphoreType.DMA((4,))],
        compiler_params=PARAMS,
        cost_estimate=cost(2**20, 3 * 2**20),
    )(received, row_root, col_root, grad, weight)


def shards(activations, out_grads, weight, row_moment, col_moment):
    y, x, core, layer = (lax.axis_index(name) for name in ("y", "x", "core", "z"))
    place = jnp.stack([y, x, core, layer & 1])
    line = gather_line(out_grads)
    packed, line = lax.optimization_barrier((pack(place, activations), line))
    first = turn(place, exchange(packed, CHIPS))
    second = next_layer(first)
    low, high = (line[i : i + 2].reshape(2 * TOKENS, WIDTH) for i in (0, 2))
    back_low, ahead_high = along(low, 1), along(high, SIDE - 1)
    far = [along(back_low, 1), along(ahead_high, SIDE - 1)]
    back, ahead = [back_low, along(high, 1)], [along(low, SIDE - 1), ahead_high]
    blocks = lambda operand: [(operand, 0), (operand, 1), (operand + 1, 0), (operand + 1, 1)]
    total = product(place, (first, first), [low, high], [(0, True, blocks(0))])
    parts = [(1, True, blocks(0)), (3, True, blocks(2))]
    total = product(place, (first, first), back + ahead, parts, total)
    operands = [low, high] + back + far + ahead
    parts = [(2, True, blocks(4)), (0, False, blocks(0) + blocks(2) + blocks(4) + blocks(6))]
    theirs = product(place, (first, second), operands, parts, total, lambda core: 1 - core)
    received = lax.ppermute(theirs, "core", [(0, 1), (1, 0)])
    mine = product(place, (first, second), operands, parts, total, lambda core: core)
    weight_grad, tiles = columns(mine, received)
    new_cols, col_root, tiles = rows(exchange(tiles, ROWS), col_moment.reshape(TILE), weight_grad, weight)
    new_rows, row_root, tiles = scalars(exchange(tiles, "z"), row_moment.reshape(2, LANES))
    out = update(exchange(tiles, ROWS), row_root, col_root, weight_grad, weight)
    return (out, new_rows.reshape(-1), new_cols.reshape(-1))


def solution(mesh):
    mesh = Mesh(mesh.devices.reshape(SIDE, SIDE, 2, LAYERS), ("y", "x", "core", "z"))
    placed = (P(ROWS, None), P(ROWS, "z"), P(ROWS, "z"), P(ROWS), P("z"))
    return jax.shard_map(
        shards,
        mesh=mesh,
        in_specs=placed,
        out_specs=(P(ROWS, "z"), P(ROWS), P("z")),
        check_vma=False,
    )
```

```python
import functools

import jax
import jax.numpy as jnp
from jax import lax
from jax.experimental import pallas as pl
from jax.experimental.pallas import tpu as pltpu
from jax.sharding import Mesh, PartitionSpec as P

D = 8192
FF = 16384


BETA_TWO = 0.8
CLIP_LEVEL = 0.25
WEIGHT_DECAY = 0.1
EPSILON = 1e-06

CHIPS = ("y", "x")
ROWS = ("y", "x", "core")
SIDE = 4
COUNT = SIDE * SIDE
LAYERS = 16
DEVICES = 2 * COUNT
TOKENS = 128
HALF = TOKENS // 2
ROW_BLOCK = 256
WIDTH = 1024
LANES = 128
COLUMNS = 512
TILE = (8, LANES)

ANYWHERE = pl.BlockSpec(memory_space=pl.ANY)
WHOLE = pl.BlockSpec(memory_space=pltpu.VMEM)
SCALARS = pl.BlockSpec(memory_space=pltpu.SMEM)
PARAMS = pltpu.CompilerParams(vmem_limit_bytes=16 * 2**20)


def shape(*dims, dtype=jnp.float32):
    return jax.ShapeDtypeStruct(dims, dtype)


def cost(flops, bytes_accessed):
    return pl.CostEstimate(flops=flops, bytes_accessed=bytes_accessed, transcendentals=0)


def device(y, x, core):
    return ((y % SIDE) * SIDE + x % SIDE) * 2 + core


def along(value, step):
    pairs = []
    for y in range(SIDE):
        for x in range(SIDE):
            pairs.append((device(y, x, 0), device(y, x + step, 0)))
            pairs.append((device(y, x, 1), device(y + step, x, 1)))
    return lax.ppermute(value, ROWS, pairs)


def gather_line(value):
    groups = [[device(y, x, 0) for y in range(SIDE)] for x in range(SIDE)]
    groups += [[device(y, x, 1) for x in range(SIDE)] for y in range(SIDE)]
    sent = jnp.broadcast_to(value, (SIDE,) + value.shape)
    return lax.all_to_all(sent, ROWS, 0, 0, axis_index_groups=groups)


def next_layer(value):
    pairs = [(i, (i + 1) % LAYERS) for i in range(LAYERS)]
    pairs += [(LAYERS + i, LAYERS + (i - 1) % LAYERS) for i in range(LAYERS)]
    return lax.ppermute(value, ("core", "z"), pairs)


def exchange(tiles, axes):
    return lax.all_to_all(tiles, axes, 0, 0)


def pack_kernel(place, source, out, sems):
    rows = pl.ds(pl.multiple_of(place[3] * HALF, HALF), HALF)
    copies = [
        pltpu.make_async_copy(source.at[rows, pl.ds(i * 2 * ROW_BLOCK, 2 * ROW_BLOCK)], out.at[i], sems.at[i])
        for i in range(COUNT)
    ]
    for copy in copies:
        copy.start()
    for copy in copies:
        copy.wait()


def pack(place, activations):
    return pl.pallas_call(
        pack_kernel,
        out_shape=pltpu.VMEM((COUNT, HALF, 2 * ROW_BLOCK), jnp.bfloat16),
        in_specs=[SCALARS, ANYWHERE],
        out_specs=WHOLE,
        scratch_shapes=[pltpu.SemaphoreType.DMA((COUNT,))],
        compiler_params=PARAMS,
        cost_estimate=cost(0, 2**21),
    )(place, pltpu.with_memory_space_constraint(activations, pltpu.HBM))


def turn_kernel(place, part, out):
    y, x, core = place[0], place[1], place[2]

    def block(i):
        j, k = i // SIDE, i % SIDE
        return part[jnp.where(core == 1, ((y - j) & (SIDE - 1)) * SIDE + k, k * SIDE + ((x - j) & (SIDE - 1)))]

    for i in range(0, COUNT, 2):
        out[:, i * HALF : (i + 2) * HALF] = jnp.concatenate([block(i), block(i + 1)], axis=0).T


def turn(place, part):
    return pl.pallas_call(
        turn_kernel,
        out_shape=shape(2 * ROW_BLOCK, COUNT * HALF, dtype=jnp.bfloat16),
        in_specs=[SCALARS, WHOLE],
        out_specs=WHOLE,
        compiler_params=PARAMS,
        cost_estimate=cost(0, 2**21),
    )(place, part)


def product_kernel(parts, which, place, first, second, *refs):
    operands, out = refs[:-1], refs[-1]
    total = operands[-1] if len(operands) > 1 + max(index for *_, blocks in parts for index, _ in blocks) else None
    start = place[3] * HALF
    rows = pl.ds(0 if which is None else pl.multiple_of(which(place[2]) * ROW_BLOCK, ROW_BLOCK), out.shape[0])

    for n in range(WIDTH // COLUMNS):
        columns = slice(n * COLUMNS, (n + 1) * COLUMNS)
        value = None if total is None else total[rows, columns]
        for group, exchanged, blocks in parts:
            depth = slice(group * SIDE * HALF, group * SIDE * HALF + len(blocks) * HALF)
            features, offset = (first, start) if exchanged else (second, HALF - start)
            offset = pl.multiple_of(offset, HALF)
            grads = [operands[index][pl.ds(i * TOKENS + offset, HALF), columns] for index, i in blocks]
            term = jnp.dot(features[rows, depth], jnp.concatenate(grads, axis=0), preferred_element_type=jnp.float32)
            value = term if value is None else value + term
        out[:, columns] = value


def product(place, features, operands, parts, total=None, which=None):
    count = 2 * ROW_BLOCK if which is None else ROW_BLOCK
    operands = [*features, *operands] + ([] if total is None else [total])
    return pl.pallas_call(
        functools.partial(product_kernel, parts, which),
        out_shape=shape(count, WIDTH),
        in_specs=[SCALARS] + [WHOLE] * len(operands),
        out_specs=WHOLE,
        input_output_aliases={len(operands): 0} if total is not None and which is None else {},
        compiler_params=PARAMS,
        cost_estimate=cost(24 * count * HALF * WIDTH * sum(len(part[2]) for part in parts), 2**20),
    )(place, *operands)


def columns_kernel(mine, theirs, grad, sent):
    value = mine[...] + theirs[...]
    grad[...] = value
    sums = jnp.sum(value * value, axis=0, keepdims=True)
    tile = jnp.concatenate([sums[:, i * LANES : (i + 1) * LANES] for i in range(8)], axis=0)
    for i in range(DEVICES):
        sent[i] = tile


def columns(mine, theirs):
    return pl.pallas_call(
        columns_kernel,
        out_shape=(shape(ROW_BLOCK, WIDTH), shape(DEVICES, *TILE)),
        in_specs=[WHOLE] * 2,
        out_specs=(WHOLE, WHOLE),
        compiler_params=PARAMS,
        cost_estimate=cost(2**20, 3 * 2**20),
    )(mine, theirs)


def rows_kernel(received, moment, grad, weight, cols, col_root, sent):
    new = BETA_TWO * moment[...] + (1.0 - BETA_TWO) * (jnp.sum(received[...], axis=0) / D)
    cols[...] = new
    root = lax.rsqrt(new)
    col_root[...] = root
    sums = [jnp.zeros((ROW_BLOCK, LANES), jnp.float32)] * 4
    for i in range(WIDTH // LANES):
        lanes = slice(i * LANES, (i + 1) * LANES)
        value, held = grad[:, lanes], weight[:, lanes]
        by_cols = value * root[i : i + 1, :]
        terms = (value * value, by_cols * by_cols, by_cols * held, held * held)
        sums = [a + b for a, b in zip(sums, terms)]
    parts = []
    for value in sums:
        for row in range(0, ROW_BLOCK, LANES):
            parts.append(jnp.sum(value[row : row + LANES, :].T, axis=0, keepdims=True))
    tile = jnp.concatenate(parts, axis=0)
    for i in range(LAYERS):
        sent[i] = tile


def rows(received, moment, grad, weight):
    return pl.pallas_call(
        rows_kernel,
        out_shape=(shape(*TILE), shape(*TILE), shape(LAYERS, *TILE)),
        in_specs=[WHOLE] * 4,
        out_specs=(WHOLE, WHOLE, WHOLE),
        compiler_params=PARAMS,
        cost_estimate=cost(2**21, 2**21),
    )(received, moment, grad, weight)


def scalars_kernel(received, moment, rows_out, row_root, sent):
    parts = jnp.sum(received[...], axis=0)
    new = BETA_TWO * moment[...] + (1.0 - BETA_TWO) * (parts[0:2] / FF)
    rows_out[...] = new
    root = lax.rsqrt(new)
    row_root[...] = root
    sums = [jnp.sum(part, axis=0, keepdims=True) for part in (parts[2:4] * root * root, parts[4:6] * root, parts[6:8])]
    tile = jnp.concatenate(sums + [jnp.zeros_like(sums[0])], axis=0)
    for i in range(DEVICES):
        sent[i] = tile


def scalars(received, moment):
    return pl.pallas_call(
        scalars_kernel,
        out_shape=(shape(2, LANES), shape(2, LANES), shape(DEVICES, 4, LANES)),
        in_specs=[WHOLE] * 2,
        out_specs=(WHOLE, WHOLE, WHOLE),
        compiler_params=PARAMS,
        cost_estimate=cost(2**14, 2**18),
    )(received, moment)


def update_kernel(received, row_root, col_root, grad, weight, out, done, sems):
    parts = jnp.sum(received[...], axis=0)
    scaled_sum, cross_sum, weight_sum = (jnp.sum(parts[i : i + 1], keepdims=True) for i in range(3))
    factor = 1.0 / jnp.maximum(1.0, jnp.sqrt(scaled_sum / (D * FF)) / CLIP_LEVEL)
    direction_sum = (
        factor * factor * scaled_sum + 2.0 * WEIGHT_DECAY * factor * cross_sum + WEIGHT_DECAY * WEIGHT_DECAY * weight_sum
    )
    trust_ratio = jnp.sqrt(weight_sum / (jnp.maximum(direction_sum, 0.0) + EPSILON))
    by_row = row_root[...] * (trust_ratio * factor)
    by_col = col_root[...]
    decay = trust_ratio * WEIGHT_DECAY
    copies = []
    for half in range(2):
        scales = jnp.broadcast_to(by_row[half : half + 1, :], (LANES, LANES)).T
        for part in range(2):
            scale = scales[part * HALF : (part + 1) * HALF]
            here = slice(half * LANES + part * HALF, half * LANES + (part + 1) * HALF)
            for i in range(WIDTH // LANES):
                lanes = slice(i * LANES, (i + 1) * LANES)
                done[here, lanes] = grad[here, lanes] * by_col[i : i + 1, :] * scale + decay * weight[here, lanes]
            copies.append(pltpu.make_async_copy(done.at[here], out.at[here], sems.at[len(copies)]))
            copies[-1].start()
    for copy in copies:
        copy.wait()


def update(received, row_root, col_root, grad, weight):
    return pl.pallas_call(
        update_kernel,
        out_shape=shape(ROW_BLOCK, WIDTH),
        in_specs=[WHOLE] * 5,
        out_specs=ANYWHERE,
        scratch_shapes=[pltpu.VMEM((ROW_BLOCK, WIDTH), jnp.float32), pltpu.SemaphoreType.DMA((4,))],
        compiler_params=PARAMS,
        cost_estimate=cost(2**20, 3 * 2**20),
    )(received, row_root, col_root, grad, weight)


def shards(activations, out_grads, weight, row_moment, col_moment):
    y, x, core, layer = (lax.axis_index(name) for name in ("y", "x", "core", "z"))
    place = jnp.stack([y, x, core, layer & 1])
    line = gather_line(out_grads)
    packed, line = lax.optimization_barrier((pack(place, activations), line))
    first = exchange(packed, CHIPS)
    first, second = turn(place, first), turn(place, next_layer(first))
    low, high = (line[i : i + 2].reshape(2 * TOKENS, WIDTH) for i in (0, 2))
    back_low, ahead_high = along(low, 1), along(high, SIDE - 1)
    far = [along(back_low, 1), along(ahead_high, SIDE - 1)]
    back, ahead = [back_low, along(high, 1)], [along(low, SIDE - 1), ahead_high]
    blocks = lambda operand: [(operand, 0), (operand, 1), (operand + 1, 0), (operand + 1, 1)]
    total = product(place, (first, first), [low, high], [(0, True, blocks(0))])
    parts = [(1, True, blocks(0)), (3, True, blocks(2))]
    total = product(place, (first, first), back + ahead, parts, total)
    operands = [low, high] + back + far + ahead
    parts = [(2, True, blocks(4)), (0, False, blocks(0) + blocks(2) + blocks(4) + blocks(6))]
    theirs = product(place, (first, second), operands, parts, total, lambda core: 1 - core)
    received = lax.ppermute(theirs, "core", [(0, 1), (1, 0)])
    mine = product(place, (first, second), operands, parts, total, lambda core: core)
    weight_grad, tiles = columns(mine, received)
    new_cols, col_root, tiles = rows(exchange(tiles, ROWS), col_moment.reshape(TILE), weight_grad, weight)
    new_rows, row_root, tiles = scalars(exchange(tiles, "z"), row_moment.reshape(2, LANES))
    out = update(exchange(tiles, ROWS), row_root, col_root, weight_grad, weight)
    return (out, new_rows.reshape(-1), new_cols.reshape(-1))


def solution(mesh):
    mesh = Mesh(mesh.devices.reshape(SIDE, SIDE, 2, LAYERS), ("y", "x", "core", "z"))
    placed = (P(ROWS, None), P(ROWS, "z"), P(ROWS, "z"), P(ROWS), P("z"))
    return jax.shard_map(
        shards,
        mesh=mesh,
        in_specs=placed,
        out_specs=(P(ROWS, "z"), P(ROWS), P("z")),
        check_vma=False,
    )
```

```python
import functools

import jax
import jax.numpy as jnp
from jax import lax
from jax.experimental import pallas as pl
from jax.experimental.pallas import tpu as pltpu
from jax.sharding import Mesh, PartitionSpec as P

D = 8192
FF = 16384


BETA_TWO = 0.8
CLIP_LEVEL = 0.25
WEIGHT_DECAY = 0.1
EPSILON = 1e-06

CHIPS = ("y", "x")
ROWS = ("y", "x", "core")
SIDE = 4
COUNT = SIDE * SIDE
LAYERS = 16
DEVICES = 2 * COUNT
TOKENS = 128
HALF = TOKENS // 2
ROW_BLOCK = 256
WIDTH = 1024
LANES = 128
GROUPS = (0, 2, 1, 3)
COLUMNS = 512
TILE = (8, LANES)

ANYWHERE = pl.BlockSpec(memory_space=pl.ANY)
WHOLE = pl.BlockSpec(memory_space=pltpu.VMEM)
SCALARS = pl.BlockSpec(memory_space=pltpu.SMEM)
PARAMS = pltpu.CompilerParams(vmem_limit_bytes=16 * 2**20)


def shape(*dims, dtype=jnp.float32):
    return jax.ShapeDtypeStruct(dims, dtype)


def cost(flops, bytes_accessed):
    return pl.CostEstimate(flops=flops, bytes_accessed=bytes_accessed, transcendentals=0)


def device(y, x, core):
    return ((y % SIDE) * SIDE + x % SIDE) * 2 + core


def along(value, step):
    pairs = []
    for y in range(SIDE):
        for x in range(SIDE):
            pairs.append((device(y, x, 0), device(y, x + step, 0)))
            pairs.append((device(y, x, 1), device(y + step, x, 1)))
    return lax.ppermute(value, ROWS, pairs)


def gather_line(value):
    groups = [[device(y, x, 0) for y in range(SIDE)] for x in range(SIDE)]
    groups += [[device(y, x, 1) for x in range(SIDE)] for y in range(SIDE)]
    sent = jnp.broadcast_to(value, (SIDE,) + value.shape)
    return lax.all_to_all(sent, ROWS, 0, 0, axis_index_groups=groups)


def next_layer(value):
    pairs = [(i, (i + 1) % LAYERS) for i in range(LAYERS)]
    pairs += [(LAYERS + i, LAYERS + (i - 1) % LAYERS) for i in range(LAYERS)]
    return lax.ppermute(value, ("core", "z"), pairs)


def exchange(tiles, axes):
    return lax.all_to_all(tiles, axes, 0, 0)


def pack_kernel(place, source, out, sems):
    rows = pl.ds(pl.multiple_of(place[3] * HALF, HALF), HALF)
    copies = [
        pltpu.make_async_copy(source.at[rows, pl.ds(i * 2 * ROW_BLOCK, 2 * ROW_BLOCK)], out.at[i], sems.at[i])
        for i in range(COUNT)
    ]
    for copy in copies:
        copy.start()
    for copy in copies:
        copy.wait()


def pack(place, activations):
    return pl.pallas_call(
        pack_kernel,
        out_shape=pltpu.VMEM((COUNT, HALF, 2 * ROW_BLOCK), jnp.bfloat16),
        in_specs=[SCALARS, ANYWHERE],
        out_specs=WHOLE,
        scratch_shapes=[pltpu.SemaphoreType.DMA((COUNT,))],
        compiler_params=PARAMS,
        cost_estimate=cost(0, 2**21),
    )(place, pltpu.with_memory_space_constraint(activations, pltpu.HBM))


def turn_kernel(place, part, out):
    y, x, core = place[0], place[1], place[2]

    def block(i):
        j, k = GROUPS[i // SIDE], i % SIDE
        return part[jnp.where(core == 1, ((y - j) & (SIDE - 1)) * SIDE + k, k * SIDE + ((x - j) & (SIDE - 1)))]

    for i in range(0, COUNT, 2):
        out[:, i * HALF : (i + 2) * HALF] = jnp.concatenate([block(i), block(i + 1)], axis=0).T


def turn(place, part):
    return pl.pallas_call(
        turn_kernel,
        out_shape=shape(2 * ROW_BLOCK, COUNT * HALF, dtype=jnp.bfloat16),
        in_specs=[SCALARS, WHOLE],
        out_specs=WHOLE,
        compiler_params=PARAMS,
        cost_estimate=cost(0, 2**21),
    )(place, part)


def product_kernel(parts, which, late, place, first, second, *refs):
    if late:
        refs, held, sems = refs[:-2], refs[-2], refs[-1]
    operands, out = list(refs[:-1]), refs[-1]
    total = operands[-1] if len(operands) > 1 + max(index for *_, blocks in parts for index, _ in blocks) else None
    copies = []
    for i, index in enumerate(late):
        copies.append(pltpu.make_async_copy(operands[index], held.at[i], sems.at[i]))
        copies[-1].start()
        operands[index] = held.at[i]
    start = place[3] * HALF
    rows = pl.ds(0 if which is None else pl.multiple_of(which(place[2]) * ROW_BLOCK, ROW_BLOCK), out.shape[0])

    def add(parts, columns, value):
        for group, exchanged, blocks in parts:
            depth = slice(group * SIDE * HALF, group * SIDE * HALF + len(blocks) * HALF)
            features, offset = (first, start) if exchanged else (second, HALF - start)
            offset = pl.multiple_of(offset, HALF)
            grads = [operands[index][pl.ds(i * TOKENS + offset, HALF), columns] for index, i in blocks]
            term = jnp.dot(features[rows, depth], jnp.concatenate(grads, axis=0), preferred_element_type=jnp.float32)
            value = term if value is None else value + term
        return value

    waits = lambda part: any(index in late for index, _ in part[2])
    tiles = [slice(n * COLUMNS, (n + 1) * COLUMNS) for n in range(WIDTH // COLUMNS)]
    for columns in tiles:
        held_total = None if total is None else total[rows, columns]
        out[:, columns] = add([part for part in parts if not waits(part)], columns, held_total)
    if late:
        for copy in copies:
            copy.wait()
        for columns in tiles:
            out[:, columns] = add([part for part in parts if waits(part)], columns, out[:, columns])


def product(place, features, operands, parts, total=None, which=None, late=()):
    count = 2 * ROW_BLOCK if which is None else ROW_BLOCK
    specs = [WHOLE] * 2 + [ANYWHERE if i in late else WHOLE for i in range(len(operands))]
    scratch = []
    if late:
        scratch = [pltpu.VMEM((len(late), 2 * TOKENS, WIDTH), jnp.bfloat16), pltpu.SemaphoreType.DMA((len(late),))]
    if total is not None:
        operands, specs = operands + [total], specs + [WHOLE]
    return pl.pallas_call(
        functools.partial(product_kernel, parts, which, late),
        out_shape=shape(count, WIDTH),
        in_specs=[SCALARS] + specs,
        out_specs=WHOLE,
        scratch_shapes=scratch,
        input_output_aliases={2 + len(operands): 0} if total is not None and which is None else {},
        compiler_params=PARAMS,
        cost_estimate=cost(24 * count * HALF * WIDTH * sum(len(part[2]) for part in parts), 2**20),
    )(place, *features, *operands)


def columns_kernel(mine, theirs, grad, sent):
    value = mine[...] + theirs[...]
    grad[...] = value
    sums = jnp.sum(value * value, axis=0, keepdims=True)
    tile = jnp.concatenate([sums[:, i * LANES : (i + 1) * LANES] for i in range(8)], axis=0)
    for i in range(DEVICES):
        sent[i] = tile


def columns(mine, theirs):
    return pl.pallas_call(
        columns_kernel,
        out_shape=(shape(ROW_BLOCK, WIDTH), shape(DEVICES, *TILE)),
        in_specs=[WHOLE] * 2,
        out_specs=(WHOLE, WHOLE),
        compiler_params=PARAMS,
        cost_estimate=cost(2**20, 3 * 2**20),
    )(mine, theirs)


def rows_kernel(received, moment, grad, weight, cols, col_root, sent):
    new = BETA_TWO * moment[...] + (1.0 - BETA_TWO) * (jnp.sum(received[...], axis=0) / D)
    cols[...] = new
    root = lax.rsqrt(new)
    col_root[...] = root
    sums = [jnp.zeros((ROW_BLOCK, LANES), jnp.float32)] * 4
    for i in range(WIDTH // LANES):
        lanes = slice(i * LANES, (i + 1) * LANES)
        value, held = grad[:, lanes], weight[:, lanes]
        by_cols = value * root[i : i + 1, :]
        terms = (value * value, by_cols * by_cols, by_cols * held, held * held)
        sums = [a + b for a, b in zip(sums, terms)]
    parts = []
    for value in sums:
        for row in range(0, ROW_BLOCK, LANES):
            parts.append(jnp.sum(value[row : row + LANES, :].T, axis=0, keepdims=True))
    tile = jnp.concatenate(parts, axis=0)
    for i in range(LAYERS):
        sent[i] = tile


def rows(received, moment, grad, weight):
    return pl.pallas_call(
        rows_kernel,
        out_shape=(shape(*TILE), shape(*TILE), shape(LAYERS, *TILE)),
        in_specs=[WHOLE] * 4,
        out_specs=(WHOLE, WHOLE, WHOLE),
        compiler_params=PARAMS,
        cost_estimate=cost(2**21, 2**21),
    )(received, moment, grad, weight)


def scalars_kernel(received, moment, rows_out, row_root, sent):
    parts = jnp.sum(received[...], axis=0)
    new = BETA_TWO * moment[...] + (1.0 - BETA_TWO) * (parts[0:2] / FF)
    rows_out[...] = new
    root = lax.rsqrt(new)
    row_root[...] = root
    sums = [jnp.sum(part, axis=0, keepdims=True) for part in (parts[2:4] * root * root, parts[4:6] * root, parts[6:8])]
    tile = jnp.concatenate(sums + [jnp.zeros_like(sums[0])], axis=0)
    for i in range(DEVICES):
        sent[i] = tile


def scalars(received, moment):
    return pl.pallas_call(
        scalars_kernel,
        out_shape=(shape(2, LANES), shape(2, LANES), shape(DEVICES, 4, LANES)),
        in_specs=[WHOLE] * 2,
        out_specs=(WHOLE, WHOLE, WHOLE),
        compiler_params=PARAMS,
        cost_estimate=cost(2**14, 2**18),
    )(received, moment)


def update_kernel(received, row_root, col_root, grad, weight, out, done, sems):
    parts = jnp.sum(received[...], axis=0)
    scaled_sum, cross_sum, weight_sum = (jnp.sum(parts[i : i + 1], keepdims=True) for i in range(3))
    factor = 1.0 / jnp.maximum(1.0, jnp.sqrt(scaled_sum / (D * FF)) / CLIP_LEVEL)
    direction_sum = (
        factor * factor * scaled_sum + 2.0 * WEIGHT_DECAY * factor * cross_sum + WEIGHT_DECAY * WEIGHT_DECAY * weight_sum
    )
    trust_ratio = jnp.sqrt(weight_sum / (jnp.maximum(direction_sum, 0.0) + EPSILON))
    by_row = row_root[...] * (trust_ratio * factor)
    by_col = col_root[...]
    decay = trust_ratio * WEIGHT_DECAY
    copies = []
    for half in range(2):
        scales = jnp.broadcast_to(by_row[half : half + 1, :], (LANES, LANES)).T
        for part in range(2):
            scale = scales[part * HALF : (part + 1) * HALF]
            here = slice(half * LANES + part * HALF, half * LANES + (part + 1) * HALF)
            for i in range(WIDTH // LANES):
                lanes = slice(i * LANES, (i + 1) * LANES)
                done[here, lanes] = grad[here, lanes] * by_col[i : i + 1, :] * scale + decay * weight[here, lanes]
            copies.append(pltpu.make_async_copy(done.at[here], out.at[here], sems.at[len(copies)]))
            copies[-1].start()
    for copy in copies:
        copy.wait()


def update(received, row_root, col_root, grad, weight):
    return pl.pallas_call(
        update_kernel,
        out_shape=shape(ROW_BLOCK, WIDTH),
        in_specs=[WHOLE] * 5,
        out_specs=ANYWHERE,
        scratch_shapes=[pltpu.VMEM((ROW_BLOCK, WIDTH), jnp.float32), pltpu.SemaphoreType.DMA((4,))],
        compiler_params=PARAMS,
        cost_estimate=cost(2**20, 3 * 2**20),
    )(received, row_root, col_root, grad, weight)


def shards(activations, out_grads, weight, row_moment, col_moment):
    y, x, core, layer = (lax.axis_index(name) for name in ("y", "x", "core", "z"))
    place = jnp.stack([y, x, core, layer & 1])
    line = gather_line(out_grads)
    packed, line = lax.optimization_barrier((pack(place, activations), line))
    first = exchange(packed, CHIPS)
    first, second = turn(place, first), turn(place, next_layer(first))
    low, high = (line[i : i + 2].reshape(2 * TOKENS, WIDTH) for i in (0, 2))
    back_low, ahead_high = along(low, 1), along(high, SIDE - 1)
    far = [along(back_low, 1), along(ahead_high, SIDE - 1)]
    back, ahead = [back_low, along(high, 1)], [along(low, SIDE - 1), ahead_high]
    blocks = lambda operand: [(operand, 0), (operand, 1), (operand + 1, 0), (operand + 1, 1)]
    total = product(place, (first, first), [low, high], [(0, True, blocks(0))])
    total = product(place, (first, first), back + ahead, [(2, True, blocks(0) + blocks(2))], total)
    operands = [low, high] + far + back + ahead
    parts = [(1, True, blocks(2)), (0, False, blocks(0) + blocks(2)), (2, False, blocks(4) + blocks(6))]
    theirs = product(place, (first, second), operands, parts, total, lambda core: 1 - core, (5, 6))
    received = lax.ppermute(theirs, "core", [(0, 1), (1, 0)])
    mine = product(place, (first, second), operands, parts, total, lambda core: core, (5, 6))
    weight_grad, tiles = columns(mine, received)
    new_cols, col_root, tiles = rows(exchange(tiles, ROWS), col_moment.reshape(TILE), weight_grad, weight)
    new_rows, row_root, tiles = scalars(exchange(tiles, "z"), row_moment.reshape(2, LANES))
    out = update(exchange(tiles, ROWS), row_root, col_root, weight_grad, weight)
    return (out, new_rows.reshape(-1), new_cols.reshape(-1))


def solution(mesh):
    mesh = Mesh(mesh.devices.reshape(SIDE, SIDE, 2, LAYERS), ("y", "x", "core", "z"))
    placed = (P(ROWS, None), P(ROWS, "z"), P(ROWS, "z"), P(ROWS), P("z"))
    return jax.shard_map(
        shards,
        mesh=mesh,
        in_specs=placed,
        out_specs=(P(ROWS, "z"), P(ROWS), P("z")),
        check_vma=False,
    )
```

```python
import functools

import jax
import jax.numpy as jnp
from jax import lax
from jax.experimental import pallas as pl
from jax.experimental.pallas import tpu as pltpu
from jax.sharding import Mesh, PartitionSpec as P

D = 8192
FF = 16384


BETA_TWO = 0.8
CLIP_LEVEL = 0.25
WEIGHT_DECAY = 0.1
EPSILON = 1e-06

CHIPS = ("y", "x")
ROWS = ("y", "x", "core")
SIDE = 4
COUNT = SIDE * SIDE
LAYERS = 16
DEVICES = 2 * COUNT
TOKENS = 128
HALF = TOKENS // 2
ROW_BLOCK = 256
WIDTH = 1024
LANES = 128
COLUMNS = 512
TILE = (8, LANES)

ANYWHERE = pl.BlockSpec(memory_space=pl.ANY)
WHOLE = pl.BlockSpec(memory_space=pltpu.VMEM)
SCALARS = pl.BlockSpec(memory_space=pltpu.SMEM)
PARAMS = pltpu.CompilerParams(vmem_limit_bytes=16 * 2**20)


def shape(*dims, dtype=jnp.float32):
    return jax.ShapeDtypeStruct(dims, dtype)


def cost(flops, bytes_accessed):
    return pl.CostEstimate(flops=flops, bytes_accessed=bytes_accessed, transcendentals=0)


def device(y, x, core):
    return ((y % SIDE) * SIDE + x % SIDE) * 2 + core


def along(value, step):
    pairs = []
    for y in range(SIDE):
        for x in range(SIDE):
            pairs.append((device(y, x, 0), device(y, x + step, 0)))
            pairs.append((device(y, x, 1), device(y + step, x, 1)))
    return lax.ppermute(value, ROWS, pairs)


def gather_line(value):
    groups = [[device(y, x, 0) for y in range(SIDE)] for x in range(SIDE)]
    groups += [[device(y, x, 1) for x in range(SIDE)] for y in range(SIDE)]
    sent = jnp.broadcast_to(value, (SIDE,) + value.shape)
    return lax.all_to_all(sent, ROWS, 0, 0, axis_index_groups=groups)


def next_layer(value):
    pairs = [(i, (i + 1) % LAYERS) for i in range(LAYERS)]
    pairs += [(LAYERS + i, LAYERS + (i - 1) % LAYERS) for i in range(LAYERS)]
    return lax.ppermute(value, ("core", "z"), pairs)


def exchange(tiles, axes):
    return lax.all_to_all(tiles, axes, 0, 0)


def pack_kernel(place, source, out, sems):
    rows = pl.ds(pl.multiple_of(place[3] * HALF, HALF), HALF)
    copies = [
        pltpu.make_async_copy(source.at[rows, pl.ds(i * 2 * ROW_BLOCK, 2 * ROW_BLOCK)], out.at[i], sems.at[i])
        for i in range(COUNT)
    ]
    for copy in copies:
        copy.start()
    for copy in copies:
        copy.wait()


def pack(place, activations):
    return pl.pallas_call(
        pack_kernel,
        out_shape=pltpu.VMEM((COUNT, HALF, 2 * ROW_BLOCK), jnp.bfloat16),
        in_specs=[SCALARS, ANYWHERE],
        out_specs=WHOLE,
        scratch_shapes=[pltpu.SemaphoreType.DMA((COUNT,))],
        compiler_params=PARAMS,
        cost_estimate=cost(0, 2**21),
    )(place, pltpu.with_memory_space_constraint(activations, pltpu.HBM))


def turn_kernel(place, part, out):
    y, x, core = place[0], place[1], place[2]

    def block(i):
        j, k = i // SIDE, i % SIDE
        return part[jnp.where(core == 1, ((y - j) & (SIDE - 1)) * SIDE + k, k * SIDE + ((x - j) & (SIDE - 1)))]

    for i in range(0, COUNT, 2):
        out[:, i * HALF : (i + 2) * HALF] = jnp.concatenate([block(i), block(i + 1)], axis=0).T


def turn(place, part):
    return pl.pallas_call(
        turn_kernel,
        out_shape=shape(2 * ROW_BLOCK, COUNT * HALF, dtype=jnp.bfloat16),
        in_specs=[SCALARS, WHOLE],
        out_specs=WHOLE,
        compiler_params=PARAMS,
        cost_estimate=cost(0, 2**21),
    )(place, part)


def product_kernel(parts, which, kept, place, first, second, *refs):
    split = len(refs) - 1 - len(kept)
    operands, out, copies = refs[:split], refs[split], refs[split + 1 :]
    total = operands[-1] if len(operands) > 1 + max(index for *_, blocks in parts for index, _ in blocks) else None
    for index, copy in zip(kept, copies):
        copy[...] = operands[index][...]
    start = place[3] * HALF
    rows = pl.ds(0 if which is None else pl.multiple_of(which(place[2]) * ROW_BLOCK, ROW_BLOCK), out.shape[0])

    for n in range(WIDTH // COLUMNS):
        columns = slice(n * COLUMNS, (n + 1) * COLUMNS)
        value = None if total is None else total[rows, columns]
        for group, exchanged, blocks in parts:
            depth = slice(group * SIDE * HALF, group * SIDE * HALF + len(blocks) * HALF)
            features, offset = (first, start) if exchanged else (second, HALF - start)
            offset = pl.multiple_of(offset, HALF)
            grads = [operands[index][pl.ds(i * TOKENS + offset, HALF), columns] for index, i in blocks]
            term = jnp.dot(features[rows, depth], jnp.concatenate(grads, axis=0), preferred_element_type=jnp.float32)
            value = term if value is None else value + term
        out[:, columns] = value


def product(place, features, operands, parts, total=None, which=None, kept=()):
    count = 2 * ROW_BLOCK if which is None else ROW_BLOCK
    operands = [*features, *operands] + ([] if total is None else [total])
    out_shape = (shape(count, WIDTH),) + (shape(2 * TOKENS, WIDTH, dtype=jnp.bfloat16),) * len(kept)
    out = pl.pallas_call(
        functools.partial(product_kernel, parts, which, kept),
        out_shape=out_shape,
        in_specs=[SCALARS] + [WHOLE] * len(operands),
        out_specs=(WHOLE,) * len(out_shape),
        input_output_aliases={len(operands): 0} if total is not None and which is None else {},
        compiler_params=PARAMS,
        cost_estimate=cost(24 * count * HALF * WIDTH * sum(len(part[2]) for part in parts), 2**20),
    )(place, *operands)
    return out if kept else out[0]


def columns_kernel(mine, theirs, grad, sent):
    value = mine[...] + theirs[...]
    grad[...] = value
    sums = jnp.sum(value * value, axis=0, keepdims=True)
    tile = jnp.concatenate([sums[:, i * LANES : (i + 1) * LANES] for i in range(8)], axis=0)
    for i in range(DEVICES):
        sent[i] = tile


def columns(mine, theirs):
    return pl.pallas_call(
        columns_kernel,
        out_shape=(shape(ROW_BLOCK, WIDTH), shape(DEVICES, *TILE)),
        in_specs=[WHOLE] * 2,
        out_specs=(WHOLE, WHOLE),
        compiler_params=PARAMS,
        cost_estimate=cost(2**20, 3 * 2**20),
    )(mine, theirs)


def rows_kernel(received, moment, grad, weight, cols, col_root, sent):
    new = BETA_TWO * moment[...] + (1.0 - BETA_TWO) * (jnp.sum(received[...], axis=0) / D)
    cols[...] = new
    root = lax.rsqrt(new)
    col_root[...] = root
    sums = [jnp.zeros((ROW_BLOCK, LANES), jnp.float32)] * 4
    for i in range(WIDTH // LANES):
        lanes = slice(i * LANES, (i + 1) * LANES)
        value, held = grad[:, lanes], weight[:, lanes]
        by_cols = value * root[i : i + 1, :]
        terms = (value * value, by_cols * by_cols, by_cols * held, held * held)
        sums = [a + b for a, b in zip(sums, terms)]
    parts = []
    for value in sums:
        for row in range(0, ROW_BLOCK, LANES):
            parts.append(jnp.sum(value[row : row + LANES, :].T, axis=0, keepdims=True))
    tile = jnp.concatenate(parts, axis=0)
    for i in range(LAYERS):
        sent[i] = tile


def rows(received, moment, grad, weight):
    return pl.pallas_call(
        rows_kernel,
        out_shape=(shape(*TILE), shape(*TILE), shape(LAYERS, *TILE)),
        in_specs=[WHOLE] * 4,
        out_specs=(WHOLE, WHOLE, WHOLE),
        compiler_params=PARAMS,
        cost_estimate=cost(2**21, 2**21),
    )(received, moment, grad, weight)


def scalars_kernel(received, moment, rows_out, row_root, sent):
    parts = jnp.sum(received[...], axis=0)
    new = BETA_TWO * moment[...] + (1.0 - BETA_TWO) * (parts[0:2] / FF)
    rows_out[...] = new
    root = lax.rsqrt(new)
    row_root[...] = root
    sums = [jnp.sum(part, axis=0, keepdims=True) for part in (parts[2:4] * root * root, parts[4:6] * root, parts[6:8])]
    tile = jnp.concatenate(sums + [jnp.zeros_like(sums[0])], axis=0)
    for i in range(DEVICES):
        sent[i] = tile


def scalars(received, moment):
    return pl.pallas_call(
        scalars_kernel,
        out_shape=(shape(2, LANES), shape(2, LANES), shape(DEVICES, 4, LANES)),
        in_specs=[WHOLE] * 2,
        out_specs=(WHOLE, WHOLE, WHOLE),
        compiler_params=PARAMS,
        cost_estimate=cost(2**14, 2**18),
    )(received, moment)


def update_kernel(received, row_root, col_root, grad, weight, out, done, sems):
    parts = jnp.sum(received[...], axis=0)
    scaled_sum, cross_sum, weight_sum = (jnp.sum(parts[i : i + 1], keepdims=True) for i in range(3))
    factor = 1.0 / jnp.maximum(1.0, jnp.sqrt(scaled_sum / (D * FF)) / CLIP_LEVEL)
    direction_sum = (
        factor * factor * scaled_sum + 2.0 * WEIGHT_DECAY * factor * cross_sum + WEIGHT_DECAY * WEIGHT_DECAY * weight_sum
    )
    trust_ratio = jnp.sqrt(weight_sum / (jnp.maximum(direction_sum, 0.0) + EPSILON))
    by_row = row_root[...] * (trust_ratio * factor)
    by_col = col_root[...]
    decay = trust_ratio * WEIGHT_DECAY
    copies = []
    for half in range(2):
        scales = jnp.broadcast_to(by_row[half : half + 1, :], (LANES, LANES)).T
        for part in range(2):
            scale = scales[part * HALF : (part + 1) * HALF]
            here = slice(half * LANES + part * HALF, half * LANES + (part + 1) * HALF)
            for i in range(WIDTH // LANES):
                lanes = slice(i * LANES, (i + 1) * LANES)
                done[here, lanes] = grad[here, lanes] * by_col[i : i + 1, :] * scale + decay * weight[here, lanes]
            copies.append(pltpu.make_async_copy(done.at[here], out.at[here], sems.at[len(copies)]))
            copies[-1].start()
    for copy in copies:
        copy.wait()


def update(received, row_root, col_root, grad, weight):
    return pl.pallas_call(
        update_kernel,
        out_shape=shape(ROW_BLOCK, WIDTH),
        in_specs=[WHOLE] * 5,
        out_specs=ANYWHERE,
        scratch_shapes=[pltpu.VMEM((ROW_BLOCK, WIDTH), jnp.float32), pltpu.SemaphoreType.DMA((4,))],
        compiler_params=PARAMS,
        cost_estimate=cost(2**20, 3 * 2**20),
    )(received, row_root, col_root, grad, weight)


def shards(activations, out_grads, weight, row_moment, col_moment):
    y, x, core, layer = (lax.axis_index(name) for name in ("y", "x", "core", "z"))
    place = jnp.stack([y, x, core, layer & 1])
    line = gather_line(out_grads)
    packed, line = lax.optimization_barrier((pack(place, activations), line))
    first = exchange(packed, CHIPS)
    first, second = turn(place, first), turn(place, next_layer(first))
    low, high = (line[i : i + 2].reshape(2 * TOKENS, WIDTH) for i in (0, 2))
    back_low, ahead_high = along(low, 1), along(high, SIDE - 1)
    far = [along(back_low, 1), along(ahead_high, SIDE - 1)]
    back, ahead = [back_low, along(high, 1)], [along(low, SIDE - 1), ahead_high]
    blocks = lambda operand: [(operand, 0), (operand, 1), (operand + 1, 0), (operand + 1, 1)]
    total = product(place, (first, first), [low, high], [(0, True, blocks(0))])
    parts = [(1, True, blocks(0)), (3, True, blocks(2))]
    total, back[1], ahead[0] = product(place, (first, first), back + ahead, parts, total, kept=(1, 2))
    operands = [low, high] + back + far + ahead
    parts = [(2, True, blocks(4)), (0, False, blocks(0) + blocks(2) + blocks(4) + blocks(6))]
    theirs = product(place, (first, second), operands, parts, total, lambda core: 1 - core)
    received = lax.ppermute(theirs, "core", [(0, 1), (1, 0)])
    mine = product(place, (first, second), operands, parts, total, lambda core: core)
    weight_grad, tiles = columns(mine, received)
    new_cols, col_root, tiles = rows(exchange(tiles, ROWS), col_moment.reshape(TILE), weight_grad, weight)
    new_rows, row_root, tiles = scalars(exchange(tiles, "z"), row_moment.reshape(2, LANES))
    out = update(exchange(tiles, ROWS), row_root, col_root, weight_grad, weight)
    return (out, new_rows.reshape(-1), new_cols.reshape(-1))


def solution(mesh):
    mesh = Mesh(mesh.devices.reshape(SIDE, SIDE, 2, LAYERS), ("y", "x", "core", "z"))
    placed = (P(ROWS, None), P(ROWS, "z"), P(ROWS, "z"), P(ROWS), P("z"))
    return jax.shard_map(
        shards,
        mesh=mesh,
        in_specs=placed,
        out_specs=(P(ROWS, "z"), P(ROWS), P("z")),
        check_vma=False,
    )
```

```python
import functools

import jax
import jax.numpy as jnp
from jax import lax
from jax.experimental import pallas as pl
from jax.experimental.pallas import tpu as pltpu
from jax.sharding import Mesh, PartitionSpec as P

D = 8192
FF = 16384


BETA_TWO = 0.8
CLIP_LEVEL = 0.25
WEIGHT_DECAY = 0.1
EPSILON = 1e-06

CHIPS = ("y", "x")
ROWS = ("y", "x", "core")
SIDE = 4
COUNT = SIDE * SIDE
LAYERS = 16
DEVICES = 2 * COUNT
TOKENS = 128
HALF = TOKENS // 2
ROW_BLOCK = 256
WIDTH = 1024
LANES = 128
COLUMNS = 512
TILE = (8, LANES)

ANYWHERE = pl.BlockSpec(memory_space=pl.ANY)
WHOLE = pl.BlockSpec(memory_space=pltpu.VMEM)
SCALARS = pl.BlockSpec(memory_space=pltpu.SMEM)
PARAMS = pltpu.CompilerParams(vmem_limit_bytes=16 * 2**20)


def shape(*dims, dtype=jnp.float32):
    return jax.ShapeDtypeStruct(dims, dtype)


def cost(flops, bytes_accessed):
    return pl.CostEstimate(flops=flops, bytes_accessed=bytes_accessed, transcendentals=0)


def device(y, x, core):
    return ((y % SIDE) * SIDE + x % SIDE) * 2 + core


def along(value, step):
    pairs = []
    for y in range(SIDE):
        for x in range(SIDE):
            pairs.append((device(y, x, 0), device(y, x + step, 0)))
            pairs.append((device(y, x, 1), device(y + step, x, 1)))
    return lax.ppermute(value, ROWS, pairs)


def gather_line(value):
    groups = [[device(y, x, 0) for y in range(SIDE)] for x in range(SIDE)]
    groups += [[device(y, x, 1) for x in range(SIDE)] for y in range(SIDE)]
    sent = jnp.broadcast_to(value, (SIDE,) + value.shape)
    return lax.all_to_all(sent, ROWS, 0, 0, axis_index_groups=groups)


def next_layer(value):
    pairs = [(i, (i + 1) % LAYERS) for i in range(LAYERS)]
    pairs += [(LAYERS + i, LAYERS + (i - 1) % LAYERS) for i in range(LAYERS)]
    return lax.ppermute(value, ("core", "z"), pairs)


def exchange(tiles, axes):
    return lax.all_to_all(tiles, axes, 0, 0)


def pack_kernel(place, source, out, sems):
    rows = pl.ds(pl.multiple_of(place[3] * HALF, HALF), HALF)
    copies = [
        pltpu.make_async_copy(source.at[rows, pl.ds(i * 2 * ROW_BLOCK, 2 * ROW_BLOCK)], out.at[i], sems.at[i])
        for i in range(COUNT)
    ]
    for copy in copies:
        copy.start()
    for copy in copies:
        copy.wait()


def pack(place, activations):
    return pl.pallas_call(
        pack_kernel,
        out_shape=pltpu.VMEM((COUNT, HALF, 2 * ROW_BLOCK), jnp.bfloat16),
        in_specs=[SCALARS, ANYWHERE],
        out_specs=WHOLE,
        scratch_shapes=[pltpu.SemaphoreType.DMA((COUNT,))],
        compiler_params=PARAMS,
        cost_estimate=cost(0, 2**21),
    )(place, pltpu.with_memory_space_constraint(activations, pltpu.HBM))


def turn_kernel(place, part, out):
    y, x, core = place[0], place[1], place[2]

    def block(i):
        j, k = i // SIDE, i % SIDE
        return part[jnp.where(core == 1, ((y - j) & (SIDE - 1)) * SIDE + k, k * SIDE + ((x - j) & (SIDE - 1)))]

    for i in range(0, COUNT, 2):
        out[:, i * HALF : (i + 2) * HALF] = jnp.concatenate([block(i), block(i + 1)], axis=0).T


def turn(place, part):
    return pl.pallas_call(
        turn_kernel,
        out_shape=shape(2 * ROW_BLOCK, COUNT * HALF, dtype=jnp.bfloat16),
        in_specs=[SCALARS, WHOLE],
        out_specs=WHOLE,
        compiler_params=PARAMS,
        cost_estimate=cost(0, 2**21),
    )(place, part)


def product_kernel(parts, which, kept, place, first, second, *refs):
    split = len(refs) - 1 - len(kept)
    operands, out, copies = refs[:split], refs[split], refs[split + 1 :]
    total = operands[-1] if len(operands) > 1 + max(index for *_, blocks in parts for index, _ in blocks) else None
    for index, copy in zip(kept, copies):
        copy[...] = operands[index][...]
    start = place[3] * HALF
    rows = pl.ds(0 if which is None else pl.multiple_of(which(place[2]) * ROW_BLOCK, ROW_BLOCK), out.shape[0])

    for n in range(WIDTH // COLUMNS):
        columns = slice(n * COLUMNS, (n + 1) * COLUMNS)
        value = None if total is None else total[rows, columns]
        for group, exchanged, blocks in parts:
            depth = slice(group * SIDE * HALF, group * SIDE * HALF + len(blocks) * HALF)
            features, offset = (first, start) if exchanged else (second, HALF - start)
            offset = pl.multiple_of(offset, HALF)
            grads = [operands[index][pl.ds(i * TOKENS + offset, HALF), columns] for index, i in blocks]
            term = jnp.dot(features[rows, depth], jnp.concatenate(grads, axis=0), preferred_element_type=jnp.float32)
            value = term if value is None else value + term
        out[:, columns] = value


def product(place, features, operands, parts, total=None, which=None, kept=()):
    count = 2 * ROW_BLOCK if which is None else ROW_BLOCK
    operands = [*features, *operands] + ([] if total is None else [total])
    out_shape = (shape(count, WIDTH),) + (shape(2 * TOKENS, WIDTH, dtype=jnp.bfloat16),) * len(kept)
    out = pl.pallas_call(
        functools.partial(product_kernel, parts, which, kept),
        out_shape=out_shape,
        in_specs=[SCALARS] + [WHOLE] * len(operands),
        out_specs=(WHOLE,) * len(out_shape),
        input_output_aliases={len(operands): 0} if total is not None and which is None else {},
        compiler_params=PARAMS,
        cost_estimate=cost(24 * count * HALF * WIDTH * sum(len(part[2]) for part in parts), 2**20),
    )(place, *operands)
    return out if kept else out[0]


def columns_kernel(mine, theirs, grad, sent):
    value = mine[...] + theirs[...]
    grad[...] = value
    sums = jnp.sum(value * value, axis=0, keepdims=True)
    tile = jnp.concatenate([sums[:, i * LANES : (i + 1) * LANES] for i in range(8)], axis=0)
    for i in range(DEVICES):
        sent[i] = tile


def columns(mine, theirs):
    return pl.pallas_call(
        columns_kernel,
        out_shape=(shape(ROW_BLOCK, WIDTH), shape(DEVICES, *TILE)),
        in_specs=[WHOLE] * 2,
        out_specs=(WHOLE, WHOLE),
        compiler_params=PARAMS,
        cost_estimate=cost(2**20, 3 * 2**20),
    )(mine, theirs)


def by_rows(value):
    halves = (value[:LANES], value[LANES:])
    return jnp.concatenate([jnp.sum(half.T, axis=0, keepdims=True) for half in halves], axis=0)


def weights_kernel(weight, out):
    value = jnp.zeros((ROW_BLOCK, LANES), jnp.float32)
    for i in range(WIDTH // LANES):
        held = weight[:, i * LANES : (i + 1) * LANES]
        value += held * held
    out[...] = by_rows(value)


def weights(weight):
    return pl.pallas_call(
        weights_kernel,
        out_shape=shape(2, LANES),
        in_specs=[WHOLE],
        out_specs=WHOLE,
        compiler_params=PARAMS,
        cost_estimate=cost(2**19, 2**20),
    )(weight)


def rows_kernel(received, moment, grad, weight, weight_rows, cols, col_root, sent):
    new = BETA_TWO * moment[...] + (1.0 - BETA_TWO) * (jnp.sum(received[...], axis=0) / D)
    cols[...] = new
    root = lax.rsqrt(new)
    col_root[...] = root
    sums = [jnp.zeros((ROW_BLOCK, LANES), jnp.float32)] * 3
    for i in range(WIDTH // LANES):
        lanes = slice(i * LANES, (i + 1) * LANES)
        value, held = grad[:, lanes], weight[:, lanes]
        by_cols = value * root[i : i + 1, :]
        terms = (value * value, by_cols * by_cols, by_cols * held)
        sums = [a + b for a, b in zip(sums, terms)]
    tile = jnp.concatenate([by_rows(value) for value in sums] + [weight_rows[...]], axis=0)
    for i in range(LAYERS):
        sent[i] = tile


def rows(received, moment, grad, weight, weight_rows):
    return pl.pallas_call(
        rows_kernel,
        out_shape=(shape(*TILE), shape(*TILE), shape(LAYERS, *TILE)),
        in_specs=[WHOLE] * 5,
        out_specs=(WHOLE, WHOLE, WHOLE),
        compiler_params=PARAMS,
        cost_estimate=cost(2**21, 2**21),
    )(received, moment, grad, weight, weight_rows)


def scalars_kernel(received, moment, rows_out, row_root, sent):
    parts = jnp.sum(received[...], axis=0)
    new = BETA_TWO * moment[...] + (1.0 - BETA_TWO) * (parts[0:2] / FF)
    rows_out[...] = new
    root = lax.rsqrt(new)
    row_root[...] = root
    sums = [jnp.sum(part, axis=0, keepdims=True) for part in (parts[2:4] * root * root, parts[4:6] * root, parts[6:8])]
    tile = jnp.concatenate(sums + [jnp.zeros_like(sums[0])], axis=0)
    for i in range(DEVICES):
        sent[i] = tile


def scalars(received, moment):
    return pl.pallas_call(
        scalars_kernel,
        out_shape=(shape(2, LANES), shape(2, LANES), shape(DEVICES, 4, LANES)),
        in_specs=[WHOLE] * 2,
        out_specs=(WHOLE, WHOLE, WHOLE),
        compiler_params=PARAMS,
        cost_estimate=cost(2**14, 2**18),
    )(received, moment)


def update_kernel(received, row_root, col_root, grad, weight, out, done, sems):
    parts = jnp.sum(received[...], axis=0)
    scaled_sum, cross_sum, weight_sum = (jnp.sum(parts[i : i + 1], keepdims=True) for i in range(3))
    factor = 1.0 / jnp.maximum(1.0, jnp.sqrt(scaled_sum / (D * FF)) / CLIP_LEVEL)
    direction_sum = (
        factor * factor * scaled_sum + 2.0 * WEIGHT_DECAY * factor * cross_sum + WEIGHT_DECAY * WEIGHT_DECAY * weight_sum
    )
    trust_ratio = jnp.sqrt(weight_sum / (jnp.maximum(direction_sum, 0.0) + EPSILON))
    by_row = row_root[...] * (trust_ratio * factor)
    by_col = col_root[...]
    decay = trust_ratio * WEIGHT_DECAY
    copies = []
    for half in range(2):
        scales = jnp.broadcast_to(by_row[half : half + 1, :], (LANES, LANES)).T
        for part in range(2):
            scale = scales[part * HALF : (part + 1) * HALF]
            here = slice(half * LANES + part * HALF, half * LANES + (part + 1) * HALF)
            for i in range(WIDTH // LANES):
                lanes = slice(i * LANES, (i + 1) * LANES)
                done[here, lanes] = grad[here, lanes] * by_col[i : i + 1, :] * scale + decay * weight[here, lanes]
            copies.append(pltpu.make_async_copy(done.at[here], out.at[here], sems.at[len(copies)]))
            copies[-1].start()
    for copy in copies:
        copy.wait()


def update(received, row_root, col_root, grad, weight):
    return pl.pallas_call(
        update_kernel,
        out_shape=shape(ROW_BLOCK, WIDTH),
        in_specs=[WHOLE] * 5,
        out_specs=ANYWHERE,
        scratch_shapes=[pltpu.VMEM((ROW_BLOCK, WIDTH), jnp.float32), pltpu.SemaphoreType.DMA((4,))],
        compiler_params=PARAMS,
        cost_estimate=cost(2**20, 3 * 2**20),
    )(received, row_root, col_root, grad, weight)


def shards(activations, out_grads, weight, row_moment, col_moment):
    y, x, core, layer = (lax.axis_index(name) for name in ("y", "x", "core", "z"))
    place = jnp.stack([y, x, core, layer & 1])
    line = gather_line(out_grads)
    packed, line = lax.optimization_barrier((pack(place, activations), line))
    first = exchange(packed, CHIPS)
    first, second = turn(place, first), turn(place, next_layer(first))
    low, high = (line[i : i + 2].reshape(2 * TOKENS, WIDTH) for i in (0, 2))
    back_low, ahead_high = along(low, 1), along(high, SIDE - 1)
    far = [along(back_low, 1), along(ahead_high, SIDE - 1)]
    back, ahead = [back_low, along(high, 1)], [along(low, SIDE - 1), ahead_high]
    blocks = lambda operand: [(operand, 0), (operand, 1), (operand + 1, 0), (operand + 1, 1)]
    total = product(place, (first, first), [low, high], [(0, True, blocks(0))])
    total, held = lax.optimization_barrier((total, weight))
    total, weight_rows = lax.optimization_barrier((total, weights(held)))
    parts = [(1, True, blocks(0)), (3, True, blocks(2))]
    total, back[1], ahead[0] = product(place, (first, first), back + ahead, parts, total, kept=(1, 2))
    operands = [low, high] + back + far + ahead
    parts = [(2, True, blocks(4)), (0, False, blocks(0) + blocks(2) + blocks(4) + blocks(6))]
    theirs = product(place, (first, second), operands, parts, total, lambda core: 1 - core)
    received = lax.ppermute(theirs, "core", [(0, 1), (1, 0)])
    mine = product(place, (first, second), operands, parts, total, lambda core: core)
    weight_grad, tiles = columns(mine, received)
    new_cols, col_root, tiles = rows(exchange(tiles, ROWS), col_moment.reshape(TILE), weight_grad, weight, weight_rows)
    new_rows, row_root, tiles = scalars(exchange(tiles, "z"), row_moment.reshape(2, LANES))
    out = update(exchange(tiles, ROWS), row_root, col_root, weight_grad, weight)
    return (out, new_rows.reshape(-1), new_cols.reshape(-1))


def solution(mesh):
    mesh = Mesh(mesh.devices.reshape(SIDE, SIDE, 2, LAYERS), ("y", "x", "core", "z"))
    placed = (P(ROWS, None), P(ROWS, "z"), P(ROWS, "z"), P(ROWS), P("z"))
    return jax.shard_map(
        shards,
        mesh=mesh,
        in_specs=placed,
        out_specs=(P(ROWS, "z"), P(ROWS), P("z")),
        check_vma=False,
    )
```

```python
import functools

import jax
import jax.numpy as jnp
from jax import lax
from jax.experimental import pallas as pl
from jax.experimental.pallas import tpu as pltpu
from jax.sharding import Mesh, PartitionSpec as P

D = 8192
FF = 16384


BETA_TWO = 0.8
CLIP_LEVEL = 0.25
WEIGHT_DECAY = 0.1
EPSILON = 1e-06

CHIPS = ("y", "x")
ROWS = ("y", "x", "core")
SIDE = 4
COUNT = SIDE * SIDE
LAYERS = 16
DEVICES = 2 * COUNT
TOKENS = 128
HALF = TOKENS // 2
ROW_BLOCK = 256
WIDTH = 1024
LANES = 128
COLUMNS = 512
TILE = (8, LANES)

ANYWHERE = pl.BlockSpec(memory_space=pl.ANY)
WHOLE = pl.BlockSpec(memory_space=pltpu.VMEM)
SCALARS = pl.BlockSpec(memory_space=pltpu.SMEM)
PARAMS = pltpu.CompilerParams(vmem_limit_bytes=16 * 2**20)


def shape(*dims, dtype=jnp.float32):
    return jax.ShapeDtypeStruct(dims, dtype)


def cost(flops, bytes_accessed):
    return pl.CostEstimate(flops=flops, bytes_accessed=bytes_accessed, transcendentals=0)


def device(y, x, core):
    return ((y % SIDE) * SIDE + x % SIDE) * 2 + core


def along(value, step):
    pairs = []
    for y in range(SIDE):
        for x in range(SIDE):
            pairs.append((device(y, x, 0), device(y, x + step, 0)))
            pairs.append((device(y, x, 1), device(y + step, x, 1)))
    return lax.ppermute(value, ROWS, pairs)


def gather_line(value):
    groups = [[device(y, x, 0) for y in range(SIDE)] for x in range(SIDE)]
    groups += [[device(y, x, 1) for x in range(SIDE)] for y in range(SIDE)]
    sent = jnp.broadcast_to(value, (SIDE,) + value.shape)
    return lax.all_to_all(sent, ROWS, 0, 0, axis_index_groups=groups)


def next_layer(value):
    pairs = [(i, (i - 1) % LAYERS) for i in range(LAYERS)]
    pairs += [(LAYERS + i, LAYERS + (i + 1) % LAYERS) for i in range(LAYERS)]
    return lax.ppermute(value, ("core", "z"), pairs)


def exchange(tiles, axes):
    return lax.all_to_all(tiles, axes, 0, 0)


def pack_kernel(place, source, out, sems):
    rows = pl.ds(pl.multiple_of(place[3] * HALF, HALF), HALF)
    copies = [
        pltpu.make_async_copy(source.at[rows, pl.ds(i * 2 * ROW_BLOCK, 2 * ROW_BLOCK)], out.at[i], sems.at[i])
        for i in range(COUNT)
    ]
    for copy in copies:
        copy.start()
    for copy in copies:
        copy.wait()


def pack(place, activations):
    return pl.pallas_call(
        pack_kernel,
        out_shape=pltpu.VMEM((COUNT, HALF, 2 * ROW_BLOCK), jnp.bfloat16),
        in_specs=[SCALARS, ANYWHERE],
        out_specs=WHOLE,
        scratch_shapes=[pltpu.SemaphoreType.DMA((COUNT,))],
        compiler_params=PARAMS,
        cost_estimate=cost(0, 2**21),
    )(place, pltpu.with_memory_space_constraint(activations, pltpu.HBM))


def turn_kernel(place, part, out):
    y, x, core = place[0], place[1], place[2]

    def block(i):
        j, k = i // SIDE, i % SIDE
        return part[jnp.where(core == 1, ((y - j) & (SIDE - 1)) * SIDE + k, k * SIDE + ((x - j) & (SIDE - 1)))]

    for i in range(0, COUNT, 2):
        out[:, i * HALF : (i + 2) * HALF] = jnp.concatenate([block(i), block(i + 1)], axis=0).T


def turn(place, part):
    return pl.pallas_call(
        turn_kernel,
        out_shape=shape(2 * ROW_BLOCK, COUNT * HALF, dtype=jnp.bfloat16),
        in_specs=[SCALARS, WHOLE],
        out_specs=WHOLE,
        compiler_params=PARAMS,
        cost_estimate=cost(0, 2**21),
    )(place, part)


def product_kernel(parts, which, kept, place, first, second, *refs):
    split = len(refs) - 1 - len(kept)
    operands, out, copies = refs[:split], refs[split], refs[split + 1 :]
    total = operands[-1] if len(operands) > 1 + max(index for *_, blocks in parts for index, _ in blocks) else None
    for index, copy in zip(kept, copies):
        copy[...] = operands[index][...]
    start = place[3] * HALF
    rows = pl.ds(0 if which is None else pl.multiple_of(which(place[2]) * ROW_BLOCK, ROW_BLOCK), out.shape[0])

    for n in range(WIDTH // COLUMNS):
        columns = slice(n * COLUMNS, (n + 1) * COLUMNS)
        value = None if total is None else total[rows, columns]
        for group, exchanged, blocks in parts:
            depth = slice(group * SIDE * HALF, group * SIDE * HALF + len(blocks) * HALF)
            features, offset = (first, start) if exchanged else (second, HALF - start)
            offset = pl.multiple_of(offset, HALF)
            grads = [operands[index][pl.ds(i * TOKENS + offset, HALF), columns] for index, i in blocks]
            term = jnp.dot(features[rows, depth], jnp.concatenate(grads, axis=0), preferred_element_type=jnp.float32)
            value = term if value is None else value + term
        out[:, columns] = value


def product(place, features, operands, parts, total=None, which=None, kept=()):
    count = 2 * ROW_BLOCK if which is None else ROW_BLOCK
    operands = [*features, *operands] + ([] if total is None else [total])
    out_shape = (shape(count, WIDTH),) + (shape(2 * TOKENS, WIDTH, dtype=jnp.bfloat16),) * len(kept)
    out = pl.pallas_call(
        functools.partial(product_kernel, parts, which, kept),
        out_shape=out_shape,
        in_specs=[SCALARS] + [WHOLE] * len(operands),
        out_specs=(WHOLE,) * len(out_shape),
        input_output_aliases={len(operands): 0} if total is not None and which is None else {},
        compiler_params=PARAMS,
        cost_estimate=cost(24 * count * HALF * WIDTH * sum(len(part[2]) for part in parts), 2**20),
    )(place, *operands)
    return out if kept else out[0]


def columns_kernel(mine, theirs, grad, sent):
    value = mine[...] + theirs[...]
    grad[...] = value
    sums = jnp.sum(value * value, axis=0, keepdims=True)
    tile = jnp.concatenate([sums[:, i * LANES : (i + 1) * LANES] for i in range(8)], axis=0)
    for i in range(DEVICES):
        sent[i] = tile


def columns(mine, theirs):
    return pl.pallas_call(
        columns_kernel,
        out_shape=(shape(ROW_BLOCK, WIDTH), shape(DEVICES, *TILE)),
        in_specs=[WHOLE] * 2,
        out_specs=(WHOLE, WHOLE),
        compiler_params=PARAMS,
        cost_estimate=cost(2**20, 3 * 2**20),
    )(mine, theirs)


def rows_kernel(received, moment, grad, weight, cols, col_root, sent):
    new = BETA_TWO * moment[...] + (1.0 - BETA_TWO) * (jnp.sum(received[...], axis=0) / D)
    cols[...] = new
    root = lax.rsqrt(new)
    col_root[...] = root
    sums = [jnp.zeros((ROW_BLOCK, LANES), jnp.float32)] * 4
    for i in range(WIDTH // LANES):
        lanes = slice(i * LANES, (i + 1) * LANES)
        value, held = grad[:, lanes], weight[:, lanes]
        by_cols = value * root[i : i + 1, :]
        terms = (value * value, by_cols * by_cols, by_cols * held, held * held)
        sums = [a + b for a, b in zip(sums, terms)]
    parts = []
    for value in sums:
        for row in range(0, ROW_BLOCK, LANES):
            parts.append(jnp.sum(value[row : row + LANES, :].T, axis=0, keepdims=True))
    tile = jnp.concatenate(parts, axis=0)
    for i in range(LAYERS):
        sent[i] = tile


def rows(received, moment, grad, weight):
    return pl.pallas_call(
        rows_kernel,
        out_shape=(shape(*TILE), shape(*TILE), shape(LAYERS, *TILE)),
        in_specs=[WHOLE] * 4,
        out_specs=(WHOLE, WHOLE, WHOLE),
        compiler_params=PARAMS,
        cost_estimate=cost(2**21, 2**21),
    )(received, moment, grad, weight)


def scalars_kernel(received, moment, rows_out, row_root, sent):
    parts = jnp.sum(received[...], axis=0)
    new = BETA_TWO * moment[...] + (1.0 - BETA_TWO) * (parts[0:2] / FF)
    rows_out[...] = new
    root = lax.rsqrt(new)
    row_root[...] = root
    sums = [jnp.sum(part, axis=0, keepdims=True) for part in (parts[2:4] * root * root, parts[4:6] * root, parts[6:8])]
    tile = jnp.concatenate(sums + [jnp.zeros_like(sums[0])], axis=0)
    for i in range(DEVICES):
        sent[i] = tile


def scalars(received, moment):
    return pl.pallas_call(
        scalars_kernel,
        out_shape=(shape(2, LANES), shape(2, LANES), shape(DEVICES, 4, LANES)),
        in_specs=[WHOLE] * 2,
        out_specs=(WHOLE, WHOLE, WHOLE),
        compiler_params=PARAMS,
        cost_estimate=cost(2**14, 2**18),
    )(received, moment)


def update_kernel(received, row_root, col_root, grad, weight, out, done, sems):
    parts = jnp.sum(received[...], axis=0)
    scaled_sum, cross_sum, weight_sum = (jnp.sum(parts[i : i + 1], keepdims=True) for i in range(3))
    factor = 1.0 / jnp.maximum(1.0, jnp.sqrt(scaled_sum / (D * FF)) / CLIP_LEVEL)
    direction_sum = (
        factor * factor * scaled_sum + 2.0 * WEIGHT_DECAY * factor * cross_sum + WEIGHT_DECAY * WEIGHT_DECAY * weight_sum
    )
    trust_ratio = jnp.sqrt(weight_sum / (jnp.maximum(direction_sum, 0.0) + EPSILON))
    by_row = row_root[...] * (trust_ratio * factor)
    by_col = col_root[...]
    decay = trust_ratio * WEIGHT_DECAY
    copies = []
    for half in range(2):
        scales = jnp.broadcast_to(by_row[half : half + 1, :], (LANES, LANES)).T
        for part in range(2):
            scale = scales[part * HALF : (part + 1) * HALF]
            here = slice(half * LANES + part * HALF, half * LANES + (part + 1) * HALF)
            for i in range(WIDTH // LANES):
                lanes = slice(i * LANES, (i + 1) * LANES)
                done[here, lanes] = grad[here, lanes] * by_col[i : i + 1, :] * scale + decay * weight[here, lanes]
            copies.append(pltpu.make_async_copy(done.at[here], out.at[here], sems.at[len(copies)]))
            copies[-1].start()
    for copy in copies:
        copy.wait()


def update(received, row_root, col_root, grad, weight):
    return pl.pallas_call(
        update_kernel,
        out_shape=shape(ROW_BLOCK, WIDTH),
        in_specs=[WHOLE] * 5,
        out_specs=ANYWHERE,
        scratch_shapes=[pltpu.VMEM((ROW_BLOCK, WIDTH), jnp.float32), pltpu.SemaphoreType.DMA((4,))],
        compiler_params=PARAMS,
        cost_estimate=cost(2**20, 3 * 2**20),
    )(received, row_root, col_root, grad, weight)


def shards(activations, out_grads, weight, row_moment, col_moment):
    y, x, core, layer = (lax.axis_index(name) for name in ("y", "x", "core", "z"))
    place = jnp.stack([y, x, core, layer & 1])
    line = gather_line(out_grads)
    packed, line = lax.optimization_barrier((pack(place, activations), line))
    first = exchange(packed, CHIPS)
    first, second = turn(place, first), turn(place, next_layer(first))
    low, high = (line[i : i + 2].reshape(2 * TOKENS, WIDTH) for i in (0, 2))
    back_low, ahead_high = along(low, 1), along(high, SIDE - 1)
    far = [along(back_low, 1), along(ahead_high, SIDE - 1)]
    back, ahead = [back_low, along(high, 1)], [along(low, SIDE - 1), ahead_high]
    blocks = lambda operand: [(operand, 0), (operand, 1), (operand + 1, 0), (operand + 1, 1)]
    total = product(place, (first, first), [low, high], [(0, True, blocks(0))])
    parts = [(1, True, blocks(0)), (3, True, blocks(2))]
    total, back[1], ahead[0] = product(place, (first, first), back + ahead, parts, total, kept=(1, 2))
    operands = [low, high] + back + far + ahead
    parts = [(2, True, blocks(4)), (0, False, blocks(0) + blocks(2) + blocks(4) + blocks(6))]
    theirs = product(place, (first, second), operands, parts, total, lambda core: 1 - core)
    received = lax.ppermute(theirs, "core", [(0, 1), (1, 0)])
    mine = product(place, (first, second), operands, parts, total, lambda core: core)
    weight_grad, tiles = columns(mine, received)
    new_cols, col_root, tiles = rows(exchange(tiles, ROWS), col_moment.reshape(TILE), weight_grad, weight)
    new_rows, row_root, tiles = scalars(exchange(tiles, "z"), row_moment.reshape(2, LANES))
    out = update(exchange(tiles, ROWS), row_root, col_root, weight_grad, weight)
    return (out, new_rows.reshape(-1), new_cols.reshape(-1))


def solution(mesh):
    mesh = Mesh(mesh.devices.reshape(SIDE, SIDE, 2, LAYERS), ("y", "x", "core", "z"))
    placed = (P(ROWS, None), P(ROWS, "z"), P(ROWS, "z"), P(ROWS), P("z"))
    return jax.shard_map(
        shards,
        mesh=mesh,
        in_specs=placed,
        out_specs=(P(ROWS, "z"), P(ROWS), P("z")),
        check_vma=False,
    )
```
